32 devices in a mesh: tm: 8 (over z, y), clus: 4 (over x, core).
Axes of the slice: x: 2, y: 2, z: 4, core: 2. Of those that a mesh axis runs over, the one named last changes fastest.
Arguments:
- right_side: float32 [15, 32768], P(None, ('tm', 'clus')), may hold values from -8 to 8
- transition: float32 [15, 15, 32768], P(None, None, ('tm', 'clus')), may hold values from -1.5 to 1.5
- precond: float32 [15, 15, 32768], P(None, None, ('tm', 'clus')), as said below
- slot_of: int32 [32768], P(('tm', 'clus')), may hold values from 0 to 1023, as said below
- cluster_id: int32 [8, 4096], P('tm', 'clus'), may hold values from 0 to 63, never falling along the last dimension, each value on 1 to 128 neighbouring positions
- damping: float32 [8, 64], P('tm'), may hold values from 0.3 to 3
- pair_first: int32 [8, 8192], P('tm', 'clus'), may hold values from 0 to 4095
- pair_second: int32 [8, 8192], P('tm', 'clus'), may hold values from 0 to 4095
- pair_blocks: float32 [15, 15, 8, 8192], P(None, None, 'tm', 'clus'), may hold values from -1.5 to 1.5
Outputs:
- solution_field: float32 [15, 32768], P(None, ('tm', 'clus'))
- residual: float32 [15, 32768], P(None, ('tm', 'clus'))
The draws below stay inside these ranges and needn't reach their ends.
Inputs may be any that keep to these rules, and one draw needn't show every extreme that they name: `slot_of`: the 1024 entries of each device's block are a permutation of 0 to 1023. `cluster_id`: never falling along each group's keyframes. `precond`: each keyframe's block is symmetric positive definite.
All inputs are finite; a program needn't handle non-finite values.
Results may differ from the reference program's by a relative error of at most 0.00015.
Values sent between devices are 32-bit elements; how exact they have to be, the bound alone decides.
No kernel may reach another device: no remote copies, remote signals or barrier semaphores. Data moves between devices by JAX's collectives and lax.ppermute only.
A program may use at most 128 MiB of HBM per device.

```python
import math
import jax
import jax.numpy as jnp
import numpy as np
from jax import lax

STATE = 15
KF_DEV = 1024
CLUSTERS = 64
ITERS = 2
KEYFRAMES = 32768
GROUP_KF = 4096
PAIR_GROUP = 8192
N_TM = 8
N_CLUS = 4


def draw_precond(key, part):
    first, second = jax.random.split(key)
    diag = jnp.exp(jax.random.uniform(first, (STATE, KEYFRAMES), jnp.float32, jnp.log(0.5), jnp.log(4.0)))
    noise = jax.random.uniform(second, (STATE, STATE, KEYFRAMES), jnp.float32, -1.0, 1.0)
    eye = jnp.eye(STATE, dtype=jnp.float32)
    sym = (noise + jnp.transpose(noise, (1, 0, 2))) * 0.0175 * (1.0 - eye)[:, :, None]
    return sym + eye[:, :, None] * diag[:, None, :]


def draw_slot_of(key, part):
    blocks = KEYFRAMES // KF_DEV
    keys = jax.random.split(key, blocks)
    perms = jax.vmap(lambda one: jax.random.permutation(one, KF_DEV))(keys)
    return perms.reshape(-1).astype(jnp.int32)


def set_ends(drawn, stream_key, low, top_value):
    spot = [jax.random.randint(jax.random.fold_in(stream_key, axis), (), 0, length) for axis, length in enumerate(drawn.shape)]
    widest = drawn.shape.index(max(drawn.shape))
    next_to = spot[:widest] + [(spot[widest] + 1) % drawn.shape[widest]] + spot[widest + 1:]
    return drawn.at[tuple(spot)].set(low).at[tuple(next_to)].set(top_value)


def block_scale(key, shape, cuts, smallest, top_value):
    factor_of, own = 1.0, jax.random.fold_in(key, 6)
    for position, parts in cuts:
        draws = jnp.exp(jax.random.uniform(jax.random.fold_in(own, position), (parts,), jnp.float32, smallest / len(cuts), top_value / len(cuts)))
        factor_of = factor_of * jnp.repeat(draws, shape[position] // parts).reshape([-1 if axis == position else 1 for axis in range(len(shape))])
    return factor_of


def profile(count, total, most, slope):
    portions = [(1 << 20) // math.isqrt(rank ** slope) + 1 for rank in range(2, count + 1)]
    spare, holding = total - most - (count - 1), [1] * (count - 1)
    while spare > 0:
        free = [i for i in range(count - 1) if holding[i] < most]
        mass, budget = sum([portions[i] for i in free]), spare
        for i in free:
            addition = min(most - holding[i], max(1, budget * portions[i] // mass), spare)
            holding[i] = holding[i] + addition
            spare = spare - addition
    return np.array([most] + holding)


def uneven_parts(rng, count, total, most, skew):
    if count == 2:
        one = jax.random.randint(rng, (), max(1, total - most), min(most, total - 1) + 1)
        return jnp.stack([one, total - one])
    lengths = jnp.asarray(profile(count, total, most, skew), jnp.int32)
    couples = (count - 1) // 2
    giver, taker = lengths[1:1 + 2 * couples:2], lengths[2:2 + 2 * couples:2]
    margin = jnp.minimum(giver - 1, most - taker)
    passed = jax.random.randint(jax.random.fold_in(rng, 1), (couples,), 0, 1 << 20) % (margin + 1)
    lengths = lengths.at[1:1 + 2 * couples:2].set(giver - passed).at[2:2 + 2 * couples:2].set(taker + passed)
    return lengths[jax.random.permutation(jax.random.fold_in(rng, 2), count)]


def scatter_about(own_key, extent, width, reach, pieces=(), kind=jnp.bfloat16):
    entries = jax.random.normal(own_key, extent, jnp.float32) * width
    if len(pieces) > 0:
        entries = block_scale(own_key, extent, pieces, -0.22, 0.18) * entries
    return jnp.clip(entries, min=-reach, max=reach).astype(kind)


def setup_inputs(seed: int = 0) -> dict:
    key_of = jax.random.split(jax.random.key(seed), 10)
    return {
        "right_side": scatter_about(key_of[0], (STATE, KEYFRAMES), 1.0, 8.0, ((1, 32),), jnp.float32),
        "transition": scatter_about(key_of[1], (STATE, STATE, KEYFRAMES), STATE ** -0.5, 1.5, ((2, 32),), jnp.float32),
        "precond": draw_precond(jax.random.fold_in(key_of[9], 71), 0),
        "slot_of": draw_slot_of(jax.random.fold_in(key_of[9], 71), 0),
        "cluster_id": jax.vmap(lambda own: jnp.searchsorted(jnp.cumsum(uneven_parts(own, CLUSTERS, GROUP_KF, 2 * GROUP_KF // CLUSTERS, 1)), jnp.arange(GROUP_KF), side="right"))(jax.random.split(key_of[4], N_TM)).reshape((N_TM, GROUP_KF)).astype(jnp.int32),
        "damping": jnp.clip(jnp.exp(math.log(3.0) - 2.3025851 * jax.random.uniform(key_of[5], (N_TM, CLUSTERS), jnp.float32) ** block_scale(key_of[5], (N_TM, CLUSTERS), ((0, 8),), -0.2, 0.2)), 0.3, 3.0),
        "pair_first": set_ends(jax.random.randint(key_of[6], (N_TM, PAIR_GROUP), 0, GROUP_KF), jax.random.fold_in(key_of[6], 1), 0, GROUP_KF - 1).astype(jnp.int32),
        "pair_second": set_ends(jax.random.randint(key_of[7], (N_TM, PAIR_GROUP), 0, GROUP_KF), jax.random.fold_in(key_of[7], 1), 0, GROUP_KF - 1).astype(jnp.int32),
        "pair_blocks": scatter_about(key_of[8], (STATE, STATE, N_TM, PAIR_GROUP), STATE ** -0.5, 1.5, ((2, 8), (3, 4)), jnp.float32),
    }


def inertial(field, transition):
    total = field.shape[1]
    moved = jnp.einsum('ijk,jk->ik', transition, field, precision=lax.Precision.HIGHEST)
    following = jnp.concatenate([field[:, 1:], jnp.zeros((field.shape[0], 1), field.dtype)], axis=1)
    keep = jnp.where(jnp.arange(total) < total - 1, 1.0, 0.0).astype(field.dtype)
    errors = (following - moved) * keep[None, :]
    back = jnp.einsum('jik,jk->ik', transition, errors, precision=lax.Precision.HIGHEST)
    earlier = jnp.concatenate([jnp.zeros((field.shape[0], 1), field.dtype), errors[:, :-1]], axis=1)
    return earlier - back


def positions(slot_of):
    share = KF_DEV // N_TM
    index = jnp.arange(KEYFRAMES).astype(jnp.int32)
    block = index // KF_DEV
    tpos = block // N_CLUS
    cpos = block % N_CLUS
    group = slot_of // share
    inner = slot_of % share
    return ((group * N_CLUS + cpos) * KF_DEV + tpos * share + inner).astype(jnp.int32)


def visual(field, place, cluster_id, damping, pair_first, pair_second, pair_blocks):
    clustered = jnp.zeros_like(field).at[:, place].set(field)
    offsets = (jnp.arange(N_TM).astype(jnp.int32) * GROUP_KF)[:, None]
    heads = (pair_first + offsets).reshape(-1)
    tails = (pair_second + offsets).reshape(-1)
    blocks = pair_blocks.reshape(pair_blocks.shape[0], pair_blocks.shape[1], -1)
    near = jnp.take(clustered, heads, axis=1)
    far = jnp.take(clustered, tails, axis=1)
    errors = near - jnp.einsum('ijp,jp->ip', blocks, far, precision=lax.Precision.HIGHEST)
    back = jnp.einsum('jip,jp->ip', blocks, errors, precision=lax.Precision.HIGHEST)
    lam = jnp.take_along_axis(damping, cluster_id, axis=1).reshape(-1)
    image = jnp.zeros_like(field).at[:, heads].add(errors).at[:, tails].add(-back) + lam[None, :] * clustered
    return jnp.take(image, place, axis=1)


def reference(right_side, transition, precond, slot_of, cluster_id, damping, pair_first, pair_second, pair_blocks):
    place = positions(slot_of)

    def apply(field):
        return inertial(field, transition) + visual(field, place, cluster_id, damping, pair_first, pair_second, pair_blocks)

    def condition(field):
        return jnp.einsum('ijk,jk->ik', precond, field, precision=lax.Precision.HIGHEST)

    solution_field = jnp.zeros_like(right_side)
    residual = right_side
    scaled = condition(residual)
    direction = scaled
    rz_now = jnp.sum(residual * scaled)
    for step in range(ITERS):
        image = apply(direction)
        alpha = rz_now / jnp.sum(direction * image)
        solution_field = solution_field + alpha * direction
        residual = residual - alpha * image
        scaled = condition(residual)
        rz_next = jnp.sum(residual * scaled)
        direction = scaled + (rz_next / rz_now) * direction
        rz_now = rz_next
    return solution_field, residual
```

```python
import functools
import jax
import jax.numpy as jnp
from jax import lax
from jax.experimental import pallas as pl
from jax.experimental.pallas import tpu as pltpu
from jax.sharding import PartitionSpec as P

F32 = jnp.float32
BF16 = jnp.bfloat16
ROWS = 16
SUB = 256
LANE = 128
VMEM_LIMIT = 48 * 1024 * 1024


def iota(shape, axis):
    return lax.broadcasted_iota(jnp.int32, shape, axis)


def halves(value):
    high = value.astype(BF16).astype(F32)
    return high, value - high


def join(pieces):
    return pieces[0] if len(pieces) == 1 else jnp.concatenate(pieces, axis=1)


def hot_table(hot, index_ref, width):
    for start in range(0, width, SUB):
        low = index_ref[0:1, start : start + SUB] & (SUB - 1)
        table = jnp.where(iota((SUB, SUB), 0) == low, 1.0, 0.0)
        hot[:, start : start + SUB] = table.astype(BF16)


def column_to_row(column, state, share):
    spot = iota((ROWS, LANE), 1) % share
    row = iota((ROWS, LANE), 0)
    return jnp.sum(jnp.where((spot == row) & (row < state), column, 0.0), axis=0, keepdims=True)


def row_to_column(row, state):
    width = row.shape[1]
    sub = iota((ROWS, width), 0)
    keep = (sub == iota((ROWS, width), 1)) & (sub < state)
    return jnp.sum(jnp.where(keep, row, 0.0), axis=1, keepdims=True)


def note(column, scalar, state, share):
    spot = iota((1, LANE), 1) % share
    return jnp.where(spot == state, scalar, column_to_row(column, state, share))


def total(value):
    return jnp.sum(jnp.sum(value, axis=0, keepdims=True), axis=1, keepdims=True)


def apply_precond(precond, residual, scaled):
    state, width = residual.shape
    dot = jnp.zeros((state, LANE), F32)
    for start in range(0, width, LANE):
        at = slice(start, start + LANE)
        out = precond[0, :, at] * residual[0:1, at]
        for j in range(1, state):
            out = out + precond[j, :, at] * residual[j : j + 1, at]
        scaled[0:state, at] = out
        scaled[state:ROWS, at] = jnp.zeros((ROWS - state, LANE), F32)
        dot = dot + out * residual[:, at]
    return total(dot)


def send_states(scaled, dot, slot, hot, left, send, state):
    width = scaled.shape[1]
    groups, copies, _, share = send.shape
    parts = width // SUB
    for start in range(0, width, SUB):
        at = slice(start, start + SUB)
        high, low = halves(scaled[:, at])
        part = slot[0:1, at] >> 8
        for k in range(parts):
            left[k * 2 * ROWS : k * 2 * ROWS + ROWS, at] = jnp.where(part == k, high, 0.0).astype(BF16)
            left[k * 2 * ROWS + ROWS : (k + 1) * 2 * ROWS, at] = jnp.where(part == k, low, 0.0).astype(BF16)
    moved = lax.dot_general(left[...], hot[...], (((1,), (1,)), ((), ())), preferred_element_type=F32)
    notes = note(scaled[:, 0:1], dot, state, share)
    sub = iota((ROWS, share), 0)
    for k in range(parts):
        piece = moved[k * 2 * ROWS : k * 2 * ROWS + ROWS] + moved[k * 2 * ROWS + ROWS : (k + 1) * 2 * ROWS]
        for m in range(SUB // share):
            one = jnp.where(sub == state, notes[:, :share], piece[:, m * share : (m + 1) * share])
            for copy in range(copies):
                send[k * (SUB // share) + m, copy] = one


def begin_kernel(right, precond, slot, send, scaled, hot, left):
    state = right.shape[0]
    hot_table(hot, slot, right.shape[1])
    dot = apply_precond(precond, right, scaled)
    send_states(scaled, dot, slot, hot, left, send, state)


def group_kernel(n_time, n_clus, axes, got, heads, tails, blocks, damping, cluster, scaled, transition,
                 send, inertial, sums, field, hot, pulled, values, left, errors):
    state = transition.shape[0]
    width = scaled.shape[1]
    share = got.shape[2]
    pairs = heads.shape[1]
    parts = n_clus * width // SUB
    per_part = SUB // share
    chunks = pairs // LANE
    time_at, clus_at = lax.axis_index(axes[0]), lax.axis_index(axes[1])
    flat = time_at * n_clus + clus_at
    devices = n_time * n_clus

    def source(piece):
        return (piece % n_time) * n_clus + piece // n_time

    sums[...] = jnp.sum(got[:, state : state + 1, :], axis=0)

    following = row_to_column(got[jnp.minimum(flat + 1, devices - 1), state : state + 1, :], state)
    own = scaled[...]
    lane = iota((ROWS, width), 1)
    ahead = jnp.where(lane == width - 1, following, pltpu.roll(own, width - 1, 1))
    errors[...] = ahead
    for i in range(state):
        moved = jnp.sum(transition[i] * scaled[0:state, :], axis=0, keepdims=True)
        errors[i : i + 1, :] = errors[i : i + 1, :] - moved
    closed = (lane == width - 1) & (flat == devices - 1)
    error = jnp.where(closed | (iota((ROWS, width), 0) >= state), 0.0, errors[...])
    errors[...] = error
    prior = jnp.where(lane == 0, 0.0, pltpu.roll(error, 1, 1))
    inertial[state:ROWS, :] = jnp.zeros((ROWS - state, width), F32)
    energy = jnp.zeros((ROWS, LANE), F32)
    for start in range(0, width, LANE):
        at = slice(start, start + LANE)
        back = transition[0, :, at] * errors[0:1, at]
        for j in range(1, state):
            back = back + transition[j, :, at] * errors[j : j + 1, at]
        inertial[0:state, at] = prior[0:state, at] - back
        energy = energy + error[:, at] * error[:, at]
    product = total(energy)

    for k in range(parts):
        high, low = halves(join([got[source(k * per_part + m)] for m in range(per_part)]))
        field[k * 2 * ROWS : k * 2 * ROWS + ROWS, :] = high.astype(BF16)
        field[k * 2 * ROWS + ROWS : (k + 1) * 2 * ROWS, :] = low.astype(BF16)

    def pull(ends, base, n):
        at = pl.ds(pl.multiple_of(n * SUB, SUB), SUB)
        index = ends[0:1, at]
        low, part = index & (SUB - 1), index >> 8
        table = jnp.where(iota((SUB, SUB), 0) == low, 1.0, 0.0).astype(BF16)
        hot[:, pl.ds(pl.multiple_of(base * LANE + n * SUB, SUB), SUB)] = table
        found = jnp.dot(field[...], table, preferred_element_type=F32)
        out = jnp.zeros((ROWS, SUB), F32)
        for k in range(parts):
            one = found[k * 2 * ROWS : k * 2 * ROWS + ROWS] + found[k * 2 * ROWS + ROWS : (k + 1) * 2 * ROWS]
            out = jnp.where(part == k, one, out)
        for m in range(SUB // LANE):
            row = (base + n * (SUB // LANE) + m) * ROWS
            pulled[pl.ds(pl.multiple_of(row, ROWS), ROWS), :] = out[:, m * LANE : (m + 1) * LANE]

    def pull_both(n, carry):
        pull(heads, 0, n)
        pull(tails, chunks, n)
        return carry

    lax.fori_loop(0, pairs // SUB, pull_both, 0)

    squares = jnp.zeros((8, LANE), F32)
    for h in range(0, chunks, 8):
        far = [pulled[pl.ds((chunks + h) * ROWS + j, 8, stride=ROWS), :] for j in range(state)]
        back = [None] * state
        for i in range(state):
            row = [blocks[i * state + j, h : h + 8, :] for j in range(state)]
            f = pulled[pl.ds(h * ROWS + i, 8, stride=ROWS), :]
            for j in range(state):
                f = f - row[j] * far[j]
            squares = squares + f * f
            values[pl.ds(h * ROWS + i, 8, stride=ROWS), :] = f
            for j in range(state):
                back[j] = row[j] * f if i == 0 else back[j] + row[j] * f
        for j in range(state):
            values[pl.ds((chunks + h) * ROWS + j, 8, stride=ROWS), :] = -back[j]
        for j in range(state, ROWS):
            values[pl.ds(h * ROWS + j, 8, stride=ROWS), :] = jnp.zeros((8, LANE), F32)
            values[pl.ds((chunks + h) * ROWS + j, 8, stride=ROWS), :] = jnp.zeros((8, LANE), F32)
    product = product + total(squares)

    def spread(ends, base, n):
        at = pl.ds(pl.multiple_of(base * LANE + n * SUB, SUB), SUB)
        part = ends[0:1, pl.ds(pl.multiple_of(n * SUB, SUB), SUB)] >> 8
        row = (base + n * (SUB // LANE)) * ROWS
        high, low = halves(join([
            values[pl.ds(pl.multiple_of(row + m * ROWS, ROWS), ROWS), :] for m in range(SUB // LANE)
        ]))
        for k in range(parts):
            left[k * 2 * ROWS : k * 2 * ROWS + ROWS, at] = jnp.where(part == k, high, 0.0).astype(BF16)
            left[k * 2 * ROWS + ROWS : (k + 1) * 2 * ROWS, at] = jnp.where(part == k, low, 0.0).astype(BF16)

    def spread_both(n, carry):
        spread(heads, 0, n)
        spread(tails, chunks, n)
        return carry

    lax.fori_loop(0, pairs // SUB, spread_both, 0)
    summed = lax.dot_general(left[...], hot[...], (((1,), (1,)), ((), ())), preferred_element_type=F32)

    lam = jnp.zeros((1, width), F32)
    for label in range(damping.shape[1]):
        lam = jnp.where(cluster[...] == label, damping[0:1, label : label + 1], lam)
    sub = iota((ROWS, share), 0)
    damped = jnp.zeros((ROWS, share), F32)
    out = {}
    for k in range(parts):
        one = summed[k * 2 * ROWS : k * 2 * ROWS + ROWS] + summed[k * 2 * ROWS + ROWS : (k + 1) * 2 * ROWS]
        for m in range(per_part):
            piece = k * per_part + m
            c, t = piece // n_time, piece % n_time
            here = jnp.where(clus_at == c, lam[:, t * share : (t + 1) * share], 0.0)
            states = jnp.where(sub < state, got[source(piece)], 0.0)
            extra = here * states
            damped = damped + extra * states
            send[source(piece)] = one[:, m * share : (m + 1) * share] + extra
    product = product + total(damped)
    notes = note(error[:, width - 1 : width], product, state, share)
    for d in range(devices):
        send[d, state : state + 1, :] = notes[:, :share]


def image_of(n_time, n_clus, axes, got, inertial, slot, hot, field, image, state):
    width = image.shape[1]
    share = got.shape[2]
    per_part = SUB // share
    parts = width // SUB
    flat = lax.axis_index(axes[0]) * n_clus + lax.axis_index(axes[1])
    for k in range(parts):
        pieces = []
        for m in range(per_part):
            t = k * per_part + m
            one = got[t * n_clus]
            for c in range(1, n_clus):
                one = one + got[t * n_clus + c]
            pieces.append(one)
        high, low = halves(join(pieces))
        field[k * 2 * ROWS : k * 2 * ROWS + ROWS, :] = high.astype(BF16)
        field[k * 2 * ROWS + ROWS : (k + 1) * 2 * ROWS, :] = low.astype(BF16)
    prior = row_to_column(got[jnp.maximum(flat - 1, 0), state : state + 1, :], state)
    prior = jnp.where(flat == 0, 0.0, prior)
    for start in range(0, width, SUB):
        at = slice(start, start + SUB)
        found = jnp.dot(field[...], hot[:, at], preferred_element_type=F32)
        part = slot[0:1, at] >> 8
        out = jnp.zeros((ROWS, SUB), F32)
        for k in range(parts):
            one = found[k * 2 * ROWS : k * 2 * ROWS + ROWS] + found[k * 2 * ROWS + ROWS : (k + 1) * 2 * ROWS]
            out = jnp.where(part == k, one, out)
        out = out + inertial[:, at]
        if start == 0:
            out = jnp.where(iota((ROWS, SUB), 1) == 0, out + prior, out)
        image[:, at] = out
    return jnp.sum(got[:, state : state + 1, :], axis=0)[:, state : state + 1]


def step_kernel(n_time, n_clus, axes, got, right, inertial, precond, slot, sums,
                send, scaled, residual, image, scalars, hot, field, left):
    state, width = right.shape
    hot_table(hot, slot, width)
    product = image_of(n_time, n_clus, axes, got, inertial, slot, hot, field, image, state)
    alpha = sums[0:1, state : state + 1] / product
    residual[...] = right[...] - alpha * image[0:state, :]
    dot = apply_precond(precond, residual, scaled)
    send_states(scaled, dot, slot, hot, left, send, state)
    scalars[...] = jnp.broadcast_to(alpha, scalars.shape)


def end_kernel(n_time, n_clus, axes, got, residual, inertial, slot, first, scaled, along, sums, sums_next, scalars,
               solution_field, residual_out, hot, field, image):
    state, width = residual.shape
    hot_table(hot, slot, width)
    product = image_of(n_time, n_clus, axes, got, inertial, slot, hot, field, image, state)
    alpha = scalars[0:1, 0:1]
    rz, rz_next = sums[0:1, state : state + 1], sums_next[0:1, state : state + 1]
    ratio = rz_next / rz
    step = rz_next / (product - ratio * rz_next / alpha)
    direction = scaled[0:state, :] + ratio * first[0:state, :]
    solution_field[...] = alpha * first[0:state, :] + step * direction
    residual_out[...] = residual[...] - step * (image[0:state, :] + ratio * along[0:state, :])


def on_device(
    right_side,
    transition,
    precond,
    slot_of,
    cluster_id,
    damping,
    pair_first,
    pair_second,
    pair_blocks,
):
    axes = ("tm", "clus")
    state, width = right_side.shape
    n_time = lax.axis_size("tm")
    n_clus = lax.axis_size("clus")
    devices = n_time * n_clus
    share = width // n_time
    pairs = pair_first.shape[1]
    positions = n_clus * width
    slot = slot_of.reshape(1, width)
    blocks = pair_blocks.reshape(state * state, pairs // LANE, LANE)
    params = pltpu.CompilerParams(vmem_limit_bytes=VMEM_LIMIT)

    def like(*shape):
        return jax.ShapeDtypeStruct(shape, F32)

    message = like(devices, ROWS, share)
    outgoing = like(n_time, n_clus, ROWS, share)
    row = like(1, share)
    tile = like(ROWS, width)
    hot = pltpu.VMEM((SUB, width), BF16)
    left = pltpu.VMEM((2 * ROWS * width // SUB, width), BF16)
    field = pltpu.VMEM((2 * ROWS * width // SUB, SUB), BF16)

    def exchange(sent):
        return lax.all_to_all(sent.reshape(devices, ROWS, share), axes, split_axis=0, concat_axis=0, tiled=True)

    def grouped(got, scaled):
        return pl.pallas_call(
            functools.partial(group_kernel, n_time, n_clus, axes),
            out_shape=(message, tile, row),
            scratch_shapes=[
                pltpu.VMEM((2 * ROWS * positions // SUB, SUB), BF16),
                pltpu.VMEM((SUB, 2 * pairs), BF16),
                pltpu.VMEM((2 * pairs // LANE * ROWS, LANE), F32),
                pltpu.VMEM((2 * pairs // LANE * ROWS, LANE), F32),
                pltpu.VMEM((2 * ROWS * positions // SUB, 2 * pairs), BF16),
                pltpu.VMEM((ROWS, width), F32),
            ],
            compiler_params=params,
            name="group",
        )(got, pair_first, pair_second, blocks, damping, cluster_id, scaled, transition)

    sent, first = pl.pallas_call(
        begin_kernel,
        out_shape=(outgoing, tile),
        scratch_shapes=[hot, left],
        compiler_params=params,
        name="begin",
    )(right_side, precond, slot)
    back, inertial, sums = grouped(exchange(sent), first)
    sent, scaled, residual, along, scalars = pl.pallas_call(
        functools.partial(step_kernel, n_time, n_clus, axes),
        out_shape=(outgoing, tile, like(state, width), tile, like(1, LANE)),
        scratch_shapes=[hot, field, left],
        compiler_params=params,
        name="step",
    )(exchange(back), right_side, inertial, precond, slot, sums)
    back, inertial, sums_next = grouped(exchange(sent), scaled)
    return pl.pallas_call(
        functools.partial(end_kernel, n_time, n_clus, axes),
        out_shape=(like(state, width), like(state, width)),
        scratch_shapes=[hot, field, pltpu.VMEM((ROWS, width), F32)],
        compiler_params=params,
        name="end",
    )(exchange(back), residual, inertial, slot, first, scaled, along, sums, sums_next, scalars)


def solution(mesh):
    placed = (
        P(None, ("tm", "clus")),
        P(None, None, ("tm", "clus")),
        P(None, None, ("tm", "clus")),
        P(("tm", "clus")),
        P("tm", "clus"),
        P("tm", None),
        P("tm", "clus"),
        P("tm", "clus"),
        P(None, None, "tm", "clus"),
    )
    return jax.shard_map(
        on_device,
        mesh=mesh,
        in_specs=placed,
        out_specs=(P(None, ("tm", "clus")), P(None, ("tm", "clus"))),
        check_vma=False,
    )
```

```python
import functools
import jax
import jax.numpy as jnp
from jax import lax
from jax.experimental import pallas as pl
from jax.experimental.pallas import tpu as pltpu
from jax.sharding import PartitionSpec as P

F32 = jnp.float32
BF16 = jnp.bfloat16
ROWS = 16
SUB = 256
LANE = 128
VMEM_LIMIT = 16 * 1024 * 1024


def iota(shape, axis):
    return lax.broadcasted_iota(jnp.int32, shape, axis)


def halves(value):
    high = value.astype(BF16)
    return high, (value - high.astype(F32)).astype(BF16)


def join(pieces):
    return pieces[0] if len(pieces) == 1 else jnp.concatenate(pieces, axis=1)


def spread_row(row, count):
    return jnp.broadcast_to(row.astype(F32), (count, row.shape[1])).astype(BF16)


def hot_tile(index):
    rows = iota((SUB, index.shape[1]), 0).astype(F32).astype(BF16)
    low = spread_row(index & (SUB - 1), SUB)
    return jnp.where(rows == low, jnp.ones((), BF16), jnp.zeros((), BF16))


def hot_table(hot, index_ref, width):
    for start in range(0, width, SUB):
        hot[:, start : start + SUB] = hot_tile(index_ref[0:1, start : start + SUB])


def masked(part, k, value):
    return jnp.where(part == jnp.asarray(k, BF16), value, jnp.zeros((), BF16))


def both(left, right, contract):
    return lax.dot_general(left, right, (contract, ((), ())), preferred_element_type=F32)


def column_to_row(column, state, share):
    spot = iota((ROWS, LANE), 1) % share
    row = iota((ROWS, LANE), 0)
    return jnp.sum(jnp.where((spot == row) & (row < state), column, 0.0), axis=0, keepdims=True)


def row_to_column(row, state):
    width = row.shape[1]
    sub = iota((ROWS, width), 0)
    keep = (sub == iota((ROWS, width), 1)) & (sub < state)
    return jnp.sum(jnp.where(keep, row, 0.0), axis=1, keepdims=True)


def note(column, scalar, state, share):
    spot = iota((1, LANE), 1) % share
    return jnp.where(spot == state, scalar, column_to_row(column, state, share))


def total(value):
    return jnp.sum(jnp.sum(value, axis=0, keepdims=True), axis=1, keepdims=True)


def apply_precond(precond, residual, scaled):
    state, width = residual.shape
    dot = jnp.zeros((state, LANE), F32)
    for start in range(0, width, LANE):
        at = slice(start, start + LANE)
        out = precond[0, :, at] * residual[0:1, at]
        for j in range(1, state):
            out = out + precond[j, :, at] * residual[j : j + 1, at]
        scaled[0:state, at] = out
        scaled[state:ROWS, at] = jnp.zeros((ROWS - state, LANE), F32)
        dot = dot + out * residual[:, at]
    return total(dot)


def send_states(scaled, dot, slot, hot, left, send, state):
    width = scaled.shape[1]
    groups, copies, _, share = send.shape
    parts = width // SUB
    for start in range(0, width, SUB):
        at = slice(start, start + SUB)
        also = slice(width + start, width + start + SUB)
        high, low = halves(scaled[:, at])
        part = spread_row(slot[0:1, at] >> 8, ROWS)
        for k in range(parts):
            rows = slice(k * ROWS, (k + 1) * ROWS)
            left[rows, at] = masked(part, k, high)
            left[rows, also] = masked(part, k, low)
    table = hot[...]
    moved = both(left[:, :width], table, ((1,), (1,))) + both(left[:, width:], table, ((1,), (1,)))
    notes = note(scaled[:, 0:1], dot, state, share)
    sub = iota((ROWS, share), 0)
    for k in range(parts):
        piece = moved[k * ROWS : (k + 1) * ROWS]
        for m in range(SUB // share):
            one = jnp.where(sub == state, notes[:, :share], piece[:, m * share : (m + 1) * share])
            for copy in range(copies):
                send[k * (SUB // share) + m, copy] = one


def begin_kernel(right_in, precond_in, slot_in, send, scaled, hot, left, right, precond, slot, sems):
    state = right.shape[0]
    copies = [
        pltpu.make_async_copy(source, place, sems.at[i])
        for i, (source, place) in enumerate(((precond_in, precond), (right_in, right), (slot_in, slot)))
    ]
    for copy in copies:
        copy.start()
    copies[2].wait()
    hot_table(hot, slot, right.shape[1])
    copies[1].wait()
    copies[0].wait()
    dot = apply_precond(precond, right, scaled)
    send_states(scaled, dot, slot, hot, left, send, state)


def group_kernel(n_time, n_clus, axes, got, heads, tails, blocks, damping, cluster, scaled, transition,
                 send, inertial, sums, field, hot, pulled, values, left, errors):
    state = transition.shape[0]
    width = scaled.shape[1]
    share = got.shape[2]
    pairs = heads.shape[1]
    parts = n_clus * width // SUB
    per_part = SUB // share
    chunks = pairs // LANE
    time_at, clus_at = lax.axis_index(axes[0]), lax.axis_index(axes[1])
    flat = time_at * n_clus + clus_at
    devices = n_time * n_clus

    def source(piece):
        return (piece % n_time) * n_clus + piece // n_time

    sums[...] = jnp.sum(got[:, state : state + 1, :], axis=0)

    following = row_to_column(got[jnp.minimum(flat + 1, devices - 1), state : state + 1, :], state)
    own = scaled[...]
    lane = iota((ROWS, width), 1)
    ahead = jnp.where(lane == width - 1, following, pltpu.roll(own, width - 1, 1))
    errors[...] = ahead
    for i in range(state):
        moved = jnp.sum(transition[i] * scaled[0:state, :], axis=0, keepdims=True)
        errors[i : i + 1, :] = errors[i : i + 1, :] - moved
    closed = (lane == width - 1) & (flat == devices - 1)
    error = jnp.where(closed | (iota((ROWS, width), 0) >= state), 0.0, errors[...])
    errors[...] = error
    prior = jnp.where(lane == 0, 0.0, pltpu.roll(error, 1, 1))
    inertial[state:ROWS, :] = jnp.zeros((ROWS - state, width), F32)
    energy = jnp.zeros((ROWS, LANE), F32)
    for start in range(0, width, LANE):
        at = slice(start, start + LANE)
        back = transition[0, :, at] * errors[0:1, at]
        for j in range(1, state):
            back = back + transition[j, :, at] * errors[j : j + 1, at]
        inertial[0:state, at] = prior[0:state, at] - back
        energy = energy + error[:, at] * error[:, at]
    product = total(energy)

    for k in range(parts):
        rows = slice(k * ROWS, (k + 1) * ROWS)
        field[rows, 0:SUB], field[rows, SUB:] = halves(join([got[source(k * per_part + m)] for m in range(per_part)]))

    def pull(ends, base, n):
        index = ends[0:1, n * SUB : (n + 1) * SUB]
        part = index >> 8
        table = hot_tile(index)
        hot[:, base * LANE + n * SUB : base * LANE + (n + 1) * SUB] = table
        found = both(field[:, 0:SUB], table, ((1,), (0,))) + both(field[:, SUB:], table, ((1,), (0,)))
        out = found[0:ROWS]
        for k in range(1, parts):
            out = jnp.where(part == k, found[k * ROWS : (k + 1) * ROWS], out)
        for m in range(SUB // LANE):
            row = (base + n * (SUB // LANE) + m) * ROWS
            pulled[row : row + ROWS, :] = out[:, m * LANE : (m + 1) * LANE]

    for n in range(pairs // SUB):
        pull(heads, 0, n)
        pull(tails, chunks, n)

    squares = jnp.zeros((8, LANE), F32)
    for h in range(0, chunks, 8):
        far = [pulled[pl.ds((chunks + h) * ROWS + j, 8, stride=ROWS), :] for j in range(state)]
        back = [None] * state
        for i in range(state):
            row = [blocks[i * state + j, h : h + 8, :] for j in range(state)]
            f = pulled[pl.ds(h * ROWS + i, 8, stride=ROWS), :]
            for j in range(state):
                f = f - row[j] * far[j]
            squares = squares + f * f
            values[pl.ds(h * ROWS + i, 8, stride=ROWS), :] = f
            for j in range(state):
                back[j] = row[j] * f if i == 0 else back[j] + row[j] * f
        for j in range(state):
            values[pl.ds((chunks + h) * ROWS + j, 8, stride=ROWS), :] = -back[j]
        for j in range(state, ROWS):
            values[pl.ds(h * ROWS + j, 8, stride=ROWS), :] = jnp.zeros((8, LANE), F32)
            values[pl.ds((chunks + h) * ROWS + j, 8, stride=ROWS), :] = jnp.zeros((8, LANE), F32)
    product = product + total(squares)

    def spread(ends, base, n):
        at = slice(base * LANE + n * SUB, base * LANE + (n + 1) * SUB)
        also = slice(2 * pairs + at.start, 2 * pairs + at.stop)
        part = spread_row(ends[0:1, n * SUB : (n + 1) * SUB] >> 8, ROWS)
        row = (base + n * (SUB // LANE)) * ROWS
        high, low = halves(join([values[row + m * ROWS : row + (m + 1) * ROWS, :] for m in range(SUB // LANE)]))
        for k in range(parts):
            rows = slice(k * ROWS, (k + 1) * ROWS)
            left[rows, at] = masked(part, k, high)
            left[rows, also] = masked(part, k, low)

    for n in range(pairs // SUB):
        spread(heads, 0, n)
        spread(tails, chunks, n)
    table = hot[...]
    summed = both(left[:, : 2 * pairs], table, ((1,), (1,))) + both(left[:, 2 * pairs :], table, ((1,), (1,)))

    lam = jnp.zeros((1, width), F32)
    for label in range(damping.shape[1]):
        lam = jnp.where(cluster[...] == label, damping[0:1, label : label + 1], lam)
    sub = iota((ROWS, share), 0)
    damped = jnp.zeros((ROWS, share), F32)
    out = {}
    for k in range(parts):
        one = summed[k * ROWS : (k + 1) * ROWS]
        for m in range(per_part):
            piece = k * per_part + m
            c, t = piece // n_time, piece % n_time
            here = jnp.where(clus_at == c, lam[:, t * share : (t + 1) * share], 0.0)
            states = jnp.where(sub < state, got[source(piece)], 0.0)
            extra = here * states
            damped = damped + extra * states
            send[source(piece)] = one[:, m * share : (m + 1) * share] + extra
    product = product + total(damped)
    notes = note(error[:, width - 1 : width], product, state, share)
    for d in range(devices):
        send[d, state : state + 1, :] = notes[:, :share]


def image_of(n_time, n_clus, axes, got, inertial, slot, hot, field, image, state):
    width = image.shape[1]
    share = got.shape[2]
    per_part = SUB // share
    parts = width // SUB
    flat = lax.axis_index(axes[0]) * n_clus + lax.axis_index(axes[1])
    for k in range(parts):
        pieces = []
        for m in range(per_part):
            t = k * per_part + m
            one = got[t * n_clus]
            for c in range(1, n_clus):
                one = one + got[t * n_clus + c]
            pieces.append(one)
        rows = slice(k * ROWS, (k + 1) * ROWS)
        field[rows, 0:SUB], field[rows, SUB:] = halves(join(pieces))
    prior = row_to_column(got[jnp.maximum(flat - 1, 0), state : state + 1, :], state)
    prior = jnp.where(flat == 0, 0.0, prior)
    for start in range(0, width, SUB):
        at = slice(start, start + SUB)
        table = hot[:, at]
        found = both(field[:, 0:SUB], table, ((1,), (0,))) + both(field[:, SUB:], table, ((1,), (0,)))
        part = slot[0:1, at] >> 8
        out = found[0:ROWS]
        for k in range(1, parts):
            out = jnp.where(part == k, found[k * ROWS : (k + 1) * ROWS], out)
        out = out + inertial[:, at]
        if start == 0:
            out = jnp.where(iota((ROWS, SUB), 1) == 0, out + prior, out)
        image[:, at] = out
    return jnp.sum(got[:, state : state + 1, :], axis=0)[:, state : state + 1]


def step_kernel(n_time, n_clus, axes, got, right, inertial, precond, slot, sums,
                send, scaled, residual, image, scalars, hot, field, left):
    state, width = right.shape
    hot_table(hot, slot, width)
    product = image_of(n_time, n_clus, axes, got, inertial, slot, hot, field, image, state)
    alpha = sums[0:1, state : state + 1] / product
    residual[...] = right[...] - alpha * image[0:state, :]
    dot = apply_precond(precond, residual, scaled)
    send_states(scaled, dot, slot, hot, left, send, state)
    scalars[...] = jnp.broadcast_to(alpha, scalars.shape)


def end_kernel(n_time, n_clus, axes, got, residual, inertial, slot, first, scaled, along, sums, sums_next, scalars,
               solution_field, residual_out, hot, field, image):
    state, width = residual.shape
    hot_table(hot, slot, width)
    product = image_of(n_time, n_clus, axes, got, inertial, slot, hot, field, image, state)
    alpha = scalars[0:1, 0:1]
    rz, rz_next = sums[0:1, state : state + 1], sums_next[0:1, state : state + 1]
    ratio = rz_next / rz
    step = rz_next / (product - ratio * rz_next / alpha)
    direction = scaled[0:state, :] + ratio * first[0:state, :]
    solution_field[...] = alpha * first[0:state, :] + step * direction
    residual_out[...] = residual[...] - step * (image[0:state, :] + ratio * along[0:state, :])


def on_device(
    right_side,
    transition,
    precond,
    slot_of,
    cluster_id,
    damping,
    pair_first,
    pair_second,
    pair_blocks,
):
    axes = ("tm", "clus")
    state, width = right_side.shape
    n_time = lax.axis_size("tm")
    n_clus = lax.axis_size("clus")
    devices = n_time * n_clus
    share = width // n_time
    pairs = pair_first.shape[1]
    positions = n_clus * width
    slot = slot_of.reshape(1, width)
    blocks = pair_blocks.reshape(state * state, pairs // LANE, LANE)
    params = pltpu.CompilerParams(vmem_limit_bytes=VMEM_LIMIT)

    def like(*shape):
        return jax.ShapeDtypeStruct(shape, F32)

    message = like(devices, ROWS, share)
    outgoing = like(n_time, n_clus, ROWS, share)
    row = like(1, share)
    tile = like(ROWS, width)
    hot = pltpu.VMEM((SUB, width), BF16)
    left = pltpu.VMEM((ROWS * width // SUB, 2 * width), BF16)
    field = pltpu.VMEM((ROWS * width // SUB, 2 * SUB), BF16)

    def exchange(sent):
        return lax.all_to_all(sent.reshape(devices, ROWS, share), axes, split_axis=0, concat_axis=0, tiled=True)

    def grouped(got, scaled):
        return pl.pallas_call(
            functools.partial(group_kernel, n_time, n_clus, axes),
            out_shape=(message, tile, row),
            scratch_shapes=[
                pltpu.VMEM((ROWS * positions // SUB, 2 * SUB), BF16),
                pltpu.VMEM((SUB, 2 * pairs), BF16),
                pltpu.VMEM((2 * pairs // LANE * ROWS, LANE), F32),
                pltpu.VMEM((2 * pairs // LANE * ROWS, LANE), F32),
                pltpu.VMEM((ROWS * positions // SUB, 4 * pairs), BF16),
                pltpu.VMEM((ROWS, width), F32),
            ],
            compiler_params=params,
            name="group",
        )(got, pair_first, pair_second, blocks, damping, cluster_id, scaled, transition)

    sent, first = pl.pallas_call(
        begin_kernel,
        out_shape=(outgoing, tile),
        in_specs=[pl.BlockSpec(memory_space=pltpu.HBM)] * 3,
        scratch_shapes=[
            hot,
            left,
            pltpu.VMEM(right_side.shape, F32),
            pltpu.VMEM(precond.shape, F32),
            pltpu.VMEM(slot.shape, jnp.int32),
            pltpu.SemaphoreType.DMA((3,)),
        ],
        compiler_params=params,
        name="begin",
    )(right_side, precond, slot)
    back, inertial, sums = grouped(exchange(sent), first)
    sent, scaled, residual, along, scalars = pl.pallas_call(
        functools.partial(step_kernel, n_time, n_clus, axes),
        out_shape=(outgoing, tile, like(state, width), tile, like(1, LANE)),
        scratch_shapes=[hot, field, left],
        compiler_params=params,
        name="step",
    )(exchange(back), right_side, inertial, precond, slot, sums)
    back, inertial, sums_next = grouped(exchange(sent), scaled)
    return pl.pallas_call(
        functools.partial(end_kernel, n_time, n_clus, axes),
        out_shape=(like(state, width), like(state, width)),
        scratch_shapes=[hot, field, pltpu.VMEM((ROWS, width), F32)],
        compiler_params=params,
        name="end",
    )(exchange(back), residual, inertial, slot, first, scaled, along, sums, sums_next, scalars)


def solution(mesh):
    placed = (
        P(None, ("tm", "clus")),
        P(None, None, ("tm", "clus")),
        P(None, None, ("tm", "clus")),
        P(("tm", "clus")),
        P("tm", "clus"),
        P("tm", None),
        P("tm", "clus"),
        P("tm", "clus"),
        P(None, None, "tm", "clus"),
    )
    return jax.shard_map(
        on_device,
        mesh=mesh,
        in_specs=placed,
        out_specs=(P(None, ("tm", "clus")), P(None, ("tm", "clus"))),
        check_vma=False,
    )
```

```python
import functools
import jax
import jax.numpy as jnp
from jax import lax
from jax.experimental import pallas as pl
from jax.experimental.pallas import tpu as pltpu
from jax.sharding import PartitionSpec as P

F32 = jnp.float32
BF16 = jnp.bfloat16
ROWS = 16
SUB = 256
LANE = 128
VMEM_LIMIT = 16 * 1024 * 1024


def iota(shape, axis):
    return lax.broadcasted_iota(jnp.int32, shape, axis)


def halves(value):
    high = value.astype(BF16)
    return high, (value - high.astype(F32)).astype(BF16)


def join(pieces):
    return pieces[0] if len(pieces) == 1 else jnp.concatenate(pieces, axis=1)


def spread_row(row, count):
    return jnp.broadcast_to(row.astype(F32), (count, row.shape[1])).astype(BF16)


def hot_tile(index):
    rows = iota((SUB, index.shape[1]), 0).astype(F32).astype(BF16)
    low = spread_row(index & (SUB - 1), SUB)
    return jnp.where(rows == low, jnp.ones((), BF16), jnp.zeros((), BF16))


def hot_table(hot, index_ref, width):
    for start in range(0, width, SUB):
        hot[:, start : start + SUB] = hot_tile(index_ref[0:1, start : start + SUB])


def masked(part, k, value):
    return jnp.where(part == jnp.asarray(k, BF16), value, jnp.zeros((), BF16))


def both(left, right, contract):
    return lax.dot_general(left, right, (contract, ((), ())), preferred_element_type=F32)


def column_to_row(column, state, share):
    spot = iota((ROWS, LANE), 1) % share
    row = iota((ROWS, LANE), 0)
    return jnp.sum(jnp.where((spot == row) & (row < state), column, 0.0), axis=0, keepdims=True)


def row_to_column(row, state):
    width = row.shape[1]
    sub = iota((ROWS, width), 0)
    keep = (sub == iota((ROWS, width), 1)) & (sub < state)
    return jnp.sum(jnp.where(keep, row, 0.0), axis=1, keepdims=True)


def note(column, scalar, state, share):
    spot = iota((1, LANE), 1) % share
    return jnp.where(spot == state, scalar, column_to_row(column, state, share))


def total(value):
    return jnp.sum(jnp.sum(value, axis=0, keepdims=True), axis=1, keepdims=True)


def apply_precond(precond, residual, scaled):
    state, width = residual.shape
    dot = jnp.zeros((state, LANE), F32)
    for start in range(0, width, LANE):
        at = slice(start, start + LANE)
        out = precond[0, :, at] * residual[0:1, at]
        for j in range(1, state):
            out = out + precond[j, :, at] * residual[j : j + 1, at]
        scaled[0:state, at] = out
        scaled[state:ROWS, at] = jnp.zeros((ROWS - state, LANE), F32)
        dot = dot + out * residual[:, at]
    return total(dot)


def send_states(scaled, dot, slot, hot, left, send, state):
    width = scaled.shape[1]
    groups, copies, _, share = send.shape
    parts = width // SUB
    for start in range(0, width, SUB):
        at = slice(start, start + SUB)
        also = slice(width + start, width + start + SUB)
        high, low = halves(scaled[:, at])
        part = spread_row(slot[0:1, at] >> 8, ROWS)
        for k in range(parts):
            rows = slice(k * ROWS, (k + 1) * ROWS)
            left[rows, at] = masked(part, k, high)
            left[rows, also] = masked(part, k, low)
    table = hot[...]
    moved = both(left[:, :width], table, ((1,), (1,))) + both(left[:, width:], table, ((1,), (1,)))
    notes = note(scaled[:, 0:1], dot, state, share)
    sub = iota((ROWS, share), 0)
    for k in range(parts):
        piece = moved[k * ROWS : (k + 1) * ROWS]
        for m in range(SUB // share):
            one = jnp.where(sub == state, notes[:, :share], piece[:, m * share : (m + 1) * share])
            for copy in range(copies):
                send[k * (SUB // share) + m, copy] = one


def begin_kernel(right_in, precond_in, slot_in, send, scaled, hot, left, right, precond, slot, sems):
    state = right.shape[0]
    copies = fetch(sems, (precond_in, precond), (right_in, right), (slot_in, slot))
    copies[2].wait()
    hot_table(hot, slot, right.shape[1])
    copies[1].wait()
    copies[0].wait()
    dot = apply_precond(precond, right, scaled)
    send_states(scaled, dot, slot, hot, left, send, state)


def fetch(sems, *pairs):
    copies = [pltpu.make_async_copy(source, place, sems.at[i]) for i, (source, place) in enumerate(pairs)]
    for copy in copies:
        copy.start()
    return copies


def tables_kernel(heads_in, tails_in, blocks_in, damping_in, cluster_in,
                  hot, heads, tails, blocks, lam, damping, cluster, sems):
    copies = fetch(sems, (heads_in, heads), (tails_in, tails), (damping_in, damping), (cluster_in, cluster),
                   (blocks_in, blocks))
    pairs = heads.shape[1]
    copies[0].wait()
    hot_table(hot.at[:, 0:pairs], heads, pairs)
    copies[1].wait()
    hot_table(hot.at[:, pairs:], tails, pairs)
    copies[2].wait()
    copies[3].wait()
    row = jnp.zeros(lam.shape, F32)
    for label in range(damping.shape[1]):
        row = jnp.where(cluster[...] == label, damping[0:1, label : label + 1], row)
    lam[...] = row
    copies[4].wait()


def inertial_kernel(scaled, transition_in, errors, inertial, ending, transition, sems):
    state = transition.shape[0]
    width = scaled.shape[1]
    (copy,) = fetch(sems, (transition_in, transition))
    lane = iota((ROWS, width), 1)
    errors[...] = jnp.where(lane == width - 1, 0.0, pltpu.roll(scaled[...], width - 1, 1))
    copy.wait()
    for i in range(state):
        moved = jnp.sum(transition[i] * scaled[0:state, :], axis=0, keepdims=True)
        errors[i : i + 1, :] = errors[i : i + 1, :] - moved
    prior = jnp.where(lane == 0, 0.0, pltpu.roll(errors[...], 1, 1))
    inertial[state:ROWS, :] = jnp.zeros((ROWS - state, width), F32)
    for start in range(0, width - LANE, LANE):
        at = slice(start, start + LANE)
        inertial[0:state, at] = prior[0:state, at] - back_product(transition, errors, at)
    inertial[0:state, width - LANE :] = prior[0:state, width - LANE :]
    ending[...] = transition[:, :, width - LANE :]


def back_product(transition, errors, at):
    back = transition[0, :, at] * errors[0:1, at]
    for j in range(1, transition.shape[0]):
        back = back + transition[j, :, at] * errors[j : j + 1, at]
    return back


def group_kernel(n_time, n_clus, axes, got, heads, tails, blocks, hot, lam, errors, partial, transition,
                 send, inertial, sums, field, pulled, values, left, last):
    state = transition.shape[0]
    width = errors.shape[1]
    share = got.shape[2]
    pairs = heads.shape[1]
    parts = n_clus * width // SUB
    per_part = SUB // share
    chunks = pairs // LANE
    time_at, clus_at = lax.axis_index(axes[0]), lax.axis_index(axes[1])
    flat = time_at * n_clus + clus_at
    devices = n_time * n_clus

    def source(piece):
        return (piece % n_time) * n_clus + piece // n_time

    sums[...] = jnp.sum(got[:, state : state + 1, :], axis=0)

    following = row_to_column(got[jnp.minimum(flat + 1, devices - 1), state : state + 1, :], state)
    at = slice(width - LANE, width)
    ending = iota((ROWS, LANE), 1) == LANE - 1
    closed = ending & (flat == devices - 1)
    ahead = jnp.where(ending, errors[:, at] + following, errors[:, at])
    last[...] = jnp.where(closed | (iota((ROWS, LANE), 0) >= state), 0.0, ahead)
    energy = last[...] * last[...]
    for start in range(0, width - LANE, LANE):
        block = errors[:, start : start + LANE]
        energy = energy + jnp.where(iota((ROWS, LANE), 0) < state, block * block, 0.0)
    product = total(energy)
    inertial[:, 0 : width - LANE] = partial[:, 0 : width - LANE]
    inertial[state:ROWS, at] = partial[state:ROWS, at]
    back = transition[0] * last[0:1, :]
    for j in range(1, state):
        back = back + transition[j] * last[j : j + 1, :]
    inertial[0:state, at] = partial[0:state, at] - back

    for k in range(parts):
        rows = slice(k * ROWS, (k + 1) * ROWS)
        field[rows, 0:SUB], field[rows, SUB:] = halves(join([got[source(k * per_part + m)] for m in range(per_part)]))

    def pull(ends, base, n):
        part = ends[0:1, n * SUB : (n + 1) * SUB] >> 8
        table = hot[:, base * LANE + n * SUB : base * LANE + (n + 1) * SUB]
        found = both(field[:, 0:SUB], table, ((1,), (0,))) + both(field[:, SUB:], table, ((1,), (0,)))
        out = found[0:ROWS]
        for k in range(1, parts):
            out = jnp.where(part == k, found[k * ROWS : (k + 1) * ROWS], out)
        for m in range(SUB // LANE):
            row = (base + n * (SUB // LANE) + m) * ROWS
            pulled[row : row + ROWS, :] = out[:, m * LANE : (m + 1) * LANE]

    for n in range(pairs // SUB):
        pull(heads, 0, n)
        pull(tails, chunks, n)

    squares = jnp.zeros((8, LANE), F32)
    for h in range(0, chunks, 8):
        far = [pulled[pl.ds((chunks + h) * ROWS + j, 8, stride=ROWS), :] for j in range(state)]
        back = [None] * state
        for i in range(state):
            row = [blocks[i * state + j, h : h + 8, :] for j in range(state)]
            f = pulled[pl.ds(h * ROWS + i, 8, stride=ROWS), :]
            for j in range(state):
                f = f - row[j] * far[j]
            squares = squares + f * f
            values[pl.ds(h * ROWS + i, 8, stride=ROWS), :] = f
            for j in range(state):
                back[j] = row[j] * f if i == 0 else back[j] + row[j] * f
        for j in range(state):
            values[pl.ds((chunks + h) * ROWS + j, 8, stride=ROWS), :] = -back[j]
        for j in range(state, ROWS):
            values[pl.ds(h * ROWS + j, 8, stride=ROWS), :] = jnp.zeros((8, LANE), F32)
            values[pl.ds((chunks + h) * ROWS + j, 8, stride=ROWS), :] = jnp.zeros((8, LANE), F32)
    product = product + total(squares)

    def spread(ends, base, n):
        at = slice(base * LANE + n * SUB, base * LANE + (n + 1) * SUB)
        also = slice(2 * pairs + at.start, 2 * pairs + at.stop)
        part = spread_row(ends[0:1, n * SUB : (n + 1) * SUB] >> 8, ROWS)
        row = (base + n * (SUB // LANE)) * ROWS
        high, low = halves(join([values[row + m * ROWS : row + (m + 1) * ROWS, :] for m in range(SUB // LANE)]))
        for k in range(parts):
            rows = slice(k * ROWS, (k + 1) * ROWS)
            left[rows, at] = masked(part, k, high)
            left[rows, also] = masked(part, k, low)

    for n in range(pairs // SUB):
        spread(heads, 0, n)
        spread(tails, chunks, n)
    table = hot[...]
    summed = both(left[:, : 2 * pairs], table, ((1,), (1,))) + both(left[:, 2 * pairs :], table, ((1,), (1,)))

    sub = iota((ROWS, share), 0)
    damped = jnp.zeros((ROWS, share), F32)
    for k in range(parts):
        one = summed[k * ROWS : (k + 1) * ROWS]
        for m in range(per_part):
            piece = k * per_part + m
            c, t = piece // n_time, piece % n_time
            here = jnp.where(clus_at == c, lam[:, t * share : (t + 1) * share], 0.0)
            states = jnp.where(sub < state, got[source(piece)], 0.0)
            extra = here * states
            damped = damped + extra * states
            send[source(piece)] = one[:, m * share : (m + 1) * share] + extra
    product = product + total(damped)
    notes = note(last[:, LANE - 1 : LANE], product, state, share)
    for d in range(devices):
        send[d, state : state + 1, :] = notes[:, :share]


def image_of(n_time, n_clus, axes, got, inertial, slot, hot, field, image, state):
    width = image.shape[1]
    share = got.shape[2]
    per_part = SUB // share
    parts = width // SUB
    flat = lax.axis_index(axes[0]) * n_clus + lax.axis_index(axes[1])
    for k in range(parts):
        pieces = []
        for m in range(per_part):
            t = k * per_part + m
            one = got[t * n_clus]
            for c in range(1, n_clus):
                one = one + got[t * n_clus + c]
            pieces.append(one)
        rows = slice(k * ROWS, (k + 1) * ROWS)
        field[rows, 0:SUB], field[rows, SUB:] = halves(join(pieces))
    prior = row_to_column(got[jnp.maximum(flat - 1, 0), state : state + 1, :], state)
    prior = jnp.where(flat == 0, 0.0, prior)
    for start in range(0, width, SUB):
        at = slice(start, start + SUB)
        table = hot[:, at]
        found = both(field[:, 0:SUB], table, ((1,), (0,))) + both(field[:, SUB:], table, ((1,), (0,)))
        part = slot[0:1, at] >> 8
        out = found[0:ROWS]
        for k in range(1, parts):
            out = jnp.where(part == k, found[k * ROWS : (k + 1) * ROWS], out)
        out = out + inertial[:, at]
        if start == 0:
            out = jnp.where(iota((ROWS, SUB), 1) == 0, out + prior, out)
        image[:, at] = out
    return jnp.sum(got[:, state : state + 1, :], axis=0)[:, state : state + 1]


def step_kernel(n_time, n_clus, axes, got, right, inertial, precond, slot, sums,
                send, scaled, residual, image, scalars, hot, field, left):
    state, width = right.shape
    hot_table(hot, slot, width)
    product = image_of(n_time, n_clus, axes, got, inertial, slot, hot, field, image, state)
    alpha = sums[0:1, state : state + 1] / product
    residual[...] = right[...] - alpha * image[0:state, :]
    dot = apply_precond(precond, residual, scaled)
    send_states(scaled, dot, slot, hot, left, send, state)
    scalars[...] = jnp.broadcast_to(alpha, scalars.shape)


def end_kernel(n_time, n_clus, axes, got, residual, inertial, slot, first, scaled, along, sums, sums_next, scalars,
               solution_field, residual_out, hot, field, image):
    state, width = residual.shape
    hot_table(hot, slot, width)
    product = image_of(n_time, n_clus, axes, got, inertial, slot, hot, field, image, state)
    alpha = scalars[0:1, 0:1]
    rz, rz_next = sums[0:1, state : state + 1], sums_next[0:1, state : state + 1]
    ratio = rz_next / rz
    step = rz_next / (product - ratio * rz_next / alpha)
    direction = scaled[0:state, :] + ratio * first[0:state, :]
    solution_field[...] = alpha * first[0:state, :] + step * direction
    residual_out[...] = residual[...] - step * (image[0:state, :] + ratio * along[0:state, :])


def on_device(
    right_side,
    transition,
    precond,
    slot_of,
    cluster_id,
    damping,
    pair_first,
    pair_second,
    pair_blocks,
):
    axes = ("tm", "clus")
    state, width = right_side.shape
    n_time = lax.axis_size("tm")
    n_clus = lax.axis_size("clus")
    devices = n_time * n_clus
    share = width // n_time
    pairs = pair_first.shape[1]
    positions = n_clus * width
    slot = slot_of.reshape(1, width)
    blocks = pair_blocks.reshape(state * state, pairs // LANE, LANE)
    params = pltpu.CompilerParams(vmem_limit_bytes=VMEM_LIMIT)

    def like(*shape):
        return jax.ShapeDtypeStruct(shape, F32)

    message = like(devices, ROWS, share)
    outgoing = like(n_time, n_clus, ROWS, share)
    row = like(1, share)
    tile = like(ROWS, width)
    hot = pltpu.VMEM((SUB, width), BF16)
    left = pltpu.VMEM((ROWS * width // SUB, 2 * width), BF16)
    field = pltpu.VMEM((ROWS * width // SUB, 2 * SUB), BF16)

    def exchange(sent):
        return lax.all_to_all(sent.reshape(devices, ROWS, share), axes, split_axis=0, concat_axis=0, tiled=True)

    def held(*arrays):
        return tuple(pltpu.with_memory_space_constraint(array, pltpu.HBM) for array in arrays)

    in_hbm = pl.BlockSpec(memory_space=pltpu.HBM)
    hot_pairs = jax.ShapeDtypeStruct((SUB, 2 * pairs), BF16)
    ends = jax.ShapeDtypeStruct((1, pairs), jnp.int32)
    tables = pl.pallas_call(
        tables_kernel,
        out_shape=(hot_pairs, ends, ends, like(*blocks.shape), like(1, width)),
        in_specs=[in_hbm] * 5,
        scratch_shapes=[
            pltpu.VMEM(damping.shape, F32),
            pltpu.VMEM(cluster_id.shape, jnp.int32),
            pltpu.SemaphoreType.DMA((5,)),
        ],
        compiler_params=params,
        name="tables",
    )(*held(pair_first, pair_second, blocks, damping, cluster_id))
    hot_of, heads, tails, blocks_of, lam = tables

    def grouped(sent, scaled):
        errors, partial, ending = pl.pallas_call(
            inertial_kernel,
            out_shape=(tile, tile, like(state, state, LANE)),
            in_specs=[pl.BlockSpec(memory_space=pltpu.VMEM), in_hbm],
            scratch_shapes=[pltpu.VMEM(transition.shape, F32), pltpu.SemaphoreType.DMA((1,))],
            compiler_params=params,
            name="inertial",
        )(scaled, *held(transition))
        return pl.pallas_call(
            functools.partial(group_kernel, n_time, n_clus, axes),
            out_shape=(message, tile, row),
            scratch_shapes=[
                pltpu.VMEM((ROWS * positions // SUB, 2 * SUB), BF16),
                pltpu.VMEM((2 * pairs // LANE * ROWS, LANE), F32),
                pltpu.VMEM((2 * pairs // LANE * ROWS, LANE), F32),
                pltpu.VMEM((ROWS * positions // SUB, 4 * pairs), BF16),
                pltpu.VMEM((ROWS, LANE), F32),
            ],
            compiler_params=params,
            name="group",
        )(exchange(sent), heads, tails, blocks_of, hot_of, lam, errors, partial, ending)

    sent, first = pl.pallas_call(
        begin_kernel,
        out_shape=(outgoing, tile),
        in_specs=[in_hbm] * 3,
        scratch_shapes=[
            hot,
            left,
            pltpu.VMEM(right_side.shape, F32),
            pltpu.VMEM(precond.shape, F32),
            pltpu.VMEM(slot.shape, jnp.int32),
            pltpu.SemaphoreType.DMA((3,)),
        ],
        compiler_params=params,
        name="begin",
    )(*held(right_side, precond, slot))
    back, inertial, sums = grouped(sent, first)
    sent, scaled, residual, along, scalars = pl.pallas_call(
        functools.partial(step_kernel, n_time, n_clus, axes),
        out_shape=(outgoing, tile, like(state, width), tile, like(1, LANE)),
        scratch_shapes=[hot, field, left],
        compiler_params=params,
        name="step",
    )(exchange(back), right_side, inertial, precond, slot, sums)
    back, inertial, sums_next = grouped(sent, scaled)
    return pl.pallas_call(
        functools.partial(end_kernel, n_time, n_clus, axes),
        out_shape=(like(state, width), like(state, width)),
        scratch_shapes=[hot, field, pltpu.VMEM((ROWS, width), F32)],
        compiler_params=params,
        name="end",
    )(exchange(back), residual, inertial, slot, first, scaled, along, sums, sums_next, scalars)


def solution(mesh):
    placed = (
        P(None, ("tm", "clus")),
        P(None, None, ("tm", "clus")),
        P(None, None, ("tm", "clus")),
        P(("tm", "clus")),
        P("tm", "clus"),
        P("tm", None),
        P("tm", "clus"),
        P("tm", "clus"),
        P(None, None, "tm", "clus"),
    )
    return jax.shard_map(
        on_device,
        mesh=mesh,
        in_specs=placed,
        out_specs=(P(None, ("tm", "clus")), P(None, ("tm", "clus"))),
        check_vma=False,
    )
```

```python
import functools
import jax
import jax.numpy as jnp
from jax import lax
from jax.experimental import pallas as pl
from jax.experimental.pallas import tpu as pltpu
from jax.sharding import PartitionSpec as P

F32 = jnp.float32
BF16 = jnp.bfloat16
ROWS = 16
SUB = 256
LANE = 128
VMEM_LIMIT = 16 * 1024 * 1024


def iota(shape, axis):
    return lax.broadcasted_iota(jnp.int32, shape, axis)


def halves(value):
    high = value.astype(BF16)
    return high, (value - high.astype(F32)).astype(BF16)


def join(pieces):
    return pieces[0] if len(pieces) == 1 else jnp.concatenate(pieces, axis=1)


def spread_row(row, count):
    return jnp.broadcast_to(row.astype(F32), (count, row.shape[1])).astype(BF16)


def hot_tile(index):
    rows = iota((SUB, index.shape[1]), 0).astype(F32).astype(BF16)
    low = spread_row(index & (SUB - 1), SUB)
    return jnp.where(rows == low, jnp.ones((), BF16), jnp.zeros((), BF16))


def hot_table(hot, index_ref, width):
    for start in range(0, width, SUB):
        hot[:, start : start + SUB] = hot_tile(index_ref[0:1, start : start + SUB])


def masked(part, k, value):
    return jnp.where(part == jnp.asarray(k, BF16), value, jnp.zeros((), BF16))


def both(left, right, contract):
    return lax.dot_general(left, right, (contract, ((), ())), preferred_element_type=F32)


def column_to_row(column, state, share):
    spot = iota((ROWS, LANE), 1) % share
    row = iota((ROWS, LANE), 0)
    return jnp.sum(jnp.where((spot == row) & (row < state), column, 0.0), axis=0, keepdims=True)


def row_to_column(row, state):
    width = row.shape[1]
    sub = iota((ROWS, width), 0)
    keep = (sub == iota((ROWS, width), 1)) & (sub < state)
    return jnp.sum(jnp.where(keep, row, 0.0), axis=1, keepdims=True)


def note(column, scalar, state, share):
    spot = iota((1, LANE), 1) % share
    return jnp.where(spot == state, scalar, column_to_row(column, state, share))


def total(value):
    return jnp.sum(jnp.sum(value, axis=0, keepdims=True), axis=1, keepdims=True)


def apply_precond(precond, residual, scaled):
    state, width = residual.shape
    dot = jnp.zeros((state, LANE), F32)
    for start in range(0, width, LANE):
        at = slice(start, start + LANE)
        out = precond[0, :, at] * residual[0:1, at]
        for j in range(1, state):
            out = out + precond[j, :, at] * residual[j : j + 1, at]
        scaled[0:state, at] = out
        scaled[state:ROWS, at] = jnp.zeros((ROWS - state, LANE), F32)
        dot = dot + out * residual[:, at]
    return total(dot)


def send_states(scaled, dot, slot, hot, left, send, state):
    width = scaled.shape[1]
    groups, copies, _, share = send.shape
    parts = width // SUB
    for start in range(0, width, SUB):
        at = slice(start, start + SUB)
        also = slice(width + start, width + start + SUB)
        high, low = halves(scaled[:, at])
        part = spread_row(slot[0:1, at] >> 8, ROWS)
        for k in range(parts):
            rows = slice(k * ROWS, (k + 1) * ROWS)
            left[rows, at] = masked(part, k, high)
            left[rows, also] = masked(part, k, low)
    table = hot[...]
    moved = both(left[:, :width], table, ((1,), (1,))) + both(left[:, width:], table, ((1,), (1,)))
    notes = note(scaled[:, 0:1], dot, state, share)
    sub = iota((ROWS, share), 0)
    for k in range(parts):
        piece = moved[k * ROWS : (k + 1) * ROWS]
        for m in range(SUB // share):
            one = jnp.where(sub == state, notes[:, :share], piece[:, m * share : (m + 1) * share])
            for copy in range(copies):
                send[k * (SUB // share) + m, copy] = one


def begin_kernel(right_in, precond_in, slot_in, send, scaled, hot, left, right, precond, slot, sems):
    state = right.shape[0]
    copies = fetch(sems, (precond_in, precond), (right_in, right), (slot_in, slot))
    copies[2].wait()
    hot_table(hot, slot, right.shape[1])
    copies[1].wait()
    copies[0].wait()
    dot = apply_precond(precond, right, scaled)
    send_states(scaled, dot, slot, hot, left, send, state)


def fetch(sems, *pairs):
    copies = [pltpu.make_async_copy(source, place, sems.at[i]) for i, (source, place) in enumerate(pairs)]
    for copy in copies:
        copy.start()
    return copies


def back_product(transition, errors, at):
    back = transition[0, :, at] * errors[0:1, at]
    for j in range(1, transition.shape[0]):
        back = back + transition[j, :, at] * errors[j : j + 1, at]
    return back


def group_kernel(n_time, n_clus, axes, staged, got, scaled, *refs):
    inputs, (send, inertial, sums), refs = refs[:8], refs[8:11], refs[11:]
    field, hot, values, left, errors = refs[:5]
    if staged:
        places, sems = refs[5:13], refs[13]
        copies = fetch(sems, *zip(inputs, places))
        inputs = places

    def arrived(*which):
        if staged:
            for i in which:
                copies[i].wait()

    heads, tails, heads_tile, tails_tile, cluster, damping, blocks, transition = inputs
    state = transition.shape[0]
    width = scaled.shape[1]
    share = got.shape[2]
    pairs = heads.shape[1]
    parts = n_clus * width // SUB
    rows_of = n_clus * width // LANE
    per_part = SUB // share
    chunks = pairs // LANE
    time_at, clus_at = lax.axis_index(axes[0]), lax.axis_index(axes[1])
    flat = time_at * n_clus + clus_at
    devices = n_time * n_clus

    def source(piece):
        return (piece % n_time) * n_clus + piece // n_time

    sums[...] = jnp.sum(got[:, state : state + 1, :], axis=0)

    for r in range(rows_of):
        field[r] = join([got[source(r * (LANE // share) + m)] for m in range(LANE // share)])

    def pull(ends, h):
        index = ends[h : h + 8, :]
        low, part = index & (LANE - 1), index >> 7
        out = [None] * state
        for r in range(rows_of):
            here = part == r
            for c in range(state):
                from_row = jnp.broadcast_to(field[r, c : c + 1, :], (8, LANE))
                found = jnp.take_along_axis(from_row, low, axis=1)
                out[c] = found if r == 0 else jnp.where(here, found, out[c])
        return out

    arrived(0, 1, 2, 3)
    squares = jnp.zeros((8, LANE), F32)
    for h in range(0, chunks, 8):
        far = pull(tails_tile, h)
        near = pull(heads_tile, h)
        if h == 0:
            arrived(6)
        back = [None] * state
        for i in range(state):
            row = [blocks[i * state + j, h : h + 8, :] for j in range(state)]
            f = near[i]
            for j in range(state):
                f = f - row[j] * far[j]
            squares = squares + f * f
            values[pl.ds(h * ROWS + i, 8, stride=ROWS), :] = f
            for j in range(state):
                back[j] = row[j] * f if i == 0 else back[j] + row[j] * f
        for j in range(state):
            values[pl.ds((chunks + h) * ROWS + j, 8, stride=ROWS), :] = -back[j]
        for j in range(state, ROWS):
            values[pl.ds(h * ROWS + j, 8, stride=ROWS), :] = jnp.zeros((8, LANE), F32)
            values[pl.ds((chunks + h) * ROWS + j, 8, stride=ROWS), :] = jnp.zeros((8, LANE), F32)

    def spread(ends, base, n):
        at = slice(base * LANE + n * SUB, base * LANE + (n + 1) * SUB)
        index = ends[0:1, n * SUB : (n + 1) * SUB]
        hot[:, at] = hot_tile(index)
        part = spread_row(index >> 8, ROWS)
        row = (base + n * (SUB // LANE)) * ROWS
        high, low = halves(join([values[row + m * ROWS : row + (m + 1) * ROWS, :] for m in range(SUB // LANE)]))
        for k in range(parts):
            left[k * 2 * ROWS : k * 2 * ROWS + ROWS, at] = masked(part, k, high)
            left[k * 2 * ROWS + ROWS : (k + 1) * 2 * ROWS, at] = masked(part, k, low)

    for n in range(pairs // SUB):
        spread(heads, 0, n)
        spread(tails, chunks, n)
    summed = both(left[...], hot[...], ((1,), (1,)))

    arrived(7)
    following = row_to_column(got[jnp.minimum(flat + 1, devices - 1), state : state + 1, :], state)
    lane = iota((ROWS, width), 1)
    errors[...] = jnp.where(lane == width - 1, following, pltpu.roll(scaled[...], width - 1, 1))
    for i in range(state):
        moved = jnp.sum(transition[i] * scaled[0:state, :], axis=0, keepdims=True)
        errors[i : i + 1, :] = errors[i : i + 1, :] - moved
    closed = (lane == width - 1) & (flat == devices - 1)
    error = jnp.where(closed | (iota((ROWS, width), 0) >= state), 0.0, errors[...])
    errors[...] = error
    prior = jnp.where(lane == 0, 0.0, pltpu.roll(error, 1, 1))
    inertial[state:ROWS, :] = jnp.zeros((ROWS - state, width), F32)
    energy = jnp.zeros((ROWS, LANE), F32)
    for start in range(0, width, LANE):
        at = slice(start, start + LANE)
        inertial[0:state, at] = prior[0:state, at] - back_product(transition, errors, at)
        energy = energy + error[:, at] * error[:, at]
    product = total(squares) + total(energy)

    arrived(4, 5)
    lam = jnp.zeros((1, width), F32)
    for label in range(damping.shape[1]):
        lam = jnp.where(cluster[...] == label, damping[0:1, label : label + 1], lam)

    sub = iota((ROWS, share), 0)
    damped = jnp.zeros((ROWS, share), F32)
    for k in range(parts):
        one = summed[k * 2 * ROWS : k * 2 * ROWS + ROWS] + summed[k * 2 * ROWS + ROWS : (k + 1) * 2 * ROWS]
        for m in range(per_part):
            piece = k * per_part + m
            c, t = piece // n_time, piece % n_time
            here = jnp.where(clus_at == c, lam[:, t * share : (t + 1) * share], 0.0)
            states = jnp.where(sub < state, got[source(piece)], 0.0)
            extra = here * states
            damped = damped + extra * states
            send[source(piece)] = one[:, m * share : (m + 1) * share] + extra
    product = product + total(damped)
    notes = note(error[:, width - 1 : width], product, state, share)
    for d in range(devices):
        send[d, state : state + 1, :] = notes[:, :share]


def image_of(n_time, n_clus, axes, got, inertial, slot, hot, field, image, state):
    width = image.shape[1]
    share = got.shape[2]
    per_part = SUB // share
    parts = width // SUB
    flat = lax.axis_index(axes[0]) * n_clus + lax.axis_index(axes[1])
    for k in range(parts):
        pieces = []
        for m in range(per_part):
            t = k * per_part + m
            one = got[t * n_clus]
            for c in range(1, n_clus):
                one = one + got[t * n_clus + c]
            pieces.append(one)
        rows = slice(k * ROWS, (k + 1) * ROWS)
        field[rows, 0:SUB], field[rows, SUB:] = halves(join(pieces))
    prior = row_to_column(got[jnp.maximum(flat - 1, 0), state : state + 1, :], state)
    prior = jnp.where(flat == 0, 0.0, prior)
    for start in range(0, width, SUB):
        at = slice(start, start + SUB)
        table = hot[:, at]
        found = both(field[:, 0:SUB], table, ((1,), (0,))) + both(field[:, SUB:], table, ((1,), (0,)))
        part = slot[0:1, at] >> 8
        out = found[0:ROWS]
        for k in range(1, parts):
            out = jnp.where(part == k, found[k * ROWS : (k + 1) * ROWS], out)
        out = out + inertial[:, at]
        if start == 0:
            out = jnp.where(iota((ROWS, SUB), 1) == 0, out + prior, out)
        image[:, at] = out
    return jnp.sum(got[:, state : state + 1, :], axis=0)[:, state : state + 1]


def step_kernel(n_time, n_clus, axes, got, right, inertial, precond, slot, sums,
                send, scaled, residual, image, scalars, hot, field, left):
    state, width = right.shape
    hot_table(hot, slot, width)
    product = image_of(n_time, n_clus, axes, got, inertial, slot, hot, field, image, state)
    alpha = sums[0:1, state : state + 1] / product
    residual[...] = right[...] - alpha * image[0:state, :]
    dot = apply_precond(precond, residual, scaled)
    send_states(scaled, dot, slot, hot, left, send, state)
    scalars[...] = jnp.broadcast_to(alpha, scalars.shape)


def end_kernel(n_time, n_clus, axes, got, residual, inertial, slot, first, scaled, along, sums, sums_next, scalars,
               solution_field, residual_out, hot, field, image):
    state, width = residual.shape
    hot_table(hot, slot, width)
    product = image_of(n_time, n_clus, axes, got, inertial, slot, hot, field, image, state)
    alpha = scalars[0:1, 0:1]
    rz, rz_next = sums[0:1, state : state + 1], sums_next[0:1, state : state + 1]
    ratio = rz_next / rz
    step = rz_next / (product - ratio * rz_next / alpha)
    direction = scaled[0:state, :] + ratio * first[0:state, :]
    solution_field[...] = alpha * first[0:state, :] + step * direction
    residual_out[...] = residual[...] - step * (image[0:state, :] + ratio * along[0:state, :])


def on_device(
    right_side,
    transition,
    precond,
    slot_of,
    cluster_id,
    damping,
    pair_first,
    pair_second,
    pair_blocks,
):
    axes = ("tm", "clus")
    state, width = right_side.shape
    n_time = lax.axis_size("tm")
    n_clus = lax.axis_size("clus")
    devices = n_time * n_clus
    share = width // n_time
    pairs = pair_first.shape[1]
    positions = n_clus * width
    slot = slot_of.reshape(1, width)
    blocks = pair_blocks.reshape(state * state, pairs // LANE, LANE)
    params = pltpu.CompilerParams(vmem_limit_bytes=VMEM_LIMIT)

    def like(*shape):
        return jax.ShapeDtypeStruct(shape, F32)

    message = like(devices, ROWS, share)
    outgoing = like(n_time, n_clus, ROWS, share)
    row = like(1, share)
    tile = like(ROWS, width)
    hot = pltpu.VMEM((SUB, width), BF16)
    left = pltpu.VMEM((ROWS * width // SUB, 2 * width), BF16)
    field = pltpu.VMEM((ROWS * width // SUB, 2 * SUB), BF16)

    def exchange(sent):
        return lax.all_to_all(sent.reshape(devices, ROWS, share), axes, split_axis=0, concat_axis=0, tiled=True)

    def held(*arrays):
        return tuple(pltpu.with_memory_space_constraint(array, pltpu.HBM) for array in arrays)

    in_hbm = pl.BlockSpec(memory_space=pltpu.HBM)
    dense = (pairs // LANE, LANE)
    own = (pair_first, pair_second, pair_first.reshape(dense), pair_second.reshape(dense),
           cluster_id, damping, blocks, transition)

    def grouped(got, scaled, staged):
        in_vmem = pl.BlockSpec(memory_space=pltpu.VMEM)
        scratch = [
            pltpu.VMEM((positions // LANE, ROWS, LANE), F32),
            pltpu.VMEM((SUB, 2 * pairs), BF16),
            pltpu.VMEM((2 * pairs // LANE * ROWS, LANE), F32),
            pltpu.VMEM((2 * ROWS * positions // SUB, 2 * pairs), BF16),
            pltpu.VMEM((ROWS, width), F32),
        ]
        if staged:
            scratch += [pltpu.VMEM(array.shape, array.dtype) for array in own]
            scratch += [pltpu.SemaphoreType.DMA((len(own),))]
        return pl.pallas_call(
            functools.partial(group_kernel, n_time, n_clus, axes, staged),
            out_shape=(message, tile, row),
            in_specs=[in_vmem] * 2 + [in_hbm if staged else in_vmem] * len(own),
            scratch_shapes=scratch,
            compiler_params=params,
            name="group",
        )(got, scaled, *(held(*own) if staged else own))

    sent, first = pl.pallas_call(
        begin_kernel,
        out_shape=(outgoing, tile),
        in_specs=[in_hbm] * 3,
        scratch_shapes=[
            hot,
            left,
            pltpu.VMEM(right_side.shape, F32),
            pltpu.VMEM(precond.shape, F32),
            pltpu.VMEM(slot.shape, jnp.int32),
            pltpu.SemaphoreType.DMA((3,)),
        ],
        compiler_params=params,
        name="begin",
    )(*held(right_side, precond, slot))
    back, inertial, sums = grouped(exchange(sent), first, True)
    sent, scaled, residual, along, scalars = pl.pallas_call(
        functools.partial(step_kernel, n_time, n_clus, axes),
        out_shape=(outgoing, tile, like(state, width), tile, like(1, LANE)),
        scratch_shapes=[hot, field, left],
        compiler_params=params,
        name="step",
    )(exchange(back), right_side, inertial, precond, slot, sums)
    back, inertial, sums_next = grouped(exchange(sent), scaled, False)
    return pl.pallas_call(
        functools.partial(end_kernel, n_time, n_clus, axes),
        out_shape=(like(state, width), like(state, width)),
        scratch_shapes=[hot, field, pltpu.VMEM((ROWS, width), F32)],
        compiler_params=params,
        name="end",
    )(exchange(back), residual, inertial, slot, first, scaled, along, sums, sums_next, scalars)


def solution(mesh):
    placed = (
        P(None, ("tm", "clus")),
        P(None, None, ("tm", "clus")),
        P(None, None, ("tm", "clus")),
        P(("tm", "clus")),
        P("tm", "clus"),
        P("tm", None),
        P("tm", "clus"),
        P("tm", "clus"),
        P(None, None, "tm", "clus"),
    )
    return jax.shard_map(
        on_device,
        mesh=mesh,
        in_specs=placed,
        out_specs=(P(None, ("tm", "clus")), P(None, ("tm", "clus"))),
        check_vma=False,
    )
```

```python
import functools
import jax
import jax.numpy as jnp
from jax import lax
from jax.experimental import pallas as pl
from jax.experimental.pallas import tpu as pltpu
from jax.sharding import PartitionSpec as P

F32 = jnp.float32
BF16 = jnp.bfloat16
ROWS = 16
SUB = 256
LANE = 128
VMEM_LIMIT = 16 * 1024 * 1024


def iota(shape, axis):
    return lax.broadcasted_iota(jnp.int32, shape, axis)


def halves(value):
    high = value.astype(BF16)
    return high, (value - high.astype(F32)).astype(BF16)


def join(pieces):
    return pieces[0] if len(pieces) == 1 else jnp.concatenate(pieces, axis=1)


def spread_row(row, count):
    return jnp.broadcast_to(row.astype(F32), (count, row.shape[1])).astype(BF16)


def hot_tile(index):
    rows = iota((SUB, index.shape[1]), 0).astype(F32).astype(BF16)
    low = spread_row(index & (SUB - 1), SUB)
    return jnp.where(rows == low, jnp.ones((), BF16), jnp.zeros((), BF16))


def hot_table(hot, index_ref, width):
    for start in range(0, width, SUB):
        hot[:, start : start + SUB] = hot_tile(index_ref[0:1, start : start + SUB])


def masked(part, k, value):
    return jnp.where(part == jnp.asarray(k, BF16), value, jnp.zeros((), BF16))


def both(left, right, contract):
    return lax.dot_general(left, right, (contract, ((), ())), preferred_element_type=F32)


def column_to_row(column, state, share):
    spot = iota((ROWS, LANE), 1) % share
    row = iota((ROWS, LANE), 0)
    return jnp.sum(jnp.where((spot == row) & (row < state), column, 0.0), axis=0, keepdims=True)


def row_to_column(row, state):
    width = row.shape[1]
    sub = iota((ROWS, width), 0)
    keep = (sub == iota((ROWS, width), 1)) & (sub < state)
    return jnp.sum(jnp.where(keep, row, 0.0), axis=1, keepdims=True)


def note(column, scalar, state, share):
    spot = iota((1, LANE), 1) % share
    return jnp.where(spot == state, scalar, column_to_row(column, state, share))


def total(value):
    return jnp.sum(jnp.sum(value, axis=0, keepdims=True), axis=1, keepdims=True)


def apply_precond(precond, residual, scaled):
    state, width = residual.shape
    dot = jnp.zeros((state, LANE), F32)
    for start in range(0, width, LANE):
        at = slice(start, start + LANE)
        out = precond[0, :, at] * residual[0:1, at]
        for j in range(1, state):
            out = out + precond[j, :, at] * residual[j : j + 1, at]
        scaled[0:state, at] = out
        scaled[state:ROWS, at] = jnp.zeros((ROWS - state, LANE), F32)
        dot = dot + out * residual[:, at]
    return total(dot)


def send_states(scaled, dot, slot, hot, left, send, state):
    width = scaled.shape[1]
    groups, copies, _, share = send.shape
    parts = width // SUB
    for start in range(0, width, SUB):
        at = slice(start, start + SUB)
        also = slice(width + start, width + start + SUB)
        high, low = halves(scaled[:, at])
        part = spread_row(slot[0:1, at] >> 8, ROWS)
        for k in range(parts):
            rows = slice(k * ROWS, (k + 1) * ROWS)
            left[rows, at] = masked(part, k, high)
            left[rows, also] = masked(part, k, low)
    table = hot[...]
    moved = both(left[:, :width], table, ((1,), (1,))) + both(left[:, width:], table, ((1,), (1,)))
    notes = note(scaled[:, 0:1], dot, state, share)
    sub = iota((ROWS, share), 0)
    for k in range(parts):
        piece = moved[k * ROWS : (k + 1) * ROWS]
        for m in range(SUB // share):
            one = jnp.where(sub == state, notes[:, :share], piece[:, m * share : (m + 1) * share])
            for copy in range(copies):
                send[k * (SUB // share) + m, copy] = one


def begin_kernel(right_in, precond_in, slot_in, *refs):
    carried = len(refs) // 2 - 4
    (send, scaled), (hot, left, right, precond, slot, sems) = refs[carried : carried + 2], refs[2 * carried + 2 :]
    state = right.shape[0]
    copies = fetch(sems, (precond_in, precond), (right_in, right), (slot_in, slot),
                   *zip(refs[:carried], refs[carried + 2 : 2 * carried + 2]))
    copies[2].wait()
    hot_table(hot, slot, right.shape[1])
    copies[1].wait()
    copies[0].wait()
    dot = apply_precond(precond, right, scaled)
    send_states(scaled, dot, slot, hot, left, send, state)
    for copy in copies[3:]:
        copy.wait()


def fetch(sems, *pairs):
    copies = [pltpu.make_async_copy(source, place, sems.at[i]) for i, (source, place) in enumerate(pairs)]
    for copy in copies:
        copy.start()
    return copies


def back_product(transition, errors, at):
    back = transition[0, :, at] * errors[0:1, at]
    for j in range(1, transition.shape[0]):
        back = back + transition[j, :, at] * errors[j : j + 1, at]
    return back


def group_kernel(n_time, n_clus, axes, staged, got, scaled, *refs):
    inputs, (send, inertial, sums), refs = refs[:8], refs[8:11], refs[11:]
    field, hot, values, left, errors = refs[:5]
    if staged:
        places, sems = refs[5:7], refs[7]
        copies = fetch(sems, *zip(inputs[6:], places))
        inputs = inputs[:6] + places

    def arrived(which):
        if staged:
            copies[which].wait()

    heads, tails, heads_tile, tails_tile, cluster, damping, blocks, transition = inputs
    state = transition.shape[0]
    width = scaled.shape[1]
    share = got.shape[2]
    pairs = heads.shape[1]
    parts = n_clus * width // SUB
    rows_of = n_clus * width // LANE
    per_part = SUB // share
    chunks = pairs // LANE
    time_at, clus_at = lax.axis_index(axes[0]), lax.axis_index(axes[1])
    flat = time_at * n_clus + clus_at
    devices = n_time * n_clus

    def source(piece):
        return (piece % n_time) * n_clus + piece // n_time

    sums[...] = jnp.sum(got[:, state : state + 1, :], axis=0)

    for r in range(rows_of):
        field[r] = join([got[source(r * (LANE // share) + m)] for m in range(LANE // share)])

    def pull(ends, h):
        index = ends[h : h + 8, :]
        low, part = index & (LANE - 1), index >> 7
        out = [None] * state
        for r in range(rows_of):
            here = part == r
            for c in range(state):
                from_row = jnp.broadcast_to(field[r, c : c + 1, :], (8, LANE))
                found = jnp.take_along_axis(from_row, low, axis=1)
                out[c] = found if r == 0 else jnp.where(here, found, out[c])
        return out

    def spread(ends, base, n):
        at = slice(base * LANE + n * SUB, base * LANE + (n + 1) * SUB)
        index = ends[0:1, n * SUB : (n + 1) * SUB]
        hot[:, at] = hot_tile(index)
        part = spread_row(index >> 8, ROWS)
        row = (base + n * (SUB // LANE)) * ROWS
        high, low = halves(join([values[row + m * ROWS : row + (m + 1) * ROWS, :] for m in range(SUB // LANE)]))
        for k in range(parts):
            left[k * 2 * ROWS : k * 2 * ROWS + ROWS, at] = masked(part, k, high)
            left[k * 2 * ROWS + ROWS : (k + 1) * 2 * ROWS, at] = masked(part, k, low)

    squares = jnp.zeros((8, LANE), F32)
    summed = []
    for h in range(0, chunks, 8):
        far = pull(tails_tile, h)
        near = pull(heads_tile, h)
        if h == 0:
            arrived(0)
        back = [None] * state
        for i in range(state):
            row = [blocks[i * state + j, h : h + 8, :] for j in range(state)]
            f = near[i]
            for j in range(state):
                f = f - row[j] * far[j]
            squares = squares + f * f
            values[pl.ds(h * ROWS + i, 8, stride=ROWS), :] = f
            for j in range(state):
                back[j] = row[j] * f if i == 0 else back[j] + row[j] * f
        for j in range(state):
            values[pl.ds((chunks + h) * ROWS + j, 8, stride=ROWS), :] = -back[j]
        for j in range(state, ROWS):
            values[pl.ds(h * ROWS + j, 8, stride=ROWS), :] = jnp.zeros((8, LANE), F32)
            values[pl.ds((chunks + h) * ROWS + j, 8, stride=ROWS), :] = jnp.zeros((8, LANE), F32)
        first, final = h * LANE // SUB, (h + 8) * LANE // SUB
        for base, ends in ((0, heads), (chunks, tails)):
            for n in range(first, final):
                spread(ends, base, n)
            at = slice(base * LANE + first * SUB, base * LANE + final * SUB)
            summed.append(both(left[:, at], hot[:, at], ((1,), (1,))))
    summed = functools.reduce(lambda one, other: one + other, summed)

    arrived(1)
    following = row_to_column(got[jnp.minimum(flat + 1, devices - 1), state : state + 1, :], state)
    lane = iota((ROWS, width), 1)
    errors[...] = jnp.where(lane == width - 1, following, pltpu.roll(scaled[...], width - 1, 1))
    for i in range(state):
        moved = jnp.sum(transition[i] * scaled[0:state, :], axis=0, keepdims=True)
        errors[i : i + 1, :] = errors[i : i + 1, :] - moved
    closed = (lane == width - 1) & (flat == devices - 1)
    error = jnp.where(closed | (iota((ROWS, width), 0) >= state), 0.0, errors[...])
    errors[...] = error
    prior = jnp.where(lane == 0, 0.0, pltpu.roll(error, 1, 1))
    inertial[state:ROWS, :] = jnp.zeros((ROWS - state, width), F32)
    energy = jnp.zeros((ROWS, LANE), F32)
    for start in range(0, width, LANE):
        at = slice(start, start + LANE)
        inertial[0:state, at] = prior[0:state, at] - back_product(transition, errors, at)
        energy = energy + error[:, at] * error[:, at]
    product = total(squares) + total(energy)

    lam = jnp.zeros((1, width), F32)
    for label in range(damping.shape[1]):
        lam = jnp.where(cluster[...] == label, damping[0:1, label : label + 1], lam)

    sub = iota((ROWS, share), 0)
    damped = jnp.zeros((ROWS, share), F32)
    for k in range(parts):
        one = summed[k * 2 * ROWS : k * 2 * ROWS + ROWS] + summed[k * 2 * ROWS + ROWS : (k + 1) * 2 * ROWS]
        for m in range(per_part):
            piece = k * per_part + m
            c, t = piece // n_time, piece % n_time
            here = jnp.where(clus_at == c, lam[:, t * share : (t + 1) * share], 0.0)
            states = jnp.where(sub < state, got[source(piece)], 0.0)
            extra = here * states
            damped = damped + extra * states
            send[source(piece)] = one[:, m * share : (m + 1) * share] + extra
    product = product + total(damped)
    notes = note(error[:, width - 1 : width], product, state, share)
    for d in range(devices):
        send[d, state : state + 1, :] = notes[:, :share]


def image_of(n_time, n_clus, axes, got, inertial, slot, hot, field, image, state):
    width = image.shape[1]
    share = got.shape[2]
    per_part = SUB // share
    parts = width // SUB
    flat = lax.axis_index(axes[0]) * n_clus + lax.axis_index(axes[1])
    for k in range(parts):
        pieces = []
        for m in range(per_part):
            t = k * per_part + m
            one = got[t * n_clus]
            for c in range(1, n_clus):
                one = one + got[t * n_clus + c]
            pieces.append(one)
        rows = slice(k * ROWS, (k + 1) * ROWS)
        field[rows, 0:SUB], field[rows, SUB:] = halves(join(pieces))
    prior = row_to_column(got[jnp.maximum(flat - 1, 0), state : state + 1, :], state)
    prior = jnp.where(flat == 0, 0.0, prior)
    for start in range(0, width, SUB):
        at = slice(start, start + SUB)
        table = hot[:, at]
        found = both(field[:, 0:SUB], table, ((1,), (0,))) + both(field[:, SUB:], table, ((1,), (0,)))
        part = slot[0:1, at] >> 8
        out = found[0:ROWS]
        for k in range(1, parts):
            out = jnp.where(part == k, found[k * ROWS : (k + 1) * ROWS], out)
        out = out + inertial[:, at]
        if start == 0:
            out = jnp.where(iota((ROWS, SUB), 1) == 0, out + prior, out)
        image[:, at] = out
    return jnp.sum(got[:, state : state + 1, :], axis=0)[:, state : state + 1]


def step_kernel(n_time, n_clus, axes, got, right, inertial, precond, slot, sums,
                send, scaled, residual, image, scalars, hot, field, left):
    state, width = right.shape
    hot_table(hot, slot, width)
    product = image_of(n_time, n_clus, axes, got, inertial, slot, hot, field, image, state)
    alpha = sums[0:1, state : state + 1] / product
    residual[...] = right[...] - alpha * image[0:state, :]
    dot = apply_precond(precond, residual, scaled)
    send_states(scaled, dot, slot, hot, left, send, state)
    scalars[...] = jnp.broadcast_to(alpha, scalars.shape)


def end_kernel(n_time, n_clus, axes, got, residual, inertial, slot, first, scaled, along, sums, sums_next, scalars,
               solution_field, residual_out, hot, field, image):
    state, width = residual.shape
    hot_table(hot, slot, width)
    product = image_of(n_time, n_clus, axes, got, inertial, slot, hot, field, image, state)
    alpha = scalars[0:1, 0:1]
    rz, rz_next = sums[0:1, state : state + 1], sums_next[0:1, state : state + 1]
    ratio = rz_next / rz
    step = rz_next / (product - ratio * rz_next / alpha)
    direction = scaled[0:state, :] + ratio * first[0:state, :]
    solution_field[...] = alpha * first[0:state, :] + step * direction
    residual_out[...] = residual[...] - step * (image[0:state, :] + ratio * along[0:state, :])


def on_device(
    right_side,
    transition,
    precond,
    slot_of,
    cluster_id,
    damping,
    pair_first,
    pair_second,
    pair_blocks,
):
    axes = ("tm", "clus")
    state, width = right_side.shape
    n_time = lax.axis_size("tm")
    n_clus = lax.axis_size("clus")
    devices = n_time * n_clus
    share = width // n_time
    pairs = pair_first.shape[1]
    positions = n_clus * width
    slot = slot_of.reshape(1, width)
    blocks = pair_blocks.reshape(state * state, pairs // LANE, LANE)
    params = pltpu.CompilerParams(vmem_limit_bytes=VMEM_LIMIT)

    def like(*shape):
        return jax.ShapeDtypeStruct(shape, F32)

    message = like(devices, ROWS, share)
    outgoing = like(n_time, n_clus, ROWS, share)
    row = like(1, share)
    tile = like(ROWS, width)
    hot = pltpu.VMEM((SUB, width), BF16)
    left = pltpu.VMEM((ROWS * width // SUB, 2 * width), BF16)
    field = pltpu.VMEM((ROWS * width // SUB, 2 * SUB), BF16)

    def exchange(sent):
        return lax.all_to_all(sent.reshape(devices, ROWS, share), axes, split_axis=0, concat_axis=0, tiled=True)

    def held(*arrays):
        return tuple(pltpu.with_memory_space_constraint(array, pltpu.HBM) for array in arrays)

    in_hbm = pl.BlockSpec(memory_space=pltpu.HBM)
    dense = (pairs // LANE, LANE)
    small = (pair_first, pair_second, pair_first.reshape(dense), pair_second.reshape(dense), cluster_id, damping)
    large = (blocks, transition)

    def grouped(got, scaled, staged):
        in_vmem = pl.BlockSpec(memory_space=pltpu.VMEM)
        scratch = [
            pltpu.VMEM((positions // LANE, ROWS, LANE), F32),
            pltpu.VMEM((SUB, 2 * pairs), BF16),
            pltpu.VMEM((2 * pairs // LANE * ROWS, LANE), F32),
            pltpu.VMEM((2 * ROWS * positions // SUB, 2 * pairs), BF16),
            pltpu.VMEM((ROWS, width), F32),
        ]
        if staged:
            scratch += [pltpu.VMEM(array.shape, array.dtype) for array in large]
            scratch += [pltpu.SemaphoreType.DMA((len(large),))]
        return pl.pallas_call(
            functools.partial(group_kernel, n_time, n_clus, axes, staged),
            out_shape=(message, tile, row),
            in_specs=[in_vmem] * (2 + len(small)) + [in_hbm if staged else in_vmem] * len(large),
            scratch_shapes=scratch,
            compiler_params=params,
            name="group",
        )(got, scaled, *carried, *(held(*large) if staged else large))

    sent, first, *carried = pl.pallas_call(
        begin_kernel,
        out_shape=(outgoing, tile, *(jax.ShapeDtypeStruct(array.shape, array.dtype) for array in small)),
        in_specs=[in_hbm] * (3 + len(small)),
        scratch_shapes=[
            hot,
            left,
            pltpu.VMEM(right_side.shape, F32),
            pltpu.VMEM(precond.shape, F32),
            pltpu.VMEM(slot.shape, jnp.int32),
            pltpu.SemaphoreType.DMA((3 + len(small),)),
        ],
        compiler_params=params,
        name="begin",
    )(*held(right_side, precond, slot, *small))
    back, inertial, sums = grouped(exchange(sent), first, True)
    sent, scaled, residual, along, scalars = pl.pallas_call(
        functools.partial(step_kernel, n_time, n_clus, axes),
        out_shape=(outgoing, tile, like(state, width), tile, like(1, LANE)),
        scratch_shapes=[hot, field, left],
        compiler_params=params,
        name="step",
    )(exchange(back), right_side, inertial, precond, slot, sums)
    back, inertial, sums_next = grouped(exchange(sent), scaled, False)
    return pl.pallas_call(
        functools.partial(end_kernel, n_time, n_clus, axes),
        out_shape=(like(state, width), like(state, width)),
        scratch_shapes=[hot, field, pltpu.VMEM((ROWS, width), F32)],
        compiler_params=params,
        name="end",
    )(exchange(back), residual, inertial, slot, first, scaled, along, sums, sums_next, scalars)


def solution(mesh):
    placed = (
        P(None, ("tm", "clus")),
        P(None, None, ("tm", "clus")),
        P(None, None, ("tm", "clus")),
        P(("tm", "clus")),
        P("tm", "clus"),
        P("tm", None),
        P("tm", "clus"),
        P("tm", "clus"),
        P(None, None, "tm", "clus"),
    )
    return jax.shard_map(
        on_device,
        mesh=mesh,
        in_specs=placed,
        out_specs=(P(None, ("tm", "clus")), P(None, ("tm", "clus"))),
        check_vma=False,
    )
```

```python
import functools
import jax
import jax.numpy as jnp
from jax import lax
from jax.experimental import pallas as pl
from jax.experimental.pallas import tpu as pltpu
from jax.sharding import PartitionSpec as P

F32 = jnp.float32
BF16 = jnp.bfloat16
ROWS = 16
SUB = 256
LANE = 128
VMEM_LIMIT = 16 * 1024 * 1024


def iota(shape, axis):
    return lax.broadcasted_iota(jnp.int32, shape, axis)


def halves(value):
    high = value.astype(BF16)
    return high, (value - high.astype(F32)).astype(BF16)


def join(pieces):
    return pieces[0] if len(pieces) == 1 else jnp.concatenate(pieces, axis=1)


def spread_row(row, count):
    return jnp.broadcast_to(row.astype(F32), (count, row.shape[1])).astype(BF16)


def hot_tile(index):
    rows = iota((SUB, index.shape[1]), 0).astype(F32).astype(BF16)
    low = spread_row(index & (SUB - 1), SUB)
    return jnp.where(rows == low, jnp.ones((), BF16), jnp.zeros((), BF16))


def hot_table(hot, index_ref, width):
    for start in range(0, width, SUB):
        hot[:, start : start + SUB] = hot_tile(index_ref[0:1, start : start + SUB])


def masked(part, k, value):
    return jnp.where(part == jnp.asarray(k, BF16), value, jnp.zeros((), BF16))


def both(left, right, contract):
    return lax.dot_general(left, right, (contract, ((), ())), preferred_element_type=F32)


def column_to_row(column, state, share):
    spot = iota((ROWS, LANE), 1) % share
    row = iota((ROWS, LANE), 0)
    return jnp.sum(jnp.where((spot == row) & (row < state), column, 0.0), axis=0, keepdims=True)


def row_to_column(row, state):
    width = row.shape[1]
    sub = iota((ROWS, width), 0)
    keep = (sub == iota((ROWS, width), 1)) & (sub < state)
    return jnp.sum(jnp.where(keep, row, 0.0), axis=1, keepdims=True)


def note(column, scalar, state, share):
    spot = iota((1, LANE), 1) % share
    return jnp.where(spot == state, scalar, column_to_row(column, state, share))


def total(value):
    return jnp.sum(jnp.sum(value, axis=0, keepdims=True), axis=1, keepdims=True)


def apply_precond(precond, residual, scaled):
    state, width = residual.shape
    dot = jnp.zeros((state, LANE), F32)
    for start in range(0, width, LANE):
        at = slice(start, start + LANE)
        out = precond[0, :, at] * residual[0:1, at]
        for j in range(1, state):
            out = out + precond[j, :, at] * residual[j : j + 1, at]
        scaled[0:state, at] = out
        scaled[state:ROWS, at] = jnp.zeros((ROWS - state, LANE), F32)
        dot = dot + out * residual[:, at]
    return total(dot)


def send_states(scaled, dot, slot, hot, left, send, state):
    width = scaled.shape[1]
    share = send.shape[2]
    parts = width // SUB
    for start in range(0, width, SUB):
        at = slice(start, start + SUB)
        also = slice(width + start, width + start + SUB)
        high, low = halves(scaled[:, at])
        part = spread_row(slot[0:1, at] >> 8, ROWS)
        for k in range(parts):
            rows = slice(k * ROWS, (k + 1) * ROWS)
            left[rows, at] = masked(part, k, high)
            left[rows, also] = masked(part, k, low)
    table = hot[...]
    moved = both(left[:, :width], table, ((1,), (1,))) + both(left[:, width:], table, ((1,), (1,)))
    notes = note(scaled[:, 0:1], dot, state, share)
    sub = iota((ROWS, share), 0)
    for k in range(parts):
        piece = moved[k * ROWS : (k + 1) * ROWS]
        for m in range(SUB // share):
            one = jnp.where(sub == state, notes[:, :share], piece[:, m * share : (m + 1) * share])
            send[k * (SUB // share) + m] = one


def begin_kernel(right_in, precond_in, slot_in, *refs):
    carried = len(refs) // 2 - 4
    (send, scaled), (hot, left, right, precond, slot, sems) = refs[carried : carried + 2], refs[2 * carried + 2 :]
    state = right.shape[0]
    copies = fetch(sems, (precond_in, precond), (right_in, right), (slot_in, slot),
                   *zip(refs[:carried], refs[carried + 2 : 2 * carried + 2]))
    copies[2].wait()
    hot_table(hot, slot, right.shape[1])
    copies[1].wait()
    copies[0].wait()
    dot = apply_precond(precond, right, scaled)
    send_states(scaled, dot, slot, hot, left, send, state)
    for copy in copies[3:]:
        copy.wait()


def fetch(sems, *pairs):
    copies = [pltpu.make_async_copy(source, place, sems.at[i]) for i, (source, place) in enumerate(pairs)]
    for copy in copies:
        copy.start()
    return copies


def back_product(transition, errors, at):
    back = transition[0, :, at] * errors[0:1, at]
    for j in range(1, transition.shape[0]):
        back = back + transition[j, :, at] * errors[j : j + 1, at]
    return back


def group_kernel(n_time, n_clus, axes, staged, got, scaled, *refs):
    inputs, (send, inertial, sums), refs = refs[:8], refs[8:11], refs[11:]
    field, hot, values, left, errors = refs[:5]
    if staged:
        (copy,) = fetch(refs[6], (inputs[7], refs[5]))
        inputs = inputs[:7] + (refs[5],)
    heads, tails, heads_tile, tails_tile, cluster, damping, transition, blocks = inputs
    state = transition.shape[0]
    width = scaled.shape[1]
    share = got.shape[2]
    pairs = heads.shape[1]
    parts = n_clus * width // SUB
    rows_of = n_clus * width // LANE
    per_part = SUB // share
    chunks = pairs // LANE
    time_at, clus_at = lax.axis_index(axes[0]), lax.axis_index(axes[1])
    flat = time_at * n_clus + clus_at
    devices = n_time * n_clus

    def source(piece):
        return (piece % n_time) * n_clus + piece // n_time

    sums[...] = jnp.sum(got[:, state : state + 1, :], axis=0)

    for r in range(rows_of):
        field[r] = join([got[r * (LANE // share) + m] for m in range(LANE // share)])

    def pull(ends, h):
        index = ends[h : h + 8, :]
        low, part = index & (LANE - 1), index >> 7
        out = [None] * state
        for r in range(rows_of):
            here = part == r
            for c in range(state):
                from_row = jnp.broadcast_to(field[r, c : c + 1, :], (8, LANE))
                found = jnp.take_along_axis(from_row, low, axis=1)
                out[c] = found if r == 0 else jnp.where(here, found, out[c])
        return out

    def spread(ends, base, n):
        at = slice(base * LANE + n * SUB, base * LANE + (n + 1) * SUB)
        index = ends[0:1, n * SUB : (n + 1) * SUB]
        hot[:, at] = hot_tile(index)
        part = spread_row(index >> 8, ROWS)
        row = (base + n * (SUB // LANE)) * ROWS
        high, low = halves(join([values[row + m * ROWS : row + (m + 1) * ROWS, :] for m in range(SUB // LANE)]))
        for k in range(parts):
            left[k * 2 * ROWS : k * 2 * ROWS + ROWS, at] = masked(part, k, high)
            left[k * 2 * ROWS + ROWS : (k + 1) * 2 * ROWS, at] = masked(part, k, low)

    squares = jnp.zeros((8, LANE), F32)
    for h in range(0, chunks, 8):
        far = pull(tails_tile, h)
        near = pull(heads_tile, h)
        if staged and h == 0:
            copy.wait()
        back = [None] * state
        for i in range(state):
            row = [blocks[i * state + j, h : h + 8, :] for j in range(state)]
            f = near[i]
            for j in range(state):
                f = f - row[j] * far[j]
            squares = squares + f * f
            values[pl.ds(h * ROWS + i, 8, stride=ROWS), :] = f
            for j in range(state):
                back[j] = row[j] * f if i == 0 else back[j] + row[j] * f
        for j in range(state):
            values[pl.ds((chunks + h) * ROWS + j, 8, stride=ROWS), :] = -back[j]
        for j in range(state, ROWS):
            values[pl.ds(h * ROWS + j, 8, stride=ROWS), :] = jnp.zeros((8, LANE), F32)
            values[pl.ds((chunks + h) * ROWS + j, 8, stride=ROWS), :] = jnp.zeros((8, LANE), F32)
    for n in range(pairs // SUB):
        spread(heads, 0, n)
        spread(tails, chunks, n)
    summed = both(left[...], hot[...], ((1,), (1,)))

    after = jnp.minimum(flat + 1, devices - 1)
    following = row_to_column(got[(after % n_clus) * n_time + after // n_clus, state : state + 1, :], state)
    lane = iota((ROWS, width), 1)
    errors[...] = jnp.where(lane == width - 1, following, pltpu.roll(scaled[...], width - 1, 1))
    for i in range(state):
        moved = jnp.sum(transition[i] * scaled[0:state, :], axis=0, keepdims=True)
        errors[i : i + 1, :] = errors[i : i + 1, :] - moved
    closed = (lane == width - 1) & (flat == devices - 1)
    error = jnp.where(closed | (iota((ROWS, width), 0) >= state), 0.0, errors[...])
    errors[...] = error
    prior = jnp.where(lane == 0, 0.0, pltpu.roll(error, 1, 1))
    inertial[state:ROWS, :] = jnp.zeros((ROWS - state, width), F32)
    energy = jnp.zeros((ROWS, LANE), F32)
    for start in range(0, width, LANE):
        at = slice(start, start + LANE)
        inertial[0:state, at] = prior[0:state, at] - back_product(transition, errors, at)
        energy = energy + error[:, at] * error[:, at]
    product = total(squares) + total(energy)

    lam = jnp.zeros((1, width), F32)
    for label in range(damping.shape[1]):
        lam = jnp.where(cluster[...] == label, damping[0:1, label : label + 1], lam)

    sub = iota((ROWS, share), 0)
    damped = jnp.zeros((ROWS, share), F32)
    for k in range(parts):
        one = summed[k * 2 * ROWS : k * 2 * ROWS + ROWS] + summed[k * 2 * ROWS + ROWS : (k + 1) * 2 * ROWS]
        for m in range(per_part):
            piece = k * per_part + m
            c, t = piece // n_time, piece % n_time
            here = jnp.where(clus_at == c, lam[:, t * share : (t + 1) * share], 0.0)
            states = jnp.where(sub < state, got[piece], 0.0)
            extra = here * states
            damped = damped + extra * states
            send[source(piece)] = one[:, m * share : (m + 1) * share] + extra
    product = product + total(damped)
    notes = note(error[:, width - 1 : width], product, state, share)
    for d in range(devices):
        send[d, state : state + 1, :] = notes[:, :share]


def image_of(n_time, n_clus, axes, got, inertial, slot, hot, field, image, state):
    width = image.shape[1]
    share = got.shape[2]
    per_part = SUB // share
    parts = width // SUB
    flat = lax.axis_index(axes[0]) * n_clus + lax.axis_index(axes[1])
    for k in range(parts):
        pieces = []
        for m in range(per_part):
            t = k * per_part + m
            one = got[t * n_clus]
            for c in range(1, n_clus):
                one = one + got[t * n_clus + c]
            pieces.append(one)
        rows = slice(k * ROWS, (k + 1) * ROWS)
        field[rows, 0:SUB], field[rows, SUB:] = halves(join(pieces))
    prior = row_to_column(got[jnp.maximum(flat - 1, 0), state : state + 1, :], state)
    prior = jnp.where(flat == 0, 0.0, prior)
    for start in range(0, width, SUB):
        at = slice(start, start + SUB)
        table = hot[:, at]
        found = both(field[:, 0:SUB], table, ((1,), (0,))) + both(field[:, SUB:], table, ((1,), (0,)))
        part = slot[0:1, at] >> 8
        out = found[0:ROWS]
        for k in range(1, parts):
            out = jnp.where(part == k, found[k * ROWS : (k + 1) * ROWS], out)
        out = out + inertial[:, at]
        if start == 0:
            out = jnp.where(iota((ROWS, SUB), 1) == 0, out + prior, out)
        image[:, at] = out
    return jnp.sum(got[:, state : state + 1, :], axis=0)[:, state : state + 1]


def step_kernel(n_time, n_clus, axes, got, right, inertial, precond, slot, sums,
                send, scaled, residual, image, scalars, hot, field, left):
    state, width = right.shape
    hot_table(hot, slot, width)
    product = image_of(n_time, n_clus, axes, got, inertial, slot, hot, field, image, state)
    alpha = sums[0:1, state : state + 1] / product
    residual[...] = right[...] - alpha * image[0:state, :]
    dot = apply_precond(precond, residual, scaled)
    send_states(scaled, dot, slot, hot, left, send, state)
    scalars[...] = jnp.broadcast_to(alpha, scalars.shape)


def end_kernel(n_time, n_clus, axes, got, residual, inertial, slot, first, scaled, along, sums, sums_next, scalars,
               solution_field, residual_out, hot, field, image):
    state, width = residual.shape
    hot_table(hot, slot, width)
    product = image_of(n_time, n_clus, axes, got, inertial, slot, hot, field, image, state)
    alpha = scalars[0:1, 0:1]
    rz, rz_next = sums[0:1, state : state + 1], sums_next[0:1, state : state + 1]
    ratio = rz_next / rz
    step = rz_next / (product - ratio * rz_next / alpha)
    direction = scaled[0:state, :] + ratio * first[0:state, :]
    solution_field[...] = alpha * first[0:state, :] + step * direction
    residual_out[...] = residual[...] - step * (image[0:state, :] + ratio * along[0:state, :])


def on_device(
    right_side,
    transition,
    precond,
    slot_of,
    cluster_id,
    damping,
    pair_first,
    pair_second,
    pair_blocks,
):
    axes = ("tm", "clus")
    state, width = right_side.shape
    n_time = lax.axis_size("tm")
    n_clus = lax.axis_size("clus")
    devices = n_time * n_clus
    share = width // n_time
    pairs = pair_first.shape[1]
    positions = n_clus * width
    slot = slot_of.reshape(1, width)
    blocks = pair_blocks.reshape(state * state, pairs // LANE, LANE)
    params = pltpu.CompilerParams(vmem_limit_bytes=VMEM_LIMIT)

    def like(*shape):
        return jax.ShapeDtypeStruct(shape, F32)

    message = like(devices, ROWS, share)
    outgoing = like(n_time, ROWS, share)
    row = like(1, share)
    tile = like(ROWS, width)
    hot = pltpu.VMEM((SUB, width), BF16)
    left = pltpu.VMEM((ROWS * width // SUB, 2 * width), BF16)
    field = pltpu.VMEM((ROWS * width // SUB, 2 * SUB), BF16)

    def exchange(sent):
        return lax.all_to_all(sent.reshape(devices, ROWS, share), axes, split_axis=0, concat_axis=0, tiled=True)

    def held(*arrays):
        return tuple(pltpu.with_memory_space_constraint(array, pltpu.HBM) for array in arrays)

    in_hbm = pl.BlockSpec(memory_space=pltpu.HBM)
    dense = (pairs // LANE, LANE)
    small = (pair_first, pair_second, pair_first.reshape(dense), pair_second.reshape(dense), cluster_id, damping)

    def collect(sent):
        own = lax.all_to_all(sent, "tm", split_axis=0, concat_axis=0, tiled=True)
        return lax.all_gather(own, "clus", axis=0, tiled=True)

    def grouped(got, scaled, staged):
        in_vmem = pl.BlockSpec(memory_space=pltpu.VMEM)
        scratch = [
            pltpu.VMEM((positions // LANE, ROWS, LANE), F32),
            pltpu.VMEM((SUB, 2 * pairs), BF16),
            pltpu.VMEM((2 * pairs // LANE * ROWS, LANE), F32),
            pltpu.VMEM((2 * ROWS * positions // SUB, 2 * pairs), BF16),
            pltpu.VMEM((ROWS, width), F32),
        ]
        if staged:
            scratch += [pltpu.VMEM(blocks.shape, F32), pltpu.SemaphoreType.DMA((1,))]
        return pl.pallas_call(
            functools.partial(group_kernel, n_time, n_clus, axes, staged),
            out_shape=(message, tile, row),
            in_specs=[in_vmem] * (3 + len(small)) + [in_hbm if staged else in_vmem],
            scratch_shapes=scratch,
            compiler_params=params,
            name="group",
        )(got, scaled, *carried, transition, *(held(blocks) if staged else [blocks]))

    sent, first, *carried = pl.pallas_call(
        begin_kernel,
        out_shape=(outgoing, tile, *(jax.ShapeDtypeStruct(array.shape, array.dtype) for array in small)),
        in_specs=[in_hbm] * (3 + len(small)),
        scratch_shapes=[
            hot,
            left,
            pltpu.VMEM(right_side.shape, F32),
            pltpu.VMEM(precond.shape, F32),
            pltpu.VMEM(slot.shape, jnp.int32),
            pltpu.SemaphoreType.DMA((3 + len(small),)),
        ],
        compiler_params=params,
        name="begin",
    )(*held(right_side, precond, slot, *small))
    back, inertial, sums = grouped(collect(sent), first, True)
    sent, scaled, residual, along, scalars = pl.pallas_call(
        functools.partial(step_kernel, n_time, n_clus, axes),
        out_shape=(outgoing, tile, like(state, width), tile, like(1, LANE)),
        scratch_shapes=[hot, field, left],
        compiler_params=params,
        name="step",
    )(exchange(back), right_side, inertial, precond, slot, sums)
    back, inertial, sums_next = grouped(collect(sent), scaled, False)
    return pl.pallas_call(
        functools.partial(end_kernel, n_time, n_clus, axes),
        out_shape=(like(state, width), like(state, width)),
        scratch_shapes=[hot, field, pltpu.VMEM((ROWS, width), F32)],
        compiler_params=params,
        name="end",
    )(exchange(back), residual, inertial, slot, first, scaled, along, sums, sums_next, scalars)


def solution(mesh):
    placed = (
        P(None, ("tm", "clus")),
        P(None, None, ("tm", "clus")),
        P(None, None, ("tm", "clus")),
        P(("tm", "clus")),
        P("tm", "clus"),
        P("tm", None),
        P("tm", "clus"),
        P("tm", "clus"),
        P(None, None, "tm", "clus"),
    )
    return jax.shard_map(
        on_device,
        mesh=mesh,
        in_specs=placed,
        out_specs=(P(None, ("tm", "clus")), P(None, ("tm", "clus"))),
        check_vma=False,
    )
```

```python
import functools
import jax
import jax.numpy as jnp
from jax import lax
from jax.experimental import pallas as pl
from jax.experimental.pallas import tpu as pltpu
from jax.sharding import PartitionSpec as P

F32 = jnp.float32
BF16 = jnp.bfloat16
ROWS = 16
SUB = 256
LANE = 128
VMEM_LIMIT = 16 * 1024 * 1024


def iota(shape, axis):
    return lax.broadcasted_iota(jnp.int32, shape, axis)


def halves(value):
    high = value.astype(BF16)
    return high, (value - high.astype(F32)).astype(BF16)


def join(pieces):
    return pieces[0] if len(pieces) == 1 else jnp.concatenate(pieces, axis=1)


def spread_row(row, count):
    return jnp.broadcast_to(row.astype(F32), (count, row.shape[1])).astype(BF16)


def hot_tile(index):
    rows = iota((SUB, index.shape[1]), 0).astype(F32).astype(BF16)
    low = spread_row(index & (SUB - 1), SUB)
    return jnp.where(rows == low, jnp.ones((), BF16), jnp.zeros((), BF16))


def hot_table(hot, index_ref, width):
    for start in range(0, width, SUB):
        hot[:, start : start + SUB] = hot_tile(index_ref[0:1, start : start + SUB])


def masked(part, k, value):
    return jnp.where(part == jnp.asarray(k, BF16), value, jnp.zeros((), BF16))


def both(left, right, contract):
    return lax.dot_general(left, right, (contract, ((), ())), preferred_element_type=F32)


def column_to_row(column, state, share):
    spot = iota((ROWS, LANE), 1) % share
    row = iota((ROWS, LANE), 0)
    return jnp.sum(jnp.where((spot == row) & (row < state), column, 0.0), axis=0, keepdims=True)


def row_to_column(row, state):
    width = row.shape[1]
    sub = iota((ROWS, width), 0)
    keep = (sub == iota((ROWS, width), 1)) & (sub < state)
    return jnp.sum(jnp.where(keep, row, 0.0), axis=1, keepdims=True)


def note(column, scalar, state, share):
    spot = iota((1, LANE), 1) % share
    return jnp.where(spot == state, scalar, column_to_row(column, state, share))


def total(value):
    return jnp.sum(jnp.sum(value, axis=0, keepdims=True), axis=1, keepdims=True)


def apply_precond(precond, residual, scaled):
    state, width = residual.shape
    dot = jnp.zeros((state, LANE), F32)
    for start in range(0, width, LANE):
        at = slice(start, start + LANE)
        out = precond[0, :, at] * residual[0:1, at]
        for j in range(1, state):
            out = out + precond[j, :, at] * residual[j : j + 1, at]
        scaled[0:state, at] = out
        scaled[state:ROWS, at] = jnp.zeros((ROWS - state, LANE), F32)
        dot = dot + out * residual[:, at]
    return total(dot)


def send_states(scaled, dot, slot, hot, left, send, state):
    width = scaled.shape[1]
    groups, copies, _, share = send.shape
    parts = width // SUB
    for start in range(0, width, SUB):
        at = slice(start, start + SUB)
        also = slice(width + start, width + start + SUB)
        high, low = halves(scaled[:, at])
        part = spread_row(slot[0:1, at] >> 8, ROWS)
        for k in range(parts):
            rows = slice(k * ROWS, (k + 1) * ROWS)
            left[rows, at] = masked(part, k, high)
            left[rows, also] = masked(part, k, low)
    table = hot[...]
    moved = both(left[:, :width], table, ((1,), (1,))) + both(left[:, width:], table, ((1,), (1,)))
    notes = note(scaled[:, 0:1], dot, state, share)
    sub = iota((ROWS, share), 0)
    for k in range(parts):
        piece = moved[k * ROWS : (k + 1) * ROWS]
        for m in range(SUB // share):
            one = jnp.where(sub == state, notes[:, :share], piece[:, m * share : (m + 1) * share])
            for copy in range(copies):
                send[k * (SUB // share) + m, copy] = one


def begin_kernel(right_in, precond_in, slot_in, *refs):
    carried = len(refs) // 2 - 4
    (send, scaled), (hot, left, right, precond, slot, sems) = refs[carried : carried + 2], refs[2 * carried + 2 :]
    state = right.shape[0]
    copies = fetch(sems, (precond_in, precond), (right_in, right), (slot_in, slot),
                   *zip(refs[:carried], refs[carried + 2 : 2 * carried + 2]))
    copies[2].wait()
    hot_table(hot, slot, right.shape[1])
    copies[1].wait()
    copies[0].wait()
    dot = apply_precond(precond, right, scaled)
    send_states(scaled, dot, slot, hot, left, send, state)
    for copy in copies[3:]:
        copy.wait()


def fetch(sems, *pairs):
    copies = [pltpu.make_async_copy(source, place, sems.at[i]) for i, (source, place) in enumerate(pairs)]
    for copy in copies:
        copy.start()
    return copies


def back_product(transition, errors, at):
    back = transition[0, :, at] * errors[0:1, at]
    for j in range(1, transition.shape[0]):
        back = back + transition[j, :, at] * errors[j : j + 1, at]
    return back


def pull(ends, h, field, parity, state, found_before):
    index = ends[h : h + 8, :]
    low, part = index & (LANE - 1), index >> 7
    out = list(found_before)
    half, tiles = field.shape[0], field.shape[1]
    for i in range(half):
        for r in range(tiles):
            here = part == (2 * i + parity) * tiles + r
            for c in range(state):
                from_row = jnp.broadcast_to(field[i, r, c : c + 1, :], (8, LANE))
                out[c] = jnp.where(here, jnp.take_along_axis(from_row, low, axis=1), out[c])
    return out


def fill(field, got):
    half, tiles = field.shape[0], field.shape[1]
    per = LANE // got.shape[2]
    for i in range(half):
        for r in range(tiles):
            field[i, r] = join([got[(r * per + m) * half + i] for m in range(per)])


def half_kernel(axes, once, got, heads_tile, tails_tile, scaled, transition, *refs):
    state = transition.shape[0]
    width = scaled.shape[1]
    chunks = heads_tile.shape[0]
    if once:
        heads, tails, cluster, damping, blocks_in = refs[:5]
        pulled, errors, inertial, hot, lam, blocks, field, sems = refs[5:]
        (copy,) = fetch(sems, (blocks_in, blocks))
    else:
        pulled, errors, inertial, field = refs
    fill(field, got)
    parity = lax.axis_index(axes[1]) % 2
    zero = [jnp.zeros((8, LANE), F32)] * state
    for h in range(0, chunks, 8):
        for which, ends in enumerate((heads_tile, tails_tile)):
            for c, value in enumerate(pull(ends, h, field, parity, state, zero)):
                pulled[which * state + c, h : h + 8, :] = value
    lane = iota((ROWS, width), 1)
    errors[...] = jnp.where(lane == width - 1, 0.0, pltpu.roll(scaled[...], width - 1, 1))
    for i in range(state):
        moved = jnp.sum(transition[i] * scaled[0:state, :], axis=0, keepdims=True)
        errors[i : i + 1, :] = errors[i : i + 1, :] - moved
    prior = jnp.where(lane == 0, 0.0, pltpu.roll(errors[...], 1, 1))
    inertial[state:ROWS, :] = jnp.zeros((ROWS - state, width), F32)
    for start in range(0, width - LANE, LANE):
        at = slice(start, start + LANE)
        inertial[0:state, at] = prior[0:state, at] - back_product(transition, errors, at)
    inertial[0:state, width - LANE :] = prior[0:state, width - LANE :]
    if once:
        pairs = heads.shape[1]
        hot_table(hot.at[:, 0:pairs], heads, pairs)
        hot_table(hot.at[:, pairs:], tails, pairs)
        row = jnp.zeros(lam.shape, F32)
        for label in range(damping.shape[1]):
            row = jnp.where(cluster[...] == label, damping[0:1, label : label + 1], row)
        lam[...] = row
        copy.wait()


def group_kernel(n_time, n_clus, axes, got, other, pulled, heads, tails, heads_tile, tails_tile, hot, lam, blocks,
                 errors, partial, transition, send, inertial, sums, field, values, left, last):
    state = transition.shape[0]
    width = errors.shape[1]
    share = got.shape[2]
    pairs = heads.shape[1]
    parts = n_clus * width // SUB
    per_part = SUB // share
    chunks = pairs // LANE
    half = n_clus // 2
    time_at, clus_at = lax.axis_index(axes[0]), lax.axis_index(axes[1])
    flat = time_at * n_clus + clus_at
    devices = n_time * n_clus

    def source(piece):
        return (piece % n_time) * n_clus + piece // n_time

    sums[...] = jnp.sum(got[:, state : state + 1, :], axis=0) + jnp.sum(other[:, state : state + 1, :], axis=0)
    fill(field, other)
    parity = 1 - clus_at % 2

    def spread(ends, base, n):
        at = slice(base * LANE + n * SUB, base * LANE + (n + 1) * SUB)
        part = spread_row(ends[0:1, n * SUB : (n + 1) * SUB] >> 8, ROWS)
        row = (base + n * (SUB // LANE)) * ROWS
        high, low = halves(join([values[row + m * ROWS : row + (m + 1) * ROWS, :] for m in range(SUB // LANE)]))
        for k in range(parts):
            left[k * 2 * ROWS : k * 2 * ROWS + ROWS, at] = masked(part, k, high)
            left[k * 2 * ROWS + ROWS : (k + 1) * 2 * ROWS, at] = masked(part, k, low)

    squares = jnp.zeros((8, LANE), F32)
    for h in range(0, chunks, 8):
        near, far = (
            pull(ends, h, field, parity, state, [pulled[which * state + c, h : h + 8, :] for c in range(state)])
            for which, ends in enumerate((heads_tile, tails_tile))
        )
        back = [None] * state
        for i in range(state):
            row = [blocks[i * state + j, h : h + 8, :] for j in range(state)]
            f = near[i]
            for j in range(state):
                f = f - row[j] * far[j]
            squares = squares + f * f
            values[pl.ds(h * ROWS + i, 8, stride=ROWS), :] = f
            for j in range(state):
                back[j] = row[j] * f if i == 0 else back[j] + row[j] * f
        for j in range(state):
            values[pl.ds((chunks + h) * ROWS + j, 8, stride=ROWS), :] = -back[j]
        for j in range(state, ROWS):
            values[pl.ds(h * ROWS + j, 8, stride=ROWS), :] = jnp.zeros((8, LANE), F32)
            values[pl.ds((chunks + h) * ROWS + j, 8, stride=ROWS), :] = jnp.zeros((8, LANE), F32)
    for n in range(pairs // SUB):
        spread(heads, 0, n)
        spread(tails, chunks, n)
    summed = both(left[...], hot[...], ((1,), (1,)))

    after = jnp.minimum(flat + 1, devices - 1)
    following = row_to_column(other[after // n_clus * half + after % n_clus // 2, state : state + 1, :], state)
    at = slice(width - LANE, width)
    ending = iota((ROWS, LANE), 1) == LANE - 1
    closed = ending & (flat == devices - 1)
    ahead = jnp.where(ending, errors[:, at] + following, errors[:, at])
    last[...] = jnp.where(closed | (iota((ROWS, LANE), 0) >= state), 0.0, ahead)
    energy = last[...] * last[...]
    for start in range(0, width - LANE, LANE):
        block = errors[:, start : start + LANE]
        energy = energy + jnp.where(iota((ROWS, LANE), 0) < state, block * block, 0.0)
    product = total(squares) + total(energy)
    inertial[...] = partial[...]
    back = transition[0, :, at] * last[0:1, :]
    for j in range(1, state):
        back = back + transition[j, :, at] * last[j : j + 1, :]
    inertial[0:state, at] = partial[0:state, at] - back

    sub = iota((ROWS, share), 0)
    damped = jnp.zeros((ROWS, share), F32)
    for k in range(parts):
        one = summed[k * 2 * ROWS : k * 2 * ROWS + ROWS] + summed[k * 2 * ROWS + ROWS : (k + 1) * 2 * ROWS]
        for m in range(per_part):
            piece = k * per_part + m
            c, t = piece // n_time, piece % n_time
            here = jnp.where(clus_at == c, lam[:, t * share : (t + 1) * share], 0.0)
            states = jnp.where(sub < state, got[t * half + c // 2], 0.0)
            extra = here * states
            damped = damped + extra * states
            send[source(piece)] = one[:, m * share : (m + 1) * share] + extra
    product = product + total(damped)
    notes = note(last[:, LANE - 1 : LANE], product, state, share)
    for d in range(devices):
        send[d, state : state + 1, :] = notes[:, :share]


def image_of(n_time, n_clus, axes, got, inertial, slot, hot, field, image, state):
    width = image.shape[1]
    share = got.shape[2]
    per_part = SUB // share
    parts = width // SUB
    flat = lax.axis_index(axes[0]) * n_clus + lax.axis_index(axes[1])
    for k in range(parts):
        pieces = []
        for m in range(per_part):
            t = k * per_part + m
            one = got[t * n_clus]
            for c in range(1, n_clus):
                one = one + got[t * n_clus + c]
            pieces.append(one)
        rows = slice(k * ROWS, (k + 1) * ROWS)
        field[rows, 0:SUB], field[rows, SUB:] = halves(join(pieces))
    prior = row_to_column(got[jnp.maximum(flat - 1, 0), state : state + 1, :], state)
    prior = jnp.where(flat == 0, 0.0, prior)
    for start in range(0, width, SUB):
        at = slice(start, start + SUB)
        table = hot[:, at]
        found = both(field[:, 0:SUB], table, ((1,), (0,))) + both(field[:, SUB:], table, ((1,), (0,)))
        part = slot[0:1, at] >> 8
        out = found[0:ROWS]
        for k in range(1, parts):
            out = jnp.where(part == k, found[k * ROWS : (k + 1) * ROWS], out)
        out = out + inertial[:, at]
        if start == 0:
            out = jnp.where(iota((ROWS, SUB), 1) == 0, out + prior, out)
        image[:, at] = out
    return jnp.sum(got[:, state : state + 1, :], axis=0)[:, state : state + 1]


def step_kernel(n_time, n_clus, axes, got, right, inertial, precond, slot, sums,
                send, scaled, residual, image, scalars, hot, field, left):
    state, width = right.shape
    hot_table(hot, slot, width)
    product = image_of(n_time, n_clus, axes, got, inertial, slot, hot, field, image, state)
    alpha = sums[0:1, state : state + 1] / product
    residual[...] = right[...] - alpha * image[0:state, :]
    dot = apply_precond(precond, residual, scaled)
    send_states(scaled, dot, slot, hot, left, send, state)
    scalars[...] = jnp.broadcast_to(alpha, scalars.shape)


def end_kernel(n_time, n_clus, axes, got, residual, inertial, slot, first, scaled, along, sums, sums_next, scalars,
               solution_field, residual_out, hot, field, image):
    state, width = residual.shape
    hot_table(hot, slot, width)
    product = image_of(n_time, n_clus, axes, got, inertial, slot, hot, field, image, state)
    alpha = scalars[0:1, 0:1]
    rz, rz_next = sums[0:1, state : state + 1], sums_next[0:1, state : state + 1]
    ratio = rz_next / rz
    step = rz_next / (product - ratio * rz_next / alpha)
    direction = scaled[0:state, :] + ratio * first[0:state, :]
    solution_field[...] = alpha * first[0:state, :] + step * direction
    residual_out[...] = residual[...] - step * (image[0:state, :] + ratio * along[0:state, :])


def on_device(
    right_side,
    transition,
    precond,
    slot_of,
    cluster_id,
    damping,
    pair_first,
    pair_second,
    pair_blocks,
):
    axes = ("tm", "clus")
    state, width = right_side.shape
    n_time = lax.axis_size("tm")
    n_clus = lax.axis_size("clus")
    devices = n_time * n_clus
    share = width // n_time
    pairs = pair_first.shape[1]
    positions = n_clus * width
    slot = slot_of.reshape(1, width)
    blocks = pair_blocks.reshape(state * state, pairs // LANE, LANE)
    params = pltpu.CompilerParams(vmem_limit_bytes=VMEM_LIMIT)

    def like(*shape):
        return jax.ShapeDtypeStruct(shape, F32)

    message = like(devices, ROWS, share)
    outgoing = like(n_time, n_clus // 2, ROWS, share)
    row = like(1, share)
    tile = like(ROWS, width)
    hot = pltpu.VMEM((SUB, width), BF16)
    left = pltpu.VMEM((ROWS * width // SUB, 2 * width), BF16)
    terms = pltpu.VMEM((ROWS * width // SUB, 2 * SUB), BF16)

    def exchange(sent):
        return lax.all_to_all(sent.reshape(devices, ROWS, share), axes, split_axis=0, concat_axis=0, tiled=True)

    def held(*arrays):
        return tuple(pltpu.with_memory_space_constraint(array, pltpu.HBM) for array in arrays)

    in_hbm = pl.BlockSpec(memory_space=pltpu.HBM)
    in_vmem = pl.BlockSpec(memory_space=pltpu.VMEM)
    dense = (pairs // LANE, LANE)
    small = (pair_first, pair_second, pair_first.reshape(dense), pair_second.reshape(dense), cluster_id, damping)
    same = [[t * n_clus + c for t in range(n_time) for c in range(q, n_clus, 2)] for q in range(2)]
    field = pltpu.VMEM((n_clus // 2, width // LANE, ROWS, LANE), F32)

    def collect(sent):
        sent = sent.reshape(devices // 2, ROWS, share)
        got = lax.all_to_all(sent, axes, split_axis=0, concat_axis=0, tiled=True, axis_index_groups=same)
        return got, lax.ppermute(got, "clus", [(c, c ^ 1) for c in range(n_clus)])

    def grouped(sent, scaled, carried, tables):
        got, other = collect(sent)
        heads, tails, heads_tile, tails_tile, cluster, lam_of = carried
        shapes = (like(2 * state, *dense), tile, tile)
        operands = (got, heads_tile, tails_tile, scaled, transition)
        scratch = [field]
        if not tables:
            shapes += (jax.ShapeDtypeStruct((SUB, 2 * pairs), BF16), like(1, width), like(*blocks.shape))
            operands += (heads, tails, cluster, lam_of, *held(blocks))
            scratch += [pltpu.SemaphoreType.DMA((1,))]
        pulled, errors, partial, *fresh = pl.pallas_call(
            functools.partial(half_kernel, axes, not tables),
            out_shape=shapes,
            in_specs=[in_vmem] * (len(operands) - 1) + [in_vmem if tables else in_hbm],
            scratch_shapes=scratch,
            compiler_params=params,
            name="half",
        )(*operands)
        tables = tables or fresh
        return tables, pl.pallas_call(
            functools.partial(group_kernel, n_time, n_clus, axes),
            out_shape=(message, tile, row),
            scratch_shapes=[
                field,
                pltpu.VMEM((2 * pairs // LANE * ROWS, LANE), F32),
                pltpu.VMEM((2 * ROWS * positions // SUB, 2 * pairs), BF16),
                pltpu.VMEM((ROWS, LANE), F32),
            ],
            compiler_params=params,
            name="group",
        )(got, other, pulled, heads, tails, heads_tile, tails_tile, *tables, errors, partial, transition)

    sent, first, *carried = pl.pallas_call(
        begin_kernel,
        out_shape=(outgoing, tile, *(jax.ShapeDtypeStruct(array.shape, array.dtype) for array in small)),
        in_specs=[in_hbm] * (3 + len(small)),
        scratch_shapes=[
            hot,
            left,
            pltpu.VMEM(right_side.shape, F32),
            pltpu.VMEM(precond.shape, F32),
            pltpu.VMEM(slot.shape, jnp.int32),
            pltpu.SemaphoreType.DMA((3 + len(small),)),
        ],
        compiler_params=params,
        name="begin",
    )(*held(right_side, precond, slot, *small))
    tables, (back, inertial, sums) = grouped(sent, first, carried, None)
    sent, scaled, residual, along, scalars = pl.pallas_call(
        functools.partial(step_kernel, n_time, n_clus, axes),
        out_shape=(outgoing, tile, like(state, width), tile, like(1, LANE)),
        scratch_shapes=[hot, terms, left],
        compiler_params=params,
        name="step",
    )(exchange(back), right_side, inertial, precond, slot, sums)
    _, (back, inertial, sums_next) = grouped(sent, scaled, carried, tables)
    return pl.pallas_call(
        functools.partial(end_kernel, n_time, n_clus, axes),
        out_shape=(like(state, width), like(state, width)),
        scratch_shapes=[hot, terms, pltpu.VMEM((ROWS, width), F32)],
        compiler_params=params,
        name="end",
    )(exchange(back), residual, inertial, slot, first, scaled, along, sums, sums_next, scalars)


def solution(mesh):
    placed = (
        P(None, ("tm", "clus")),
        P(None, None, ("tm", "clus")),
        P(None, None, ("tm", "clus")),
        P(("tm", "clus")),
        P("tm", "clus"),
        P("tm", None),
        P("tm", "clus"),
        P("tm", "clus"),
        P(None, None, "tm", "clus"),
    )
    return jax.shard_map(
        on_device,
        mesh=mesh,
        in_specs=placed,
        out_specs=(P(None, ("tm", "clus")), P(None, ("tm", "clus"))),
        check_vma=False,
    )
```

```python
import functools
import jax
import jax.numpy as jnp
from jax import lax
from jax.experimental import pallas as pl
from jax.experimental.pallas import tpu as pltpu
from jax.sharding import PartitionSpec as P

F32 = jnp.float32
BF16 = jnp.bfloat16
ROWS = 16
SUB = 256
LANE = 128
VMEM_LIMIT = 16 * 1024 * 1024


def iota(shape, axis):
    return lax.broadcasted_iota(jnp.int32, shape, axis)


def halves(value):
    high = value.astype(BF16)
    return high, (value - high.astype(F32)).astype(BF16)


def join(pieces):
    return pieces[0] if len(pieces) == 1 else jnp.concatenate(pieces, axis=1)


def spread_row(row, count):
    return jnp.broadcast_to(row.astype(F32), (count, row.shape[1])).astype(BF16)


def hot_tile(index):
    rows = iota((SUB, index.shape[1]), 0).astype(F32).astype(BF16)
    low = spread_row(index & (SUB - 1), SUB)
    return jnp.where(rows == low, jnp.ones((), BF16), jnp.zeros((), BF16))


def hot_table(hot, index_ref, width):
    for start in range(0, width, SUB):
        hot[:, start : start + SUB] = hot_tile(index_ref[0:1, start : start + SUB])


def masked(part, k, value):
    return jnp.where(part == jnp.asarray(k, BF16), value, jnp.zeros((), BF16))


def both(left, right, contract):
    return lax.dot_general(left, right, (contract, ((), ())), preferred_element_type=F32)


def column_to_row(column, state, share):
    spot = iota((ROWS, LANE), 1) % share
    row = iota((ROWS, LANE), 0)
    return jnp.sum(jnp.where((spot == row) & (row < state), column, 0.0), axis=0, keepdims=True)


def row_to_column(row, state):
    width = row.shape[1]
    sub = iota((ROWS, width), 0)
    keep = (sub == iota((ROWS, width), 1)) & (sub < state)
    return jnp.sum(jnp.where(keep, row, 0.0), axis=1, keepdims=True)


def note(column, scalar, state, share):
    spot = iota((1, LANE), 1) % share
    return jnp.where(spot == state, scalar, column_to_row(column, state, share))


def total(value):
    return jnp.sum(jnp.sum(value, axis=0, keepdims=True), axis=1, keepdims=True)


def apply_precond(precond, residual, scaled):
    state, width = residual.shape
    dot = jnp.zeros((state, LANE), F32)
    for start in range(0, width, LANE):
        at = slice(start, start + LANE)
        out = precond[0, :, at] * residual[0:1, at]
        for j in range(1, state):
            out = out + precond[j, :, at] * residual[j : j + 1, at]
        scaled[0:state, at] = out
        scaled[state:ROWS, at] = jnp.zeros((ROWS - state, LANE), F32)
        dot = dot + out * residual[:, at]
    return total(dot)


def send_states(scaled, dot, slot, hot, left, send, state):
    width = scaled.shape[1]
    groups, copies, _, share = send.shape
    parts = width // SUB
    for start in range(0, width, SUB):
        at = slice(start, start + SUB)
        also = slice(width + start, width + start + SUB)
        high, low = halves(scaled[:, at])
        part = spread_row(slot[0:1, at] >> 8, ROWS)
        for k in range(parts):
            rows = slice(k * ROWS, (k + 1) * ROWS)
            left[rows, at] = masked(part, k, high)
            left[rows, also] = masked(part, k, low)
    table = hot[...]
    moved = both(left[:, :width], table, ((1,), (1,))) + both(left[:, width:], table, ((1,), (1,)))
    notes = note(scaled[:, 0:1], dot, state, share)
    sub = iota((ROWS, share), 0)
    for k in range(parts):
        piece = moved[k * ROWS : (k + 1) * ROWS]
        for m in range(SUB // share):
            one = jnp.where(sub == state, notes[:, :share], piece[:, m * share : (m + 1) * share])
            for copy in range(copies):
                send[k * (SUB // share) + m, copy] = one


def begin_kernel(right_in, precond_in, slot_in, heads_in, tails_in, heads_tile_in, tails_tile_in, cluster_in, damping_in,
                 send, scaled, heads, tails, heads_tile, tails_tile, hot_pairs, lam,
                 hot, left, right, precond, slot, cluster, damping, sems):
    state = right.shape[0]
    copies = fetch(sems, (precond_in, precond), (heads_in, heads), (tails_in, tails), (slot_in, slot), (right_in, right),
                   (cluster_in, cluster), (damping_in, damping), (heads_tile_in, heads_tile), (tails_tile_in, tails_tile))
    pairs = heads.shape[1]
    copies[1].wait()
    hot_table(hot_pairs.at[:, 0:pairs], heads, pairs)
    copies[2].wait()
    hot_table(hot_pairs.at[:, pairs:], tails, pairs)
    copies[3].wait()
    hot_table(hot, slot, right.shape[1])
    copies[5].wait()
    copies[6].wait()
    row = jnp.zeros(lam.shape, F32)
    for label in range(damping.shape[1]):
        row = jnp.where(cluster[...] == label, damping[0:1, label : label + 1], row)
    lam[...] = row
    copies[4].wait()
    copies[0].wait()
    dot = apply_precond(precond, right, scaled)
    send_states(scaled, dot, slot, hot, left, send, state)
    copies[7].wait()
    copies[8].wait()


def fetch(sems, *pairs):
    copies = [pltpu.make_async_copy(source, place, sems.at[i]) for i, (source, place) in enumerate(pairs)]
    for copy in copies:
        copy.start()
    return copies


def back_product(transition, errors, at):
    back = transition[0, :, at] * errors[0:1, at]
    for j in range(1, transition.shape[0]):
        back = back + transition[j, :, at] * errors[j : j + 1, at]
    return back


def pull(ends, h, field, parity, state, found_before):
    index = ends[h : h + 8, :]
    low, part = index & (LANE - 1), index >> 7
    out = list(found_before)
    half, tiles = field.shape[0], field.shape[1]
    for i in range(half):
        for r in range(tiles):
            here = part == (2 * i + parity) * tiles + r
            for c in range(state):
                from_row = jnp.broadcast_to(field[i, r, c : c + 1, :], (8, LANE))
                out[c] = jnp.where(here, jnp.take_along_axis(from_row, low, axis=1), out[c])
    return out


def fill(field, got):
    half, tiles = field.shape[0], field.shape[1]
    per = LANE // got.shape[2]
    for i in range(half):
        for r in range(tiles):
            field[i, r] = join([got[(r * per + m) * half + i] for m in range(per)])


def half_kernel(axes, once, got, heads_tile, tails_tile, scaled, transition, *refs):
    state = transition.shape[0]
    width = scaled.shape[1]
    chunks = heads_tile.shape[0]
    if once:
        blocks_in, pulled, errors, inertial, blocks, field, sems = refs
        (copy,) = fetch(sems, (blocks_in, blocks))
    else:
        pulled, errors, inertial, field = refs
    fill(field, got)
    parity = lax.axis_index(axes[1]) % 2
    zero = [jnp.zeros((8, LANE), F32)] * state
    for h in range(0, chunks, 8):
        for which, ends in enumerate((heads_tile, tails_tile)):
            for c, value in enumerate(pull(ends, h, field, parity, state, zero)):
                pulled[which * state + c, h : h + 8, :] = value
    lane = iota((ROWS, width), 1)
    errors[...] = jnp.where(lane == width - 1, 0.0, pltpu.roll(scaled[...], width - 1, 1))
    for i in range(state):
        moved = jnp.sum(transition[i] * scaled[0:state, :], axis=0, keepdims=True)
        errors[i : i + 1, :] = errors[i : i + 1, :] - moved
    prior = jnp.where(lane == 0, 0.0, pltpu.roll(errors[...], 1, 1))
    inertial[state:ROWS, :] = jnp.zeros((ROWS - state, width), F32)
    for start in range(0, width - LANE, LANE):
        at = slice(start, start + LANE)
        inertial[0:state, at] = prior[0:state, at] - back_product(transition, errors, at)
    inertial[0:state, width - LANE :] = prior[0:state, width - LANE :]
    if once:
        copy.wait()


def group_kernel(n_time, n_clus, axes, got, other, pulled, heads, tails, heads_tile, tails_tile, hot, lam, blocks,
                 errors, partial, transition, send, inertial, sums, field, values, left, last):
    state = transition.shape[0]
    width = errors.shape[1]
    share = got.shape[2]
    pairs = heads.shape[1]
    parts = n_clus * width // SUB
    per_part = SUB // share
    chunks = pairs // LANE
    half = n_clus // 2
    time_at, clus_at = lax.axis_index(axes[0]), lax.axis_index(axes[1])
    flat = time_at * n_clus + clus_at
    devices = n_time * n_clus

    def source(piece):
        return (piece % n_time) * n_clus + piece // n_time

    sums[...] = jnp.sum(got[:, state : state + 1, :], axis=0) + jnp.sum(other[:, state : state + 1, :], axis=0)
    fill(field, other)
    parity = 1 - clus_at % 2

    def spread(ends, base, n):
        at = slice(base * LANE + n * SUB, base * LANE + (n + 1) * SUB)
        part = spread_row(ends[0:1, n * SUB : (n + 1) * SUB] >> 8, ROWS)
        row = (base + n * (SUB // LANE)) * ROWS
        high, low = halves(join([values[row + m * ROWS : row + (m + 1) * ROWS, :] for m in range(SUB // LANE)]))
        for k in range(parts):
            left[k * 2 * ROWS : k * 2 * ROWS + ROWS, at] = masked(part, k, high)
            left[k * 2 * ROWS + ROWS : (k + 1) * 2 * ROWS, at] = masked(part, k, low)

    squares = jnp.zeros((8, LANE), F32)
    for h in range(0, chunks, 8):
        near, far = (
            pull(ends, h, field, parity, state, [pulled[which * state + c, h : h + 8, :] for c in range(state)])
            for which, ends in enumerate((heads_tile, tails_tile))
        )
        back = [None] * state
        for i in range(state):
            row = [blocks[i * state + j, h : h + 8, :] for j in range(state)]
            f = near[i]
            for j in range(state):
                f = f - row[j] * far[j]
            squares = squares + f * f
            values[pl.ds(h * ROWS + i, 8, stride=ROWS), :] = f
            for j in range(state):
                back[j] = row[j] * f if i == 0 else back[j] + row[j] * f
        for j in range(state):
            values[pl.ds((chunks + h) * ROWS + j, 8, stride=ROWS), :] = -back[j]
        for j in range(state, ROWS):
            values[pl.ds(h * ROWS + j, 8, stride=ROWS), :] = jnp.zeros((8, LANE), F32)
            values[pl.ds((chunks + h) * ROWS + j, 8, stride=ROWS), :] = jnp.zeros((8, LANE), F32)
    for n in range(pairs // SUB):
        spread(heads, 0, n)
        spread(tails, chunks, n)
    summed = both(left[...], hot[...], ((1,), (1,)))

    after = jnp.minimum(flat + 1, devices - 1)
    following = row_to_column(other[after // n_clus * half + after % n_clus // 2, state : state + 1, :], state)
    at = slice(width - LANE, width)
    ending = iota((ROWS, LANE), 1) == LANE - 1
    closed = ending & (flat == devices - 1)
    ahead = jnp.where(ending, errors[:, at] + following, errors[:, at])
    last[...] = jnp.where(closed | (iota((ROWS, LANE), 0) >= state), 0.0, ahead)
    energy = last[...] * last[...]
    for start in range(0, width - LANE, LANE):
        block = errors[:, start : start + LANE]
        energy = energy + jnp.where(iota((ROWS, LANE), 0) < state, block * block, 0.0)
    product = total(squares) + total(energy)
    inertial[...] = partial[...]
    back = transition[0, :, at] * last[0:1, :]
    for j in range(1, state):
        back = back + transition[j, :, at] * last[j : j + 1, :]
    inertial[0:state, at] = partial[0:state, at] - back

    sub = iota((ROWS, share), 0)
    damped = jnp.zeros((ROWS, share), F32)
    for k in range(parts):
        one = summed[k * 2 * ROWS : k * 2 * ROWS + ROWS] + summed[k * 2 * ROWS + ROWS : (k + 1) * 2 * ROWS]
        for m in range(per_part):
            piece = k * per_part + m
            c, t = piece // n_time, piece % n_time
            here = jnp.where(clus_at == c, lam[:, t * share : (t + 1) * share], 0.0)
            states = jnp.where(sub < state, got[t * half + c // 2], 0.0)
            extra = here * states
            damped = damped + extra * states
            send[source(piece)] = one[:, m * share : (m + 1) * share] + extra
    product = product + total(damped)
    notes = note(last[:, LANE - 1 : LANE], product, state, share)
    for d in range(devices):
        send[d, state : state + 1, :] = notes[:, :share]


def image_of(n_time, n_clus, axes, got, inertial, slot, hot, field, image, state):
    width = image.shape[1]
    share = got.shape[2]
    per_part = SUB // share
    parts = width // SUB
    flat = lax.axis_index(axes[0]) * n_clus + lax.axis_index(axes[1])
    for k in range(parts):
        pieces = []
        for m in range(per_part):
            t = k * per_part + m
            one = got[t * n_clus]
            for c in range(1, n_clus):
                one = one + got[t * n_clus + c]
            pieces.append(one)
        rows = slice(k * ROWS, (k + 1) * ROWS)
        field[rows, 0:SUB], field[rows, SUB:] = halves(join(pieces))
    prior = row_to_column(got[jnp.maximum(flat - 1, 0), state : state + 1, :], state)
    prior = jnp.where(flat == 0, 0.0, prior)
    for start in range(0, width, SUB):
        at = slice(start, start + SUB)
        table = hot[:, at]
        found = both(field[:, 0:SUB], table, ((1,), (0,))) + both(field[:, SUB:], table, ((1,), (0,)))
        part = slot[0:1, at] >> 8
        out = found[0:ROWS]
        for k in range(1, parts):
            out = jnp.where(part == k, found[k * ROWS : (k + 1) * ROWS], out)
        out = out + inertial[:, at]
        if start == 0:
            out = jnp.where(iota((ROWS, SUB), 1) == 0, out + prior, out)
        image[:, at] = out
    return jnp.sum(got[:, state : state + 1, :], axis=0)[:, state : state + 1]


def step_kernel(n_time, n_clus, axes, got, right, inertial, precond, slot, sums,
                send, scaled, residual, image, scalars, hot, field, left):
    state, width = right.shape
    hot_table(hot, slot, width)
    product = image_of(n_time, n_clus, axes, got, inertial, slot, hot, field, image, state)
    alpha = sums[0:1, state : state + 1] / product
    residual[...] = right[...] - alpha * image[0:state, :]
    dot = apply_precond(precond, residual, scaled)
    send_states(scaled, dot, slot, hot, left, send, state)
    scalars[...] = jnp.broadcast_to(alpha, scalars.shape)


def end_kernel(n_time, n_clus, axes, got, residual, inertial, slot, first, scaled, along, sums, sums_next, scalars,
               solution_field, residual_out, hot, field, image):
    state, width = residual.shape
    hot_table(hot, slot, width)
    product = image_of(n_time, n_clus, axes, got, inertial, slot, hot, field, image, state)
    alpha = scalars[0:1, 0:1]
    rz, rz_next = sums[0:1, state : state + 1], sums_next[0:1, state : state + 1]
    ratio = rz_next / rz
    step = rz_next / (product - ratio * rz_next / alpha)
    direction = scaled[0:state, :] + ratio * first[0:state, :]
    solution_field[...] = alpha * first[0:state, :] + step * direction
    residual_out[...] = residual[...] - step * (image[0:state, :] + ratio * along[0:state, :])


def on_device(
    right_side,
    transition,
    precond,
    slot_of,
    cluster_id,
    damping,
    pair_first,
    pair_second,
    pair_blocks,
):
    axes = ("tm", "clus")
    state, width = right_side.shape
    n_time = lax.axis_size("tm")
    n_clus = lax.axis_size("clus")
    devices = n_time * n_clus
    share = width // n_time
    pairs = pair_first.shape[1]
    positions = n_clus * width
    slot = slot_of.reshape(1, width)
    blocks = pair_blocks.reshape(state * state, pairs // LANE, LANE)
    params = pltpu.CompilerParams(vmem_limit_bytes=VMEM_LIMIT)

    def like(*shape):
        return jax.ShapeDtypeStruct(shape, F32)

    message = like(devices, ROWS, share)
    outgoing = like(n_time, n_clus // 2, ROWS, share)
    row = like(1, share)
    tile = like(ROWS, width)
    hot = pltpu.VMEM((SUB, width), BF16)
    left = pltpu.VMEM((ROWS * width // SUB, 2 * width), BF16)
    terms = pltpu.VMEM((ROWS * width // SUB, 2 * SUB), BF16)

    def exchange(sent):
        return lax.all_to_all(sent.reshape(devices, ROWS, share), axes, split_axis=0, concat_axis=0, tiled=True)

    def held(*arrays):
        return tuple(pltpu.with_memory_space_constraint(array, pltpu.HBM) for array in arrays)

    in_hbm = pl.BlockSpec(memory_space=pltpu.HBM)
    in_vmem = pl.BlockSpec(memory_space=pltpu.VMEM)
    dense = (pairs // LANE, LANE)
    small = (pair_first, pair_second, pair_first.reshape(dense), pair_second.reshape(dense), cluster_id, damping)
    same = [[t * n_clus + c for t in range(n_time) for c in range(q, n_clus, 2)] for q in range(2)]
    field = pltpu.VMEM((n_clus // 2, width // LANE, ROWS, LANE), F32)

    def collect(sent):
        sent = sent.reshape(devices // 2, ROWS, share)
        got = lax.all_to_all(sent, axes, split_axis=0, concat_axis=0, tiled=True, axis_index_groups=same)
        return got, lax.ppermute(got, "clus", [(c, c ^ 1) for c in range(n_clus)])

    def grouped(sent, scaled, carried, tables):
        got, other = collect(sent)
        heads, tails, heads_tile, tails_tile, hot_of, lam = carried
        shapes = (like(2 * state, *dense), tile, tile)
        operands = (got, heads_tile, tails_tile, scaled, transition)
        scratch = [field]
        if not tables:
            shapes += (like(*blocks.shape),)
            operands += held(blocks)
            scratch += [pltpu.SemaphoreType.DMA((1,))]
        pulled, errors, partial, *fresh = pl.pallas_call(
            functools.partial(half_kernel, axes, not tables),
            out_shape=shapes,
            in_specs=[in_vmem] * (len(operands) - 1) + [in_vmem if tables else in_hbm],
            scratch_shapes=scratch,
            compiler_params=params,
            name="half",
        )(*operands)
        tables = tables or fresh
        return tables, pl.pallas_call(
            functools.partial(group_kernel, n_time, n_clus, axes),
            out_shape=(message, tile, row),
            scratch_shapes=[
                field,
                pltpu.VMEM((2 * pairs // LANE * ROWS, LANE), F32),
                pltpu.VMEM((2 * ROWS * positions // SUB, 2 * pairs), BF16),
                pltpu.VMEM((ROWS, LANE), F32),
            ],
            compiler_params=params,
            name="group",
        )(got, other, pulled, heads, tails, heads_tile, tails_tile, hot_of, lam, *tables, errors, partial, transition)

    sent, first, *carried = pl.pallas_call(
        begin_kernel,
        out_shape=(
            outgoing,
            tile,
            *(jax.ShapeDtypeStruct(array.shape, array.dtype) for array in small[:4]),
            jax.ShapeDtypeStruct((SUB, 2 * pairs), BF16),
            like(1, width),
        ),
        in_specs=[in_hbm] * (3 + len(small)),
        scratch_shapes=[
            hot,
            left,
            pltpu.VMEM(right_side.shape, F32),
            pltpu.VMEM(precond.shape, F32),
            pltpu.VMEM(slot.shape, jnp.int32),
            pltpu.VMEM(cluster_id.shape, jnp.int32),
            pltpu.VMEM(damping.shape, F32),
            pltpu.SemaphoreType.DMA((3 + len(small),)),
        ],
        compiler_params=params,
        name="begin",
    )(*held(right_side, precond, slot, *small))
    tables, (back, inertial, sums) = grouped(sent, first, carried, None)
    sent, scaled, residual, along, scalars = pl.pallas_call(
        functools.partial(step_kernel, n_time, n_clus, axes),
        out_shape=(outgoing, tile, like(state, width), tile, like(1, LANE)),
        scratch_shapes=[hot, terms, left],
        compiler_params=params,
        name="step",
    )(exchange(back), right_side, inertial, precond, slot, sums)
    _, (back, inertial, sums_next) = grouped(sent, scaled, carried, tables)
    return pl.pallas_call(
        functools.partial(end_kernel, n_time, n_clus, axes),
        out_shape=(like(state, width), like(state, width)),
        scratch_shapes=[hot, terms, pltpu.VMEM((ROWS, width), F32)],
        compiler_params=params,
        name="end",
    )(exchange(back), residual, inertial, slot, first, scaled, along, sums, sums_next, scalars)


def solution(mesh):
    placed = (
        P(None, ("tm", "clus")),
        P(None, None, ("tm", "clus")),
        P(None, None, ("tm", "clus")),
        P(("tm", "clus")),
        P("tm", "clus"),
        P("tm", None),
        P("tm", "clus"),
        P("tm", "clus"),
        P(None, None, "tm", "clus"),
    )
    return jax.shard_map(
        on_device,
        mesh=mesh,
        in_specs=placed,
        out_specs=(P(None, ("tm", "clus")), P(None, ("tm", "clus"))),
        check_vma=False,
    )
```

```python
import functools
import jax
import jax.numpy as jnp
from jax import lax
from jax.experimental import pallas as pl
from jax.experimental.pallas import tpu as pltpu
from jax.sharding import PartitionSpec as P

F32 = jnp.float32
BF16 = jnp.bfloat16
ROWS = 16
SUB = 256
LANE = 128
VMEM_LIMIT = 16 * 1024 * 1024


def iota(shape, axis):
    return lax.broadcasted_iota(jnp.int32, shape, axis)


def halves(value):
    high = value.astype(BF16)
    return high, (value - high.astype(F32)).astype(BF16)


def join(pieces):
    return pieces[0] if len(pieces) == 1 else jnp.concatenate(pieces, axis=1)


def spread_row(row, count):
    return jnp.broadcast_to(row.astype(F32), (count, row.shape[1])).astype(BF16)


def hot_tile(index):
    rows = iota((SUB, index.shape[1]), 0).astype(F32).astype(BF16)
    low = spread_row(index & (SUB - 1), SUB)
    return jnp.where(rows == low, jnp.ones((), BF16), jnp.zeros((), BF16))


def hot_table(hot, index_ref, width):
    for start in range(0, width, SUB):
        hot[:, start : start + SUB] = hot_tile(index_ref[0:1, start : start + SUB])


def masked(part, k, value):
    return jnp.where(part == jnp.asarray(k, BF16), value, jnp.zeros((), BF16))


def both(left, right, contract):
    return lax.dot_general(left, right, (contract, ((), ())), preferred_element_type=F32)


def column_to_row(column, state, share):
    spot = iota((ROWS, LANE), 1) % share
    row = iota((ROWS, LANE), 0)
    return jnp.sum(jnp.where((spot == row) & (row < state), column, 0.0), axis=0, keepdims=True)


def row_to_column(row, state):
    width = row.shape[1]
    sub = iota((ROWS, width), 0)
    keep = (sub == iota((ROWS, width), 1)) & (sub < state)
    return jnp.sum(jnp.where(keep, row, 0.0), axis=1, keepdims=True)


def note(column, scalar, state, share):
    spot = iota((1, LANE), 1) % share
    return jnp.where(spot == state, scalar, column_to_row(column, state, share))


def total(value):
    return jnp.sum(jnp.sum(value, axis=0, keepdims=True), axis=1, keepdims=True)


def apply_precond(precond, residual, scaled):
    state, width = residual.shape
    dot = jnp.zeros((state, LANE), F32)
    for start in range(0, width, LANE):
        at = slice(start, start + LANE)
        out = precond[0, :, at] * residual[0:1, at]
        for j in range(1, state):
            out = out + precond[j, :, at] * residual[j : j + 1, at]
        scaled[0:state, at] = out
        scaled[state:ROWS, at] = jnp.zeros((ROWS - state, LANE), F32)
        dot = dot + out * residual[:, at]
    return total(dot)


def reorder(tiles, index):
    low = jnp.broadcast_to(index & (LANE - 1), (ROWS, LANE))
    part = jnp.broadcast_to(index >> 7, (ROWS, LANE))
    out = jnp.zeros((ROWS, LANE), F32)
    for k, one in enumerate(tiles):
        out = jnp.where(part == k, jnp.take_along_axis(one, low, axis=1), out)
    return out


def send_states(scaled, dot, origin, send, state):
    width = scaled.shape[1]
    copies, _, share = send.shape[1:]
    notes = note(scaled[:, 0:1], dot, state, share)
    tiles = [scaled[:, start : start + LANE] for start in range(0, width, LANE)]
    sub = iota((ROWS, share), 0)
    for k in range(width // LANE):
        piece = reorder(tiles, origin[0:1, k * LANE : (k + 1) * LANE])
        for m in range(LANE // share):
            one = jnp.where(sub == state, notes[:, :share], piece[:, m * share : (m + 1) * share])
            for copy in range(copies):
                send[k * (LANE // share) + m, copy] = one


def invert(slot, hot, left, origin):
    width = slot.shape[1]
    hot_table(hot, slot, width)
    sub = iota((ROWS, SUB), 0)
    for start in range(0, width, SUB):
        number = iota((ROWS, SUB), 1) + start
        digits = jnp.where(sub == 0, number >> 5, jnp.where(sub == 1, number & 31, 0)).astype(F32).astype(BF16)
        part = spread_row(slot[0:1, start : start + SUB] >> 8, ROWS)
        for k in range(width // SUB):
            left[k * ROWS : (k + 1) * ROWS, start : start + SUB] = masked(part, k, digits)
    found = both(left[...], hot[...], ((1,), (1,)))
    for k in range(width // SUB):
        row = 32.0 * found[k * ROWS : k * ROWS + 1] + found[k * ROWS + 1 : k * ROWS + 2]
        origin[0:1, k * SUB : (k + 1) * SUB] = row.astype(jnp.int32)


def begin_kernel(right_in, precond_in, slot_in, heads_in, tails_in, heads_tile_in, tails_tile_in, cluster_in, damping_in,
                 send, scaled, origin, heads, tails, heads_tile, tails_tile, hot_pairs, lam,
                 hot, left, right, precond, slot, cluster, damping, sems):
    state = right.shape[0]
    copies = fetch(sems, (precond_in, precond), (heads_in, heads), (tails_in, tails), (slot_in, slot), (right_in, right),
                   (cluster_in, cluster), (damping_in, damping), (heads_tile_in, heads_tile), (tails_tile_in, tails_tile))
    pairs = heads.shape[1]
    copies[3].wait()
    invert(slot, hot, left, origin)
    copies[1].wait()
    hot_table(hot_pairs.at[:, 0:pairs], heads, pairs)
    copies[2].wait()
    hot_table(hot_pairs.at[:, pairs:], tails, pairs)
    copies[5].wait()
    copies[6].wait()
    row = jnp.zeros(lam.shape, F32)
    for label in range(damping.shape[1]):
        row = jnp.where(cluster[...] == label, damping[0:1, label : label + 1], row)
    lam[...] = row
    copies[4].wait()
    copies[0].wait()
    dot = apply_precond(precond, right, scaled)
    send_states(scaled, dot, origin, send, state)
    copies[7].wait()
    copies[8].wait()


def fetch(sems, *pairs):
    copies = [pltpu.make_async_copy(source, place, sems.at[i]) for i, (source, place) in enumerate(pairs)]
    for copy in copies:
        copy.start()
    return copies


def back_product(transition, errors, at):
    back = transition[0, :, at] * errors[0:1, at]
    for j in range(1, transition.shape[0]):
        back = back + transition[j, :, at] * errors[j : j + 1, at]
    return back


def pull(ends, h, field, parity, state, found_before):
    index = ends[h : h + 8, :]
    low, part = index & (LANE - 1), index >> 7
    out = list(found_before)
    half, tiles = field.shape[0], field.shape[1]
    for i in range(half):
        for r in range(tiles):
            here = part == (2 * i + parity) * tiles + r
            for c in range(state):
                from_row = jnp.broadcast_to(field[i, r, c : c + 1, :], (8, LANE))
                out[c] = jnp.where(here, jnp.take_along_axis(from_row, low, axis=1), out[c])
    return out


def fill(field, got):
    half, tiles = field.shape[0], field.shape[1]
    per = LANE // got.shape[2]
    for i in range(half):
        for r in range(tiles):
            field[i, r] = join([got[(r * per + m) * half + i] for m in range(per)])


def half_kernel(axes, once, got, heads_tile, tails_tile, scaled, transition, *refs):
    state = transition.shape[0]
    width = scaled.shape[1]
    chunks = heads_tile.shape[0]
    if once:
        blocks_in, pulled, errors, inertial, blocks, field, sems = refs
        (copy,) = fetch(sems, (blocks_in, blocks))
    else:
        pulled, errors, inertial, field = refs
    fill(field, got)
    parity = lax.axis_index(axes[1]) % 2
    zero = [jnp.zeros((8, LANE), F32)] * state
    for h in range(0, chunks, 8):
        for which, ends in enumerate((heads_tile, tails_tile)):
            for c, value in enumerate(pull(ends, h, field, parity, state, zero)):
                pulled[which * state + c, h : h + 8, :] = value
    lane = iota((ROWS, width), 1)
    errors[...] = jnp.where(lane == width - 1, 0.0, pltpu.roll(scaled[...], width - 1, 1))
    for i in range(state):
        moved = jnp.sum(transition[i] * scaled[0:state, :], axis=0, keepdims=True)
        errors[i : i + 1, :] = errors[i : i + 1, :] - moved
    prior = jnp.where(lane == 0, 0.0, pltpu.roll(errors[...], 1, 1))
    inertial[state:ROWS, :] = jnp.zeros((ROWS - state, width), F32)
    for start in range(0, width - LANE, LANE):
        at = slice(start, start + LANE)
        inertial[0:state, at] = prior[0:state, at] - back_product(transition, errors, at)
    inertial[0:state, width - LANE :] = prior[0:state, width - LANE :]
    if once:
        copy.wait()


def group_kernel(n_time, n_clus, axes, got, other, pulled, heads, tails, heads_tile, tails_tile, hot, lam, blocks,
                 errors, partial, transition, send, inertial, sums, field, values, left, last):
    state = transition.shape[0]
    width = errors.shape[1]
    share = got.shape[2]
    pairs = heads.shape[1]
    parts = n_clus * width // SUB
    per_part = SUB // share
    chunks = pairs // LANE
    half = n_clus // 2
    time_at, clus_at = lax.axis_index(axes[0]), lax.axis_index(axes[1])
    flat = time_at * n_clus + clus_at
    devices = n_time * n_clus

    def source(piece):
        return (piece % n_time) * n_clus + piece // n_time

    sums[...] = jnp.sum(got[:, state : state + 1, :], axis=0) + jnp.sum(other[:, state : state + 1, :], axis=0)
    fill(field, other)
    parity = 1 - clus_at % 2

    def spread(ends, base, n):
        at = slice(base * LANE + n * SUB, base * LANE + (n + 1) * SUB)
        part = spread_row(ends[0:1, n * SUB : (n + 1) * SUB] >> 8, ROWS)
        row = (base + n * (SUB // LANE)) * ROWS
        high, low = halves(join([values[row + m * ROWS : row + (m + 1) * ROWS, :] for m in range(SUB // LANE)]))
        for k in range(parts):
            left[k * 2 * ROWS : k * 2 * ROWS + ROWS, at] = masked(part, k, high)
            left[k * 2 * ROWS + ROWS : (k + 1) * 2 * ROWS, at] = masked(part, k, low)

    squares = jnp.zeros((8, LANE), F32)
    for h in range(0, chunks, 8):
        near, far = (
            pull(ends, h, field, parity, state, [pulled[which * state + c, h : h + 8, :] for c in range(state)])
            for which, ends in enumerate((heads_tile, tails_tile))
        )
        back = [None] * state
        for i in range(state):
            row = [blocks[i * state + j, h : h + 8, :] for j in range(state)]
            f = near[i]
            for j in range(state):
                f = f - row[j] * far[j]
            squares = squares + f * f
            values[pl.ds(h * ROWS + i, 8, stride=ROWS), :] = f
            for j in range(state):
                back[j] = row[j] * f if i == 0 else back[j] + row[j] * f
        for j in range(state):
            values[pl.ds((chunks + h) * ROWS + j, 8, stride=ROWS), :] = -back[j]
        for j in range(state, ROWS):
            values[pl.ds(h * ROWS + j, 8, stride=ROWS), :] = jnp.zeros((8, LANE), F32)
            values[pl.ds((chunks + h) * ROWS + j, 8, stride=ROWS), :] = jnp.zeros((8, LANE), F32)
    for n in range(pairs // SUB):
        spread(heads, 0, n)
        spread(tails, chunks, n)
    summed = both(left[...], hot[...], ((1,), (1,)))

    after = jnp.minimum(flat + 1, devices - 1)
    following = row_to_column(other[after // n_clus * half + after % n_clus // 2, state : state + 1, :], state)
    at = slice(width - LANE, width)
    ending = iota((ROWS, LANE), 1) == LANE - 1
    closed = ending & (flat == devices - 1)
    ahead = jnp.where(ending, errors[:, at] + following, errors[:, at])
    last[...] = jnp.where(closed | (iota((ROWS, LANE), 0) >= state), 0.0, ahead)
    energy = last[...] * last[...]
    for start in range(0, width - LANE, LANE):
        block = errors[:, start : start + LANE]
        energy = energy + jnp.where(iota((ROWS, LANE), 0) < state, block * block, 0.0)
    product = total(squares) + total(energy)
    inertial[...] = partial[...]
    back = transition[0, :, at] * last[0:1, :]
    for j in range(1, state):
        back = back + transition[j, :, at] * last[j : j + 1, :]
    inertial[0:state, at] = partial[0:state, at] - back

    sub = iota((ROWS, share), 0)
    damped = jnp.zeros((ROWS, share), F32)
    for k in range(parts):
        one = summed[k * 2 * ROWS : k * 2 * ROWS + ROWS] + summed[k * 2 * ROWS + ROWS : (k + 1) * 2 * ROWS]
        for m in range(per_part):
            piece = k * per_part + m
            c, t = piece // n_time, piece % n_time
            here = jnp.where(clus_at == c, lam[:, t * share : (t + 1) * share], 0.0)
            states = jnp.where(sub < state, got[t * half + c // 2], 0.0)
            extra = here * states
            damped = damped + extra * states
            send[source(piece)] = one[:, m * share : (m + 1) * share] + extra
    product = product + total(damped)
    notes = note(last[:, LANE - 1 : LANE], product, state, share)
    for d in range(devices):
        send[d, state : state + 1, :] = notes[:, :share]


def image_of(n_time, n_clus, axes, got, inertial, slot, image, state):
    width = image.shape[1]
    per = LANE // got.shape[2]
    flat = lax.axis_index(axes[0]) * n_clus + lax.axis_index(axes[1])
    tiles = []
    for r in range(width // LANE):
        pieces = []
        for t in range(r * per, (r + 1) * per):
            one = got[t * n_clus]
            for c in range(1, n_clus):
                one = one + got[t * n_clus + c]
            pieces.append(one)
        tiles.append(join(pieces))
    prior = row_to_column(got[jnp.maximum(flat - 1, 0), state : state + 1, :], state)
    prior = jnp.where(flat == 0, 0.0, prior)
    for start in range(0, width, LANE):
        at = slice(start, start + LANE)
        out = reorder(tiles, slot[0:1, at]) + inertial[:, at]
        if start == 0:
            out = jnp.where(iota((ROWS, LANE), 1) == 0, out + prior, out)
        image[:, at] = out
    return jnp.sum(got[:, state : state + 1, :], axis=0)[:, state : state + 1]


def step_kernel(n_time, n_clus, axes, got, right, inertial, precond, slot, origin, sums,
                send, scaled, residual, image, scalars):
    state, width = right.shape
    product = image_of(n_time, n_clus, axes, got, inertial, slot, image, state)
    alpha = sums[0:1, state : state + 1] / product
    residual[...] = right[...] - alpha * image[0:state, :]
    dot = apply_precond(precond, residual, scaled)
    send_states(scaled, dot, origin, send, state)
    scalars[...] = jnp.broadcast_to(alpha, scalars.shape)


def end_kernel(n_time, n_clus, axes, got, residual, inertial, slot, first, scaled, along, sums, sums_next, scalars,
               solution_field, residual_out, image):
    state, width = residual.shape
    product = image_of(n_time, n_clus, axes, got, inertial, slot, image, state)
    alpha = scalars[0:1, 0:1]
    rz, rz_next = sums[0:1, state : state + 1], sums_next[0:1, state : state + 1]
    ratio = rz_next / rz
    step = rz_next / (product - ratio * rz_next / alpha)
    direction = scaled[0:state, :] + ratio * first[0:state, :]
    solution_field[...] = alpha * first[0:state, :] + step * direction
    residual_out[...] = residual[...] - step * (image[0:state, :] + ratio * along[0:state, :])


def on_device(
    right_side,
    transition,
    precond,
    slot_of,
    cluster_id,
    damping,
    pair_first,
    pair_second,
    pair_blocks,
):
    axes = ("tm", "clus")
    state, width = right_side.shape
    n_time = lax.axis_size("tm")
    n_clus = lax.axis_size("clus")
    devices = n_time * n_clus
    share = width // n_time
    pairs = pair_first.shape[1]
    positions = n_clus * width
    slot = slot_of.reshape(1, width)
    blocks = pair_blocks.reshape(state * state, pairs // LANE, LANE)
    params = pltpu.CompilerParams(vmem_limit_bytes=VMEM_LIMIT)

    def like(*shape):
        return jax.ShapeDtypeStruct(shape, F32)

    message = like(devices, ROWS, share)
    outgoing = like(n_time, n_clus // 2, ROWS, share)
    row = like(1, share)
    tile = like(ROWS, width)
    hot = pltpu.VMEM((SUB, width), BF16)
    left = pltpu.VMEM((ROWS * width // SUB, width), BF16)

    def exchange(sent):
        return lax.all_to_all(sent.reshape(devices, ROWS, share), axes, split_axis=0, concat_axis=0, tiled=True)

    def held(*arrays):
        return tuple(pltpu.with_memory_space_constraint(array, pltpu.HBM) for array in arrays)

    in_hbm = pl.BlockSpec(memory_space=pltpu.HBM)
    in_vmem = pl.BlockSpec(memory_space=pltpu.VMEM)
    dense = (pairs // LANE, LANE)
    small = (pair_first, pair_second, pair_first.reshape(dense), pair_second.reshape(dense), cluster_id, damping)
    same = [[t * n_clus + c for t in range(n_time) for c in range(q, n_clus, 2)] for q in range(2)]
    field = pltpu.VMEM((n_clus // 2, width // LANE, ROWS, LANE), F32)

    def collect(sent):
        sent = sent.reshape(devices // 2, ROWS, share)
        got = lax.all_to_all(sent, axes, split_axis=0, concat_axis=0, tiled=True, axis_index_groups=same)
        return got, lax.ppermute(got, "clus", [(c, c ^ 1) for c in range(n_clus)])

    def grouped(sent, scaled, carried, tables):
        got, other = collect(sent)
        heads, tails, heads_tile, tails_tile, hot_of, lam = carried
        shapes = (like(2 * state, *dense), tile, tile)
        operands = (got, heads_tile, tails_tile, scaled, transition)
        scratch = [field]
        if not tables:
            shapes += (like(*blocks.shape),)
            operands += held(blocks)
            scratch += [pltpu.SemaphoreType.DMA((1,))]
        pulled, errors, partial, *fresh = pl.pallas_call(
            functools.partial(half_kernel, axes, not tables),
            out_shape=shapes,
            in_specs=[in_vmem] * (len(operands) - 1) + [in_vmem if tables else in_hbm],
            scratch_shapes=scratch,
            compiler_params=params,
            name="half",
        )(*operands)
        tables = tables or fresh
        return tables, pl.pallas_call(
            functools.partial(group_kernel, n_time, n_clus, axes),
            out_shape=(message, tile, row),
            scratch_shapes=[
                field,
                pltpu.VMEM((2 * pairs // LANE * ROWS, LANE), F32),
                pltpu.VMEM((2 * ROWS * positions // SUB, 2 * pairs), BF16),
                pltpu.VMEM((ROWS, LANE), F32),
            ],
            compiler_params=params,
            name="group",
        )(got, other, pulled, heads, tails, heads_tile, tails_tile, hot_of, lam, *tables, errors, partial, transition)

    sent, first, origin, *carried = pl.pallas_call(
        begin_kernel,
        out_shape=(
            outgoing,
            tile,
            jax.ShapeDtypeStruct((1, width), jnp.int32),
            *(jax.ShapeDtypeStruct(array.shape, array.dtype) for array in small[:4]),
            jax.ShapeDtypeStruct((SUB, 2 * pairs), BF16),
            like(1, width),
        ),
        in_specs=[in_hbm] * (3 + len(small)),
        scratch_shapes=[
            hot,
            left,
            pltpu.VMEM(right_side.shape, F32),
            pltpu.VMEM(precond.shape, F32),
            pltpu.VMEM(slot.shape, jnp.int32),
            pltpu.VMEM(cluster_id.shape, jnp.int32),
            pltpu.VMEM(damping.shape, F32),
            pltpu.SemaphoreType.DMA((3 + len(small),)),
        ],
        compiler_params=params,
        name="begin",
    )(*held(right_side, precond, slot, *small))
    tables, (back, inertial, sums) = grouped(sent, first, carried, None)
    sent, scaled, residual, along, scalars = pl.pallas_call(
        functools.partial(step_kernel, n_time, n_clus, axes),
        out_shape=(outgoing, tile, like(state, width), tile, like(1, LANE)),
        compiler_params=params,
        name="step",
    )(exchange(back), right_side, inertial, precond, slot, origin, sums)
    _, (back, inertial, sums_next) = grouped(sent, scaled, carried, tables)
    return pl.pallas_call(
        functools.partial(end_kernel, n_time, n_clus, axes),
        out_shape=(like(state, width), like(state, width)),
        scratch_shapes=[pltpu.VMEM((ROWS, width), F32)],
        compiler_params=params,
        name="end",
    )(exchange(back), residual, inertial, slot, first, scaled, along, sums, sums_next, scalars)


def solution(mesh):
    placed = (
        P(None, ("tm", "clus")),
        P(None, None, ("tm", "clus")),
        P(None, None, ("tm", "clus")),
        P(("tm", "clus")),
        P("tm", "clus"),
        P("tm", None),
        P("tm", "clus"),
        P("tm", "clus"),
        P(None, None, "tm", "clus"),
    )
    return jax.shard_map(
        on_device,
        mesh=mesh,
        in_specs=placed,
        out_specs=(P(None, ("tm", "clus")), P(None, ("tm", "clus"))),
        check_vma=False,
    )
```

```python
import functools
import jax
import jax.numpy as jnp
from jax import lax
from jax.experimental import pallas as pl
from jax.experimental.pallas import tpu as pltpu
from jax.sharding import PartitionSpec as P

F32 = jnp.float32
BF16 = jnp.bfloat16
ROWS = 16
SUB = 256
LANE = 128
WIDE = 512
VMEM_LIMIT = 16 * 1024 * 1024


def iota(shape, axis):
    return lax.broadcasted_iota(jnp.int32, shape, axis)


def halves(value):
    high = value.astype(BF16)
    return high, (value - high.astype(F32)).astype(BF16)


def join(pieces):
    return pieces[0] if len(pieces) == 1 else jnp.concatenate(pieces, axis=1)


def spread_rows(numbers):
    return numbers.astype(F32).astype(BF16)


def spread_row(row, count):
    return jnp.broadcast_to(row.astype(F32), (count, row.shape[1])).astype(BF16)


def hot_table(hot, index_ref, width):
    size = hot.shape[0]
    ones, zeros = jnp.ones((), BF16), jnp.zeros((), BF16)
    rows = [spread_rows(iota((ROWS, SUB), 0) + r) for r in range(0, SUB, ROWS)]
    for start in range(0, width, SUB):
        at = slice(start, start + SUB)
        index = index_ref[0:1, at]
        for b in range(size // SUB):
            low = index & (SUB - 1)
            if size > SUB:
                low = jnp.where((index & (size - 1)) >> 8 == b, low, WIDE)
            low = spread_row(low, ROWS)
            for r, row in enumerate(rows):
                hot[b * SUB + r * ROWS : b * SUB + (r + 1) * ROWS, at] = jnp.where(row == low, ones, zeros)


def masked(part, k, value):
    return jnp.where(part == jnp.asarray(k, BF16), value, jnp.zeros((), BF16))


def both(left, right, contract):
    return lax.dot_general(left, right, (contract, ((), ())), preferred_element_type=F32)


def column_to_row(column, state, share):
    spot = iota((ROWS, LANE), 1) % share
    row = iota((ROWS, LANE), 0)
    return jnp.sum(jnp.where((spot == row) & (row < state), column, 0.0), axis=0, keepdims=True)


def row_to_column(row, state):
    width = row.shape[1]
    sub = iota((ROWS, width), 0)
    keep = (sub == iota((ROWS, width), 1)) & (sub < state)
    return jnp.sum(jnp.where(keep, row, 0.0), axis=1, keepdims=True)


def note(column, scalar, state, share):
    spot = iota((1, LANE), 1) % share
    return jnp.where(spot == state, scalar, column_to_row(column, state, share))


def total(value):
    return jnp.sum(jnp.sum(value, axis=0, keepdims=True), axis=1, keepdims=True)


def apply_precond(precond, residual, scaled):
    state, width = residual.shape
    dot = jnp.zeros((state, LANE), F32)
    for start in range(0, width, LANE):
        at = slice(start, start + LANE)
        out = precond[0, :, at] * residual[0:1, at]
        for j in range(1, state):
            out = out + precond[j, :, at] * residual[j : j + 1, at]
        scaled[0:state, at] = out
        scaled[state:ROWS, at] = jnp.zeros((ROWS - state, LANE), F32)
        dot = dot + out * residual[:, at]
    return total(dot)


def reorder(tiles, index):
    low = jnp.broadcast_to(index & (LANE - 1), (ROWS, LANE))
    part = jnp.broadcast_to(index >> 7, (ROWS, LANE))
    out = jnp.zeros((ROWS, LANE), F32)
    for k, one in enumerate(tiles):
        out = jnp.where(part == k, jnp.take_along_axis(one, low, axis=1), out)
    return out


def send_states(scaled, dot, origin, send, state):
    width = scaled.shape[1]
    copies, _, share = send.shape[1:]
    notes = note(scaled[:, 0:1], dot, state, share)
    tiles = [scaled[:, start : start + LANE] for start in range(0, width, LANE)]
    sub = iota((ROWS, share), 0)
    for k in range(width // LANE):
        piece = reorder(tiles, origin[0:1, k * LANE : (k + 1) * LANE])
        for m in range(LANE // share):
            one = jnp.where(sub == state, notes[:, :share], piece[:, m * share : (m + 1) * share])
            for copy in range(copies):
                send[k * (LANE // share) + m, copy] = one


def invert(slot, hot, left, origin):
    width = slot.shape[1]
    hot_table(hot, slot, width)
    sub = iota((ROWS, SUB), 0)
    for start in range(0, width, SUB):
        number = iota((ROWS, SUB), 1) + start
        digits = jnp.where(sub == 0, number >> 5, jnp.where(sub == 1, number & 31, 0)).astype(F32).astype(BF16)
        part = spread_row(slot[0:1, start : start + SUB] >> 8, ROWS)
        for k in range(width // SUB):
            left[k * ROWS : (k + 1) * ROWS, start : start + SUB] = masked(part, k, digits)
    found = both(left[...], hot[...], ((1,), (1,)))
    for k in range(width // SUB):
        row = 32.0 * found[k * ROWS : k * ROWS + 1] + found[k * ROWS + 1 : k * ROWS + 2]
        origin[0:1, k * SUB : (k + 1) * SUB] = row.astype(jnp.int32)


def begin_kernel(right_in, precond_in, slot_in, heads_in, tails_in, heads_tile_in, tails_tile_in, cluster_in, damping_in,
                 send, scaled, origin, heads, tails, heads_tile, tails_tile, hot_pairs, lam,
                 hot, left, right, precond, slot, cluster, damping, sems):
    state = right.shape[0]
    copies = fetch(sems, (precond_in, precond), (heads_in, heads), (tails_in, tails), (slot_in, slot), (right_in, right),
                   (cluster_in, cluster), (damping_in, damping), (heads_tile_in, heads_tile), (tails_tile_in, tails_tile))
    pairs = heads.shape[1]
    copies[3].wait()
    invert(slot, hot, left, origin)
    copies[1].wait()
    hot_table(hot_pairs.at[:, 0:pairs], heads, pairs)
    copies[2].wait()
    hot_table(hot_pairs.at[:, pairs:], tails, pairs)
    copies[5].wait()
    copies[6].wait()
    spare = jnp.zeros((1, LANE - damping.shape[1]), F32)
    row = jnp.broadcast_to(jnp.concatenate([damping[...], spare], axis=1), lam.shape)
    row = jnp.take_along_axis(row, cluster[...], axis=1)
    lam[...] = row
    copies[4].wait()
    copies[0].wait()
    dot = apply_precond(precond, right, scaled)
    send_states(scaled, dot, origin, send, state)
    copies[7].wait()
    copies[8].wait()


def fetch(sems, *pairs):
    copies = [pltpu.make_async_copy(source, place, sems.at[i]) for i, (source, place) in enumerate(pairs)]
    for copy in copies:
        copy.start()
    return copies


def back_product(transition, errors, at):
    back = transition[0, :, at] * errors[0:1, at]
    for j in range(1, transition.shape[0]):
        back = back + transition[j, :, at] * errors[j : j + 1, at]
    return back


def pull(ends, h, field, parity, state, found_before):
    index = ends[h : h + 8, :]
    low, part = index & (LANE - 1), index >> 7
    out = list(found_before)
    half, tiles = field.shape[0], field.shape[1]
    for i in range(half):
        for r in range(tiles):
            here = part == (2 * i + parity) * tiles + r
            for c in range(state):
                from_row = jnp.broadcast_to(field[i, r, c : c + 1, :], (8, LANE))
                out[c] = jnp.where(here, jnp.take_along_axis(from_row, low, axis=1), out[c])
    return out


def fill(field, got):
    half, tiles = field.shape[0], field.shape[1]
    per = LANE // got.shape[2]
    for i in range(half):
        for r in range(tiles):
            field[i, r] = join([got[(r * per + m) * half + i] for m in range(per)])


def row_sums(tiles):
    row = iota((8, LANE), 0)
    for step in (4, 2, 1):
        tiles = [
            jnp.where(row & step == 0, one + pltpu.roll(one, 8 - step, 0), other + pltpu.roll(other, step, 0))
            for one, other in zip(tiles[:step], tiles[step:])
        ]
    return tiles[0]


def half_kernel(axes, once, got, heads_tile, tails_tile, scaled, transition, *refs):
    state = transition.shape[0]
    width = scaled.shape[1]
    chunks = heads_tile.shape[0]
    if once:
        blocks_in, pulled, errors, inertial, blocks, field, sems = refs
        (copy,) = fetch(sems, (blocks_in, blocks))
    else:
        pulled, errors, inertial, field = refs
    fill(field, got)
    parity = lax.axis_index(axes[1]) % 2
    zero = [jnp.zeros((8, LANE), F32)] * state
    for h in range(0, chunks, 8):
        for which, ends in enumerate((heads_tile, tails_tile)):
            for c, value in enumerate(pull(ends, h, field, parity, state, zero)):
                pulled[which * state + c, h : h + 8, :] = value
    lane = iota((ROWS, width), 1)
    ahead = jnp.where(lane == width - 1, 0.0, pltpu.roll(scaled[...], width - 1, 1))
    empty = jnp.zeros((ROWS - state, LANE), F32)
    for start in range(0, width, LANE):
        at = slice(start, start + LANE)
        low, high = scaled[0:8, at], scaled[8:state, at]
        for first in range(0, ROWS, 8):
            moved = [
                transition[i, 0:8, at] * low + jnp.concatenate([transition[i, 8:state, at] * high, empty], axis=0)
                for i in range(first, min(first + 8, state))
            ]
            moved += [jnp.zeros((8, LANE), F32)] * (8 - len(moved))
            errors[first : first + 8, at] = ahead[first : first + 8, at] - row_sums(moved)
    prior = jnp.where(lane == 0, 0.0, pltpu.roll(errors[...], 1, 1))
    inertial[state:ROWS, :] = jnp.zeros((ROWS - state, width), F32)
    for start in range(0, width - LANE, LANE):
        at = slice(start, start + LANE)
        inertial[0:state, at] = prior[0:state, at] - back_product(transition, errors, at)
    inertial[0:state, width - LANE :] = prior[0:state, width - LANE :]
    if once:
        copy.wait()


def group_kernel(n_time, n_clus, axes, got, other, pulled, heads, tails, heads_tile, tails_tile, hot, lam, blocks,
                 errors, partial, transition, send, inertial, sums, field, values, left, last):
    state = transition.shape[0]
    width = errors.shape[1]
    share = got.shape[2]
    pairs = heads.shape[1]
    parts = n_clus * width // WIDE
    per_part = WIDE // share
    chunks = pairs // LANE
    half = n_clus // 2
    time_at, clus_at = lax.axis_index(axes[0]), lax.axis_index(axes[1])
    flat = time_at * n_clus + clus_at
    devices = n_time * n_clus

    def source(piece):
        return (piece % n_time) * n_clus + piece // n_time

    sums[...] = jnp.sum(got[:, state : state + 1, :], axis=0) + jnp.sum(other[:, state : state + 1, :], axis=0)
    fill(field, other)
    parity = 1 - clus_at % 2

    def spread(ends, base, n):
        at = slice(base * LANE + n * SUB, base * LANE + (n + 1) * SUB)
        part = spread_row(ends[0:1, n * SUB : (n + 1) * SUB] >> 9, ROWS)
        row = (base + n * (SUB // LANE)) * ROWS
        high, low = halves(join([values[row + m * ROWS : row + (m + 1) * ROWS, :] for m in range(SUB // LANE)]))
        for k in range(parts):
            left[k * 2 * ROWS : k * 2 * ROWS + ROWS, at] = masked(part, k, high)
            left[k * 2 * ROWS + ROWS : (k + 1) * 2 * ROWS, at] = masked(part, k, low)

    squares = jnp.zeros((8, LANE), F32)
    for h in range(0, chunks, 8):
        near, far = (
            pull(ends, h, field, parity, state, [pulled[which * state + c, h : h + 8, :] for c in range(state)])
            for which, ends in enumerate((heads_tile, tails_tile))
        )
        back = [None] * state
        for i in range(state):
            row = [blocks[i * state + j, h : h + 8, :] for j in range(state)]
            f = near[i]
            for j in range(state):
                f = f - row[j] * far[j]
            squares = squares + f * f
            values[pl.ds(h * ROWS + i, 8, stride=ROWS), :] = f
            for j in range(state):
                back[j] = row[j] * f if i == 0 else back[j] + row[j] * f
        for j in range(state):
            values[pl.ds((chunks + h) * ROWS + j, 8, stride=ROWS), :] = -back[j]
        for j in range(state, ROWS):
            values[pl.ds(h * ROWS + j, 8, stride=ROWS), :] = jnp.zeros((8, LANE), F32)
            values[pl.ds((chunks + h) * ROWS + j, 8, stride=ROWS), :] = jnp.zeros((8, LANE), F32)
    for n in range(pairs // SUB):
        spread(heads, 0, n)
        spread(tails, chunks, n)
    summed = both(left[...], hot[...], ((1,), (1,)))

    after = jnp.minimum(flat + 1, devices - 1)
    following = row_to_column(other[after // n_clus * half + after % n_clus // 2, state : state + 1, :], state)
    at = slice(width - LANE, width)
    ending = iota((ROWS, LANE), 1) == LANE - 1
    closed = ending & (flat == devices - 1)
    ahead = jnp.where(ending, errors[:, at] + following, errors[:, at])
    last[...] = jnp.where(closed | (iota((ROWS, LANE), 0) >= state), 0.0, ahead)
    energy = last[...] * last[...]
    for start in range(0, width - LANE, LANE):
        block = errors[:, start : start + LANE]
        energy = energy + jnp.where(iota((ROWS, LANE), 0) < state, block * block, 0.0)
    product = total(squares) + total(energy)
    inertial[...] = partial[...]
    back = transition[0, :, at] * last[0:1, :]
    for j in range(1, state):
        back = back + transition[j, :, at] * last[j : j + 1, :]
    inertial[0:state, at] = partial[0:state, at] - back

    sub = iota((ROWS, share), 0)
    damped = jnp.zeros((ROWS, share), F32)
    for k in range(parts):
        one = summed[k * 2 * ROWS : k * 2 * ROWS + ROWS] + summed[k * 2 * ROWS + ROWS : (k + 1) * 2 * ROWS]
        for m in range(per_part):
            piece = k * per_part + m
            c, t = piece // n_time, piece % n_time
            r, l = t * share // LANE, t * share % LANE
            here = jnp.where(clus_at == c, lam[r : r + 1, l : l + share], 0.0)
            states = jnp.where(sub < state, got[t * half + c // 2], 0.0)
            extra = here * states
            damped = damped + extra * states
            send[source(piece)] = one[:, m * share : (m + 1) * share] + extra
    product = product + total(damped)
    notes = note(last[:, LANE - 1 : LANE], product, state, share)
    for d in range(devices):
        send[d, state : state + 1, :] = notes[:, :share]


def image_of(n_time, n_clus, axes, got, inertial, slot, image, state):
    width = image.shape[1]
    per = LANE // got.shape[2]
    flat = lax.axis_index(axes[0]) * n_clus + lax.axis_index(axes[1])
    tiles = []
    for r in range(width // LANE):
        pieces = []
        for t in range(r * per, (r + 1) * per):
            one = got[t * n_clus]
            for c in range(1, n_clus):
                one = one + got[t * n_clus + c]
            pieces.append(one)
        tiles.append(join(pieces))
    prior = row_to_column(got[jnp.maximum(flat - 1, 0), state : state + 1, :], state)
    prior = jnp.where(flat == 0, 0.0, prior)
    for start in range(0, width, LANE):
        at = slice(start, start + LANE)
        out = reorder(tiles, slot[0:1, at]) + inertial[:, at]
        if start == 0:
            out = jnp.where(iota((ROWS, LANE), 1) == 0, out + prior, out)
        image[:, at] = out
    return jnp.sum(got[:, state : state + 1, :], axis=0)[:, state : state + 1]


def step_kernel(n_time, n_clus, axes, got, right, inertial, precond, slot, origin, sums,
                send, scaled, residual, image, scalars):
    state, width = right.shape
    product = image_of(n_time, n_clus, axes, got, inertial, slot, image, state)
    alpha = sums[0:1, state : state + 1] / product
    residual[...] = right[...] - alpha * image[0:state, :]
    dot = apply_precond(precond, residual, scaled)
    send_states(scaled, dot, origin, send, state)
    scalars[...] = jnp.broadcast_to(alpha, scalars.shape)


def end_kernel(n_time, n_clus, axes, got, residual, inertial, slot, first, scaled, along, sums, sums_next, scalars,
               solution_field, residual_out, image):
    state, width = residual.shape
    product = image_of(n_time, n_clus, axes, got, inertial, slot, image, state)
    alpha = scalars[0:1, 0:1]
    rz, rz_next = sums[0:1, state : state + 1], sums_next[0:1, state : state + 1]
    ratio = rz_next / rz
    step = rz_next / (product - ratio * rz_next / alpha)
    direction = scaled[0:state, :] + ratio * first[0:state, :]
    solution_field[...] = alpha * first[0:state, :] + step * direction
    residual_out[...] = residual[...] - step * (image[0:state, :] + ratio * along[0:state, :])


def on_device(
    right_side,
    transition,
    precond,
    slot_of,
    cluster_id,
    damping,
    pair_first,
    pair_second,
    pair_blocks,
):
    axes = ("tm", "clus")
    state, width = right_side.shape
    n_time = lax.axis_size("tm")
    n_clus = lax.axis_size("clus")
    devices = n_time * n_clus
    share = width // n_time
    pairs = pair_first.shape[1]
    positions = n_clus * width
    slot = slot_of.reshape(1, width)
    blocks = pair_blocks.reshape(state * state, pairs // LANE, LANE)
    params = pltpu.CompilerParams(vmem_limit_bytes=VMEM_LIMIT)

    def like(*shape):
        return jax.ShapeDtypeStruct(shape, F32)

    message = like(devices, ROWS, share)
    outgoing = like(n_time, n_clus // 2, ROWS, share)
    row = like(1, share)
    tile = like(ROWS, width)
    hot = pltpu.VMEM((SUB, width), BF16)
    left = pltpu.VMEM((ROWS * width // SUB, width), BF16)

    def exchange(sent):
        return lax.all_to_all(sent.reshape(devices, ROWS, share), axes, split_axis=0, concat_axis=0, tiled=True)

    def held(*arrays):
        return tuple(pltpu.with_memory_space_constraint(array, pltpu.HBM) for array in arrays)

    in_hbm = pl.BlockSpec(memory_space=pltpu.HBM)
    in_vmem = pl.BlockSpec(memory_space=pltpu.VMEM)
    dense = (pairs // LANE, LANE)
    small = (pair_first, pair_second, pair_first.reshape(dense), pair_second.reshape(dense),
             cluster_id.reshape(width // LANE, LANE), damping)
    same = [[t * n_clus + c for t in range(n_time) for c in range(q, n_clus, 2)] for q in range(2)]
    field = pltpu.VMEM((n_clus // 2, width // LANE, ROWS, LANE), F32)

    def collect(sent):
        sent = sent.reshape(devices // 2, ROWS, share)
        got = lax.all_to_all(sent, axes, split_axis=0, concat_axis=0, tiled=True, axis_index_groups=same)
        return got, lax.ppermute(got, "clus", [(c, c ^ 1) for c in range(n_clus)])

    def grouped(sent, scaled, carried, tables):
        got, other = collect(sent)
        heads, tails, heads_tile, tails_tile, hot_of, lam = carried
        shapes = (like(2 * state, *dense), tile, tile)
        operands = (got, heads_tile, tails_tile, scaled, transition)
        scratch = [field]
        if not tables:
            shapes += (like(*blocks.shape),)
            operands += held(blocks)
            scratch += [pltpu.SemaphoreType.DMA((1,))]
        pulled, errors, partial, *fresh = pl.pallas_call(
            functools.partial(half_kernel, axes, not tables),
            out_shape=shapes,
            in_specs=[in_vmem] * (len(operands) - 1) + [in_vmem if tables else in_hbm],
            scratch_shapes=scratch,
            compiler_params=params,
            name="half",
        )(*operands)
        tables = tables or fresh
        return tables, pl.pallas_call(
            functools.partial(group_kernel, n_time, n_clus, axes),
            out_shape=(message, tile, row),
            scratch_shapes=[
                field,
                pltpu.VMEM((2 * pairs // LANE * ROWS, LANE), F32),
                pltpu.VMEM((2 * ROWS * positions // WIDE, 2 * pairs), BF16),
                pltpu.VMEM((ROWS, LANE), F32),
            ],
            compiler_params=params,
            name="group",
        )(got, other, pulled, heads, tails, heads_tile, tails_tile, hot_of, lam, *tables, errors, partial, transition)

    sent, first, origin, *carried = pl.pallas_call(
        begin_kernel,
        out_shape=(
            outgoing,
            tile,
            jax.ShapeDtypeStruct((1, width), jnp.int32),
            *(jax.ShapeDtypeStruct(array.shape, array.dtype) for array in small[:4]),
            jax.ShapeDtypeStruct((WIDE, 2 * pairs), BF16),
            like(width // LANE, LANE),
        ),
        in_specs=[in_hbm] * (3 + len(small)),
        scratch_shapes=[
            hot,
            left,
            pltpu.VMEM(right_side.shape, F32),
            pltpu.VMEM(precond.shape, F32),
            pltpu.VMEM(slot.shape, jnp.int32),
            pltpu.VMEM((width // LANE, LANE), jnp.int32),
            pltpu.VMEM(damping.shape, F32),
            pltpu.SemaphoreType.DMA((3 + len(small),)),
        ],
        compiler_params=params,
        name="begin",
    )(*held(right_side, precond, slot, *small))
    tables, (back, inertial, sums) = grouped(sent, first, carried, None)
    sent, scaled, residual, along, scalars = pl.pallas_call(
        functools.partial(step_kernel, n_time, n_clus, axes),
        out_shape=(outgoing, tile, like(state, width), tile, like(1, LANE)),
        compiler_params=params,
        name="step",
    )(exchange(back), right_side, inertial, precond, slot, origin, sums)
    _, (back, inertial, sums_next) = grouped(sent, scaled, carried, tables)
    return pl.pallas_call(
        functools.partial(end_kernel, n_time, n_clus, axes),
        out_shape=(like(state, width), like(state, width)),
        scratch_shapes=[pltpu.VMEM((ROWS, width), F32)],
        compiler_params=params,
        name="end",
    )(exchange(back), residual, inertial, slot, first, scaled, along, sums, sums_next, scalars)


def solution(mesh):
    placed = (
        P(None, ("tm", "clus")),
        P(None, None, ("tm", "clus")),
        P(None, None, ("tm", "clus")),
        P(("tm", "clus")),
        P("tm", "clus"),
        P("tm", None),
        P("tm", "clus"),
        P("tm", "clus"),
        P(None, None, "tm", "clus"),
    )
    return jax.shard_map(
        on_device,
        mesh=mesh,
        in_specs=placed,
        out_specs=(P(None, ("tm", "clus")), P(None, ("tm", "clus"))),
        check_vma=False,
    )
```

```python
import functools
import jax
import jax.numpy as jnp
from jax import lax
from jax.experimental import pallas as pl
from jax.experimental.pallas import tpu as pltpu
from jax.sharding import PartitionSpec as P

F32 = jnp.float32
BF16 = jnp.bfloat16
ROWS = 16
SUB = 256
LANE = 128
VMEM_LIMIT = 16 * 1024 * 1024


def iota(shape, axis):
    return lax.broadcasted_iota(jnp.int32, shape, axis)


def halves(value):
    high = value.astype(BF16)
    return high, (value - high.astype(F32)).astype(BF16)


def join(pieces):
    return pieces[0] if len(pieces) == 1 else jnp.concatenate(pieces, axis=1)


def spread_rows(numbers):
    return numbers.astype(F32).astype(BF16)


def spread_row(row, count):
    return jnp.broadcast_to(row.astype(F32), (count, row.shape[1])).astype(BF16)


def hot_table(hot, index_ref, width):
    ones, zeros = jnp.ones((), BF16), jnp.zeros((), BF16)
    rows = [spread_rows(iota((ROWS, SUB), 0) + r) for r in range(0, SUB, ROWS)]
    for start in range(0, width, SUB):
        at = slice(start, start + SUB)
        low = spread_row(index_ref[0:1, at] & (SUB - 1), ROWS)
        for r, row in enumerate(rows):
            hot[r * ROWS : (r + 1) * ROWS, at] = jnp.where(row == low, ones, zeros)


def masked(part, k, value):
    return jnp.where(part == jnp.asarray(k, BF16), value, jnp.zeros((), BF16))


def both(left, right, contract):
    return lax.dot_general(left, right, (contract, ((), ())), preferred_element_type=F32)


def column_to_row(column, state, share):
    spot = iota((ROWS, LANE), 1) % share
    row = iota((ROWS, LANE), 0)
    return jnp.sum(jnp.where((spot == row) & (row < state), column, 0.0), axis=0, keepdims=True)


def row_to_column(row, state):
    width = row.shape[1]
    sub = iota((ROWS, width), 0)
    keep = (sub == iota((ROWS, width), 1)) & (sub < state)
    return jnp.sum(jnp.where(keep, row, 0.0), axis=1, keepdims=True)


def note(column, scalar, state, share):
    spot = iota((1, LANE), 1) % share
    return jnp.where(spot == state, scalar, column_to_row(column, state, share))


def total(value):
    return jnp.sum(jnp.sum(value, axis=0, keepdims=True), axis=1, keepdims=True)


def apply_precond(precond, residual, scaled):
    state, width = residual.shape
    dot = jnp.zeros((state, LANE), F32)
    for start in range(0, width, LANE):
        at = slice(start, start + LANE)
        out = precond[0, :, at] * residual[0:1, at]
        for j in range(1, state):
            out = out + precond[j, :, at] * residual[j : j + 1, at]
        scaled[0:state, at] = out
        scaled[state:ROWS, at] = jnp.zeros((ROWS - state, LANE), F32)
        dot = dot + out * residual[:, at]
    return total(dot)


def reorder(tiles, index):
    low = jnp.broadcast_to(index & (LANE - 1), (ROWS, LANE))
    part = jnp.broadcast_to(index >> 7, (ROWS, LANE))
    out = jnp.zeros((ROWS, LANE), F32)
    for k, one in enumerate(tiles):
        out = jnp.where(part == k, jnp.take_along_axis(one, low, axis=1), out)
    return out


def send_states(scaled, dot, origin, send, state):
    width = scaled.shape[1]
    copies, _, share = send.shape[1:]
    notes = note(scaled[:, 0:1], dot, state, share)
    tiles = [scaled[:, start : start + LANE] for start in range(0, width, LANE)]
    sub = iota((ROWS, share), 0)
    for k in range(width // LANE):
        piece = reorder(tiles, origin[0:1, k * LANE : (k + 1) * LANE])
        for m in range(LANE // share):
            one = jnp.where(sub == state, notes[:, :share], piece[:, m * share : (m + 1) * share])
            for copy in range(copies):
                send[k * (LANE // share) + m, copy] = one


def invert(slot, hot, left, origin):
    width = slot.shape[1]
    hot_table(hot, slot, width)
    sub = iota((ROWS, SUB), 0)
    for start in range(0, width, SUB):
        number = iota((ROWS, SUB), 1) + start
        digits = jnp.where(sub == 0, number >> 5, jnp.where(sub == 1, number & 31, 0)).astype(F32).astype(BF16)
        part = spread_row(slot[0:1, start : start + SUB] >> 8, ROWS)
        for k in range(width // SUB):
            left[k * ROWS : (k + 1) * ROWS, start : start + SUB] = masked(part, k, digits)
    found = both(left[...], hot[...], ((1,), (1,)))
    for k in range(width // SUB):
        row = 32.0 * found[k * ROWS : k * ROWS + 1] + found[k * ROWS + 1 : k * ROWS + 2]
        origin[0:1, k * SUB : (k + 1) * SUB] = row.astype(jnp.int32)


def begin_kernel(right_in, precond_in, slot_in, heads_in, tails_in, heads_tile_in, tails_tile_in, cluster_in, damping_in,
                 send, scaled, origin, heads, tails, heads_tile, tails_tile, cluster, damping,
                 hot, left, right, precond, slot, sems):
    state = right.shape[0]
    copies = fetch(sems, (precond_in, precond), (heads_in, heads), (tails_in, tails), (slot_in, slot), (right_in, right),
                   (cluster_in, cluster), (damping_in, damping), (heads_tile_in, heads_tile), (tails_tile_in, tails_tile))
    copies[3].wait()
    invert(slot, hot, left, origin)
    copies[4].wait()
    copies[0].wait()
    dot = apply_precond(precond, right, scaled)
    send_states(scaled, dot, origin, send, state)
    for copy in copies[1:3] + copies[5:]:
        copy.wait()


def fetch(sems, *pairs):
    copies = [pltpu.make_async_copy(source, place, sems.at[i]) for i, (source, place) in enumerate(pairs)]
    for copy in copies:
        copy.start()
    return copies


def back_product(transition, errors, at):
    back = transition[0, :, at] * errors[0:1, at]
    for j in range(1, transition.shape[0]):
        back = back + transition[j, :, at] * errors[j : j + 1, at]
    return back


def pull(ends, h, field, parity, state, found_before):
    index = ends[h : h + 8, :]
    low, part = index & (LANE - 1), index >> 7
    out = list(found_before)
    half, tiles = field.shape[0], field.shape[1]
    for i in range(half):
        for r in range(tiles):
            here = part == (2 * i + parity) * tiles + r
            for c in range(state):
                from_row = jnp.broadcast_to(field[i, r, c : c + 1, :], (8, LANE))
                out[c] = jnp.where(here, jnp.take_along_axis(from_row, low, axis=1), out[c])
    return out


def fill(field, got):
    half, tiles = field.shape[0], field.shape[1]
    per = LANE // got.shape[2]
    for i in range(half):
        for r in range(tiles):
            field[i, r] = join([got[(r * per + m) * half + i] for m in range(per)])


def row_sums(tiles):
    row = iota((8, LANE), 0)
    for step in (4, 2, 1):
        tiles = [
            jnp.where(row & step == 0, one + pltpu.roll(one, 8 - step, 0), other + pltpu.roll(other, step, 0))
            for one, other in zip(tiles[:step], tiles[step:])
        ]
    return tiles[0]


def half_kernel(axes, once, got, heads_tile, tails_tile, scaled, transition, *refs):
    state = transition.shape[0]
    width = scaled.shape[1]
    chunks = heads_tile.shape[0]
    if once:
        heads, tails, cluster, damping, blocks_in, pulled, errors, inertial, hot, lam, blocks, field, sems = refs
        (copy,) = fetch(sems, (blocks_in, blocks))
        pairs = heads.shape[1]
        hot_table(hot.at[:, 0:pairs], heads, pairs)
        hot_table(hot.at[:, pairs:], tails, pairs)
        spare = jnp.zeros((1, LANE - damping.shape[1]), F32)
        row = jnp.broadcast_to(jnp.concatenate([damping[...], spare], axis=1), lam.shape)
        lam[...] = jnp.take_along_axis(row, cluster[...], axis=1)
    else:
        pulled, errors, inertial, field = refs
    fill(field, got)
    parity = lax.axis_index(axes[1]) % 2
    zero = [jnp.zeros((8, LANE), F32)] * state
    for h in range(0, chunks, 8):
        for which, ends in enumerate((heads_tile, tails_tile)):
            for c, value in enumerate(pull(ends, h, field, parity, state, zero)):
                pulled[which * state + c, h : h + 8, :] = value
    lane = iota((ROWS, width), 1)
    ahead = jnp.where(lane == width - 1, 0.0, pltpu.roll(scaled[...], width - 1, 1))
    empty = jnp.zeros((ROWS - state, LANE), F32)
    for start in range(0, width, LANE):
        at = slice(start, start + LANE)
        low, high = scaled[0:8, at], scaled[8:state, at]
        for first in range(0, ROWS, 8):
            moved = [
                transition[i, 0:8, at] * low + jnp.concatenate([transition[i, 8:state, at] * high, empty], axis=0)
                for i in range(first, min(first + 8, state))
            ]
            moved += [jnp.zeros((8, LANE), F32)] * (8 - len(moved))
            errors[first : first + 8, at] = ahead[first : first + 8, at] - row_sums(moved)
    prior = jnp.where(lane == 0, 0.0, pltpu.roll(errors[...], 1, 1))
    inertial[state:ROWS, :] = jnp.zeros((ROWS - state, width), F32)
    for start in range(0, width - LANE, LANE):
        at = slice(start, start + LANE)
        inertial[0:state, at] = prior[0:state, at] - back_product(transition, errors, at)
    inertial[0:state, width - LANE :] = prior[0:state, width - LANE :]
    if once:
        copy.wait()


def group_kernel(n_time, n_clus, axes, got, other, pulled, heads, tails, heads_tile, tails_tile, hot, lam, blocks,
                 errors, partial, transition, send, inertial, sums, field, values, left, last):
    state = transition.shape[0]
    width = errors.shape[1]
    share = got.shape[2]
    pairs = heads.shape[1]
    parts = n_clus * width // SUB
    per_part = SUB // share
    chunks = pairs // LANE
    half = n_clus // 2
    time_at, clus_at = lax.axis_index(axes[0]), lax.axis_index(axes[1])
    flat = time_at * n_clus + clus_at
    devices = n_time * n_clus

    def source(piece):
        return (piece % n_time) * n_clus + piece // n_time

    sums[...] = jnp.sum(got[:, state : state + 1, :], axis=0) + jnp.sum(other[:, state : state + 1, :], axis=0)
    fill(field, other)
    parity = 1 - clus_at % 2

    def spread(ends, base, n):
        at = slice(base * LANE + n * SUB, base * LANE + (n + 1) * SUB)
        part = spread_row(ends[0:1, n * SUB : (n + 1) * SUB] >> 8, ROWS)
        row = (base + n * (SUB // LANE)) * ROWS
        high, low = halves(join([values[row + m * ROWS : row + (m + 1) * ROWS, :] for m in range(SUB // LANE)]))
        for k in range(parts):
            left[k * 2 * ROWS : k * 2 * ROWS + ROWS, at] = masked(part, k, high)
            left[k * 2 * ROWS + ROWS : (k + 1) * 2 * ROWS, at] = masked(part, k, low)

    squares = jnp.zeros((8, LANE), F32)
    for h in range(0, chunks, 8):
        near, far = (
            pull(ends, h, field, parity, state, [pulled[which * state + c, h : h + 8, :] for c in range(state)])
            for which, ends in enumerate((heads_tile, tails_tile))
        )
        back = [None] * state
        for i in range(state):
            row = [blocks[i * state + j, h : h + 8, :] for j in range(state)]
            f = near[i]
            for j in range(state):
                f = f - row[j] * far[j]
            squares = squares + f * f
            values[pl.ds(h * ROWS + i, 8, stride=ROWS), :] = f
            for j in range(state):
                back[j] = row[j] * f if i == 0 else back[j] + row[j] * f
        for j in range(state):
            values[pl.ds((chunks + h) * ROWS + j, 8, stride=ROWS), :] = -back[j]
        for j in range(state, ROWS):
            values[pl.ds(h * ROWS + j, 8, stride=ROWS), :] = jnp.zeros((8, LANE), F32)
            values[pl.ds((chunks + h) * ROWS + j, 8, stride=ROWS), :] = jnp.zeros((8, LANE), F32)
    for n in range(pairs // SUB):
        spread(heads, 0, n)
        spread(tails, chunks, n)
    summed = both(left[...], hot[...], ((1,), (1,)))

    after = jnp.minimum(flat + 1, devices - 1)
    following = row_to_column(other[after // n_clus * half + after % n_clus // 2, state : state + 1, :], state)
    at = slice(width - LANE, width)
    ending = iota((ROWS, LANE), 1) == LANE - 1
    closed = ending & (flat == devices - 1)
    ahead = jnp.where(ending, errors[:, at] + following, errors[:, at])
    last[...] = jnp.where(closed | (iota((ROWS, LANE), 0) >= state), 0.0, ahead)
    energy = last[...] * last[...]
    for start in range(0, width - LANE, LANE):
        block = errors[:, start : start + LANE]
        energy = energy + jnp.where(iota((ROWS, LANE), 0) < state, block * block, 0.0)
    product = total(squares) + total(energy)
    inertial[...] = partial[...]
    back = transition[0, :, at] * last[0:1, :]
    for j in range(1, state):
        back = back + transition[j, :, at] * last[j : j + 1, :]
    inertial[0:state, at] = partial[0:state, at] - back

    sub = iota((ROWS, share), 0)
    damped = jnp.zeros((ROWS, share), F32)
    for k in range(parts):
        one = summed[k * 2 * ROWS : k * 2 * ROWS + ROWS] + summed[k * 2 * ROWS + ROWS : (k + 1) * 2 * ROWS]
        for m in range(per_part):
            piece = k * per_part + m
            c, t = piece // n_time, piece % n_time
            r, l = t * share // LANE, t * share % LANE
            here = jnp.where(clus_at == c, lam[r : r + 1, l : l + share], 0.0)
            states = jnp.where(sub < state, got[t * half + c // 2], 0.0)
            extra = here * states
            damped = damped + extra * states
            send[source(piece)] = one[:, m * share : (m + 1) * share] + extra
    product = product + total(damped)
    notes = note(last[:, LANE - 1 : LANE], product, state, share)
    for d in range(devices):
        send[d, state : state + 1, :] = notes[:, :share]


def image_of(n_time, n_clus, axes, got, inertial, slot, image, state):
    width = image.shape[1]
    per = LANE // got.shape[2]
    flat = lax.axis_index(axes[0]) * n_clus + lax.axis_index(axes[1])
    tiles = []
    for r in range(width // LANE):
        pieces = []
        for t in range(r * per, (r + 1) * per):
            one = got[t * n_clus]
            for c in range(1, n_clus):
                one = one + got[t * n_clus + c]
            pieces.append(one)
        tiles.append(join(pieces))
    prior = row_to_column(got[jnp.maximum(flat - 1, 0), state : state + 1, :], state)
    prior = jnp.where(flat == 0, 0.0, prior)
    for start in range(0, width, LANE):
        at = slice(start, start + LANE)
        out = reorder(tiles, slot[0:1, at]) + inertial[:, at]
        if start == 0:
            out = jnp.where(iota((ROWS, LANE), 1) == 0, out + prior, out)
        image[:, at] = out
    return jnp.sum(got[:, state : state + 1, :], axis=0)[:, state : state + 1]


def step_kernel(n_time, n_clus, axes, got, right, inertial, precond, slot, origin, sums,
                send, scaled, residual, image, scalars):
    state, width = right.shape
    product = image_of(n_time, n_clus, axes, got, inertial, slot, image, state)
    alpha = sums[0:1, state : state + 1] / product
    residual[...] = right[...] - alpha * image[0:state, :]
    dot = apply_precond(precond, residual, scaled)
    send_states(scaled, dot, origin, send, state)
    scalars[...] = jnp.broadcast_to(alpha, scalars.shape)


def end_kernel(n_time, n_clus, axes, got, residual, inertial, slot, first, scaled, along, sums, sums_next, scalars,
               solution_field, residual_out, image):
    state, width = residual.shape
    product = image_of(n_time, n_clus, axes, got, inertial, slot, image, state)
    alpha = scalars[0:1, 0:1]
    rz, rz_next = sums[0:1, state : state + 1], sums_next[0:1, state : state + 1]
    ratio = rz_next / rz
    step = rz_next / (product - ratio * rz_next / alpha)
    direction = scaled[0:state, :] + ratio * first[0:state, :]
    solution_field[...] = alpha * first[0:state, :] + step * direction
    residual_out[...] = residual[...] - step * (image[0:state, :] + ratio * along[0:state, :])


def on_device(
    right_side,
    transition,
    precond,
    slot_of,
    cluster_id,
    damping,
    pair_first,
    pair_second,
    pair_blocks,
):
    axes = ("tm", "clus")
    state, width = right_side.shape
    n_time = lax.axis_size("tm")
    n_clus = lax.axis_size("clus")
    devices = n_time * n_clus
    share = width // n_time
    pairs = pair_first.shape[1]
    positions = n_clus * width
    slot = slot_of.reshape(1, width)
    blocks = pair_blocks.reshape(state * state, pairs // LANE, LANE)
    params = pltpu.CompilerParams(vmem_limit_bytes=VMEM_LIMIT)

    def like(*shape):
        return jax.ShapeDtypeStruct(shape, F32)

    message = like(devices, ROWS, share)
    outgoing = like(n_time, n_clus // 2, ROWS, share)
    row = like(1, share)
    tile = like(ROWS, width)
    hot = pltpu.VMEM((SUB, width), BF16)
    left = pltpu.VMEM((ROWS * width // SUB, width), BF16)

    def exchange(sent):
        return lax.all_to_all(sent.reshape(devices, ROWS, share), axes, split_axis=0, concat_axis=0, tiled=True)

    def held(*arrays):
        return tuple(pltpu.with_memory_space_constraint(array, pltpu.HBM) for array in arrays)

    in_hbm = pl.BlockSpec(memory_space=pltpu.HBM)
    in_vmem = pl.BlockSpec(memory_space=pltpu.VMEM)
    dense = (pairs // LANE, LANE)
    small = (pair_first, pair_second, pair_first.reshape(dense), pair_second.reshape(dense),
             cluster_id.reshape(width // LANE, LANE), damping)
    same = [[t * n_clus + c for t in range(n_time) for c in range(q, n_clus, 2)] for q in range(2)]
    field = pltpu.VMEM((n_clus // 2, width // LANE, ROWS, LANE), F32)

    def collect(sent):
        sent = sent.reshape(devices // 2, ROWS, share)
        got = lax.all_to_all(sent, axes, split_axis=0, concat_axis=0, tiled=True, axis_index_groups=same)
        return got, lax.ppermute(got, "clus", [(c, c ^ 1) for c in range(n_clus)])

    def grouped(sent, scaled, carried, tables):
        got, other = collect(sent)
        heads, tails, heads_tile, tails_tile, cluster, damping_of = carried
        shapes = (like(2 * state, *dense), tile, tile)
        operands = (got, heads_tile, tails_tile, scaled, transition)
        scratch = [field]
        if not tables:
            shapes += (jax.ShapeDtypeStruct((SUB, 2 * pairs), BF16), like(width // LANE, LANE), like(*blocks.shape))
            operands += (heads, tails, cluster, damping_of, *held(blocks))
            scratch += [pltpu.SemaphoreType.DMA((1,))]
        pulled, errors, partial, *fresh = pl.pallas_call(
            functools.partial(half_kernel, axes, not tables),
            out_shape=shapes,
            in_specs=[in_vmem] * (len(operands) - 1) + [in_vmem if tables else in_hbm],
            scratch_shapes=scratch,
            compiler_params=params,
            name="half",
        )(*operands)
        tables = tables or fresh
        return tables, pl.pallas_call(
            functools.partial(group_kernel, n_time, n_clus, axes),
            out_shape=(message, tile, row),
            scratch_shapes=[
                field,
                pltpu.VMEM((2 * pairs // LANE * ROWS, LANE), F32),
                pltpu.VMEM((2 * ROWS * positions // SUB, 2 * pairs), BF16),
                pltpu.VMEM((ROWS, LANE), F32),
            ],
            compiler_params=params,
            name="group",
        )(got, other, pulled, heads, tails, heads_tile, tails_tile, *tables, errors, partial, transition)

    sent, first, origin, *carried = pl.pallas_call(
        begin_kernel,
        out_shape=(
            outgoing,
            tile,
            jax.ShapeDtypeStruct((1, width), jnp.int32),
            *(jax.ShapeDtypeStruct(array.shape, array.dtype) for array in small),
        ),
        in_specs=[in_hbm] * (3 + len(small)),
        scratch_shapes=[
            hot,
            left,
            pltpu.VMEM(right_side.shape, F32),
            pltpu.VMEM(precond.shape, F32),
            pltpu.VMEM(slot.shape, jnp.int32),
            pltpu.SemaphoreType.DMA((3 + len(small),)),
        ],
        compiler_params=params,
        name="begin",
    )(*held(right_side, precond, slot, *small))
    tables, (back, inertial, sums) = grouped(sent, first, carried, None)
    sent, scaled, residual, along, scalars = pl.pallas_call(
        functools.partial(step_kernel, n_time, n_clus, axes),
        out_shape=(outgoing, tile, like(state, width), tile, like(1, LANE)),
        compiler_params=params,
        name="step",
    )(exchange(back), right_side, inertial, precond, slot, origin, sums)
    _, (back, inertial, sums_next) = grouped(sent, scaled, carried, tables)
    return pl.pallas_call(
        functools.partial(end_kernel, n_time, n_clus, axes),
        out_shape=(like(state, width), like(state, width)),
        scratch_shapes=[pltpu.VMEM((ROWS, width), F32)],
        compiler_params=params,
        name="end",
    )(exchange(back), residual, inertial, slot, first, scaled, along, sums, sums_next, scalars)


def solution(mesh):
    placed = (
        P(None, ("tm", "clus")),
        P(None, None, ("tm", "clus")),
        P(None, None, ("tm", "clus")),
        P(("tm", "clus")),
        P("tm", "clus"),
        P("tm", None),
        P("tm", "clus"),
        P("tm", "clus"),
        P(None, None, "tm", "clus"),
    )
    return jax.shard_map(
        on_device,
        mesh=mesh,
        in_specs=placed,
        out_specs=(P(None, ("tm", "clus")), P(None, ("tm", "clus"))),
        check_vma=False,
    )
```

```python
import functools
import jax
import jax.numpy as jnp
from jax import lax
from jax.experimental import pallas as pl
from jax.experimental.pallas import tpu as pltpu
from jax.sharding import PartitionSpec as P

F32 = jnp.float32
BF16 = jnp.bfloat16
ROWS = 16
SUB = 256
LANE = 128
VMEM_LIMIT = 16 * 1024 * 1024


def iota(shape, axis):
    return lax.broadcasted_iota(jnp.int32, shape, axis)


def halves(value):
    high = value.astype(BF16)
    return high, (value - high.astype(F32)).astype(BF16)


def join(pieces):
    return pieces[0] if len(pieces) == 1 else jnp.concatenate(pieces, axis=1)


def spread_rows(numbers):
    return numbers.astype(F32).astype(BF16)


def spread_row(row, count):
    return jnp.broadcast_to(row.astype(F32), (count, row.shape[1])).astype(BF16)


def hot_table(hot, index_ref, width):
    rows = [spread_rows(iota((ROWS, SUB), 0) + r) for r in range(0, SUB, ROWS)]
    for start in range(0, width, SUB):
        at = slice(start, start + SUB)
        low = spread_row(index_ref[0:1, at] & (SUB - 1), ROWS)
        for r, row in enumerate(rows):
            hot[r * ROWS : (r + 1) * ROWS, at] = equal(row, low)


def equal(one, other):
    return jnp.maximum(jnp.asarray(1, BF16) - jnp.abs(one - other), jnp.asarray(0, BF16))


def both(left, right, contract):
    return lax.dot_general(left, right, (contract, ((), ())), preferred_element_type=F32)


def column_to_row(column, state, share):
    spot = iota((ROWS, LANE), 1) % share
    row = iota((ROWS, LANE), 0)
    return jnp.sum(jnp.where((spot == row) & (row < state), column, 0.0), axis=0, keepdims=True)


def row_to_column(row, state):
    width = row.shape[1]
    sub = iota((ROWS, width), 0)
    keep = (sub == iota((ROWS, width), 1)) & (sub < state)
    return jnp.sum(jnp.where(keep, row, 0.0), axis=1, keepdims=True)


def note(column, scalar, state, share):
    spot = iota((1, LANE), 1) % share
    return jnp.where(spot == state, scalar, column_to_row(column, state, share))


def total(value):
    return jnp.sum(jnp.sum(value, axis=0, keepdims=True), axis=1, keepdims=True)


def apply_precond(precond, residual, scaled):
    state, width = residual.shape
    dot = jnp.zeros((state, LANE), F32)
    for start in range(0, width, LANE):
        at = slice(start, start + LANE)
        out = precond[0, :, at] * residual[0:1, at]
        for j in range(1, state):
            out = out + precond[j, :, at] * residual[j : j + 1, at]
        scaled[0:state, at] = out
        scaled[state:ROWS, at] = jnp.zeros((ROWS - state, LANE), F32)
        dot = dot + out * residual[:, at]
    return total(dot)


def reorder(tiles, index):
    low = jnp.broadcast_to(index & (LANE - 1), (ROWS, LANE))
    part = jnp.broadcast_to(index >> 7, (ROWS, LANE))
    out = jnp.zeros((ROWS, LANE), F32)
    for k, one in enumerate(tiles):
        out = jnp.where(part == k, jnp.take_along_axis(one, low, axis=1), out)
    return out


def send_states(scaled, dot, origin, send, state):
    width = scaled.shape[1]
    copies, _, share = send.shape[1:]
    notes = note(scaled[:, 0:1], dot, state, share)
    tiles = [scaled[:, start : start + LANE] for start in range(0, width, LANE)]
    sub = iota((ROWS, share), 0)
    for k in range(width // LANE):
        piece = reorder(tiles, origin[0:1, k * LANE : (k + 1) * LANE])
        for m in range(LANE // share):
            one = jnp.where(sub == state, notes[:, :share], piece[:, m * share : (m + 1) * share])
            for copy in range(copies):
                send[k * (LANE // share) + m, copy] = one


def invert(slot, hot, left, origin):
    width = slot.shape[1]
    hot_table(hot, slot, width)
    sub = iota((ROWS, SUB), 0)
    for start in range(0, width, SUB):
        number = iota((ROWS, SUB), 1) + start
        digits = jnp.where(sub == 0, number >> 5, jnp.where(sub == 1, number & 31, 0)).astype(F32).astype(BF16)
        part = spread_row(slot[0:1, start : start + SUB] >> 8, ROWS)
        for k in range(width // SUB):
            left[k * ROWS : (k + 1) * ROWS, start : start + SUB] = equal(part, jnp.asarray(k, BF16)) * digits
    found = both(left[...], hot[...], ((1,), (1,)))
    for k in range(width // SUB):
        row = 32.0 * found[k * ROWS : k * ROWS + 1] + found[k * ROWS + 1 : k * ROWS + 2]
        origin[0:1, k * SUB : (k + 1) * SUB] = row.astype(jnp.int32)


def begin_kernel(right_in, precond_in, slot_in, heads_in, tails_in, heads_tile_in, tails_tile_in, cluster_in, damping_in,
                 send, scaled, origin, heads, tails, heads_tile, tails_tile, hot_pairs, lam,
                 hot, left, right, precond, slot, cluster, damping, sems):
    state = right.shape[0]
    copies = fetch(sems, (precond_in, precond), (heads_in, heads), (tails_in, tails), (slot_in, slot), (right_in, right),
                   (cluster_in, cluster), (damping_in, damping), (heads_tile_in, heads_tile), (tails_tile_in, tails_tile))
    pairs = heads.shape[1]
    copies[3].wait()
    invert(slot, hot, left, origin)
    for copy in copies[1:3] + copies[5:7]:
        copy.wait()
    hot_table(hot_pairs.at[:, 0:pairs], heads, pairs)
    hot_table(hot_pairs.at[:, pairs:], tails, pairs)
    spare = jnp.zeros((1, LANE - damping.shape[1]), F32)
    row = jnp.broadcast_to(jnp.concatenate([damping[...], spare], axis=1), lam.shape)
    lam[...] = jnp.take_along_axis(row, cluster[...], axis=1)
    copies[4].wait()
    copies[0].wait()
    dot = apply_precond(precond, right, scaled)
    send_states(scaled, dot, origin, send, state)
    copies[7].wait()
    copies[8].wait()


def fetch(sems, *pairs):
    copies = [pltpu.make_async_copy(source, place, sems.at[i]) for i, (source, place) in enumerate(pairs)]
    for copy in copies:
        copy.start()
    return copies


def back_product(transition, errors, at):
    back = transition[0, :, at] * errors[0:1, at]
    for j in range(1, transition.shape[0]):
        back = back + transition[j, :, at] * errors[j : j + 1, at]
    return back


def pull(ends, h, field, parity, state, found_before):
    index = ends[h : h + 8, :]
    low, part = index & (LANE - 1), index >> 7
    out = list(found_before)
    half, tiles = field.shape[0], field.shape[1]
    for i in range(half):
        for r in range(tiles):
            here = part == (2 * i + parity) * tiles + r
            for c in range(state):
                from_row = jnp.broadcast_to(field[i, r, c : c + 1, :], (8, LANE))
                out[c] = jnp.where(here, jnp.take_along_axis(from_row, low, axis=1), out[c])
    return out


def fill(field, got):
    half, tiles = field.shape[0], field.shape[1]
    per = LANE // got.shape[2]
    for i in range(half):
        for r in range(tiles):
            field[i, r] = join([got[(r * per + m) * half + i] for m in range(per)])


def row_sums(tiles):
    row = iota((8, LANE), 0)
    for step in (4, 2, 1):
        tiles = [
            jnp.where(row & step == 0, one + pltpu.roll(one, 8 - step, 0), other + pltpu.roll(other, step, 0))
            for one, other in zip(tiles[:step], tiles[step:])
        ]
    return tiles[0]


def half_kernel(axes, once, got, heads_tile, tails_tile, scaled, transition, *refs):
    state = transition.shape[0]
    width = scaled.shape[1]
    chunks = heads_tile.shape[0]
    if once:
        blocks_in, pulled, errors, inertial, blocks, field, sems = refs
        (copy,) = fetch(sems, (blocks_in, blocks))
    else:
        pulled, errors, inertial, field = refs
    fill(field, got)
    parity = lax.axis_index(axes[1]) % 2
    zero = [jnp.zeros((8, LANE), F32)] * state
    for h in range(0, chunks, 8):
        for which, ends in enumerate((heads_tile, tails_tile)):
            for c, value in enumerate(pull(ends, h, field, parity, state, zero)):
                pulled[which * state + c, h : h + 8, :] = value
    lane = iota((ROWS, width), 1)
    ahead = jnp.where(lane == width - 1, 0.0, pltpu.roll(scaled[...], width - 1, 1))
    empty = jnp.zeros((ROWS - state, LANE), F32)
    for start in range(0, width, LANE):
        at = slice(start, start + LANE)
        low, high = scaled[0:8, at], scaled[8:state, at]
        for first in range(0, ROWS, 8):
            moved = [
                transition[i, 0:8, at] * low + jnp.concatenate([transition[i, 8:state, at] * high, empty], axis=0)
                for i in range(first, min(first + 8, state))
            ]
            moved += [jnp.zeros((8, LANE), F32)] * (8 - len(moved))
            errors[first : first + 8, at] = ahead[first : first + 8, at] - row_sums(moved)
    prior = jnp.where(lane == 0, 0.0, pltpu.roll(errors[...], 1, 1))
    inertial[state:ROWS, :] = jnp.zeros((ROWS - state, width), F32)
    for start in range(0, width - LANE, LANE):
        at = slice(start, start + LANE)
        inertial[0:state, at] = prior[0:state, at] - back_product(transition, errors, at)
    inertial[0:state, width - LANE :] = prior[0:state, width - LANE :]
    if once:
        copy.wait()


def group_kernel(n_time, n_clus, axes, got, other, pulled, heads, tails, heads_tile, tails_tile, hot, lam, blocks,
                 errors, partial, transition, send, inertial, sums, field, values, left, last):
    state = transition.shape[0]
    width = errors.shape[1]
    share = got.shape[2]
    pairs = heads.shape[1]
    parts = n_clus * width // SUB
    per_part = SUB // share
    chunks = pairs // LANE
    half = n_clus // 2
    time_at, clus_at = lax.axis_index(axes[0]), lax.axis_index(axes[1])
    flat = time_at * n_clus + clus_at
    devices = n_time * n_clus

    def source(piece):
        return (piece % n_time) * n_clus + piece // n_time

    sums[...] = jnp.sum(got[:, state : state + 1, :], axis=0) + jnp.sum(other[:, state : state + 1, :], axis=0)
    fill(field, other)
    parity = 1 - clus_at % 2

    def spread(ends, base, n):
        at = slice(base * LANE + n * SUB, base * LANE + (n + 1) * SUB)
        part = spread_row(ends[0:1, n * SUB : (n + 1) * SUB] >> 8, ROWS)
        row = (base + n * (SUB // LANE)) * ROWS
        high, low = halves(join([values[row + m * ROWS : row + (m + 1) * ROWS, :] for m in range(SUB // LANE)]))
        for k in range(parts):
            here = equal(part, jnp.asarray(k, BF16))
            left[k * 2 * ROWS : k * 2 * ROWS + ROWS, at] = here * high
            left[k * 2 * ROWS + ROWS : (k + 1) * 2 * ROWS, at] = here * low

    squares = jnp.zeros((8, LANE), F32)
    for h in range(0, chunks, 8):
        near, far = (
            pull(ends, h, field, parity, state, [pulled[which * state + c, h : h + 8, :] for c in range(state)])
            for which, ends in enumerate((heads_tile, tails_tile))
        )
        back = [None] * state
        for i in range(state):
            row = [blocks[i * state + j, h : h + 8, :] for j in range(state)]
            f = near[i]
            for j in range(state):
                f = f - row[j] * far[j]
            squares = squares + f * f
            values[pl.ds(h * ROWS + i, 8, stride=ROWS), :] = f
            for j in range(state):
                back[j] = row[j] * f if i == 0 else back[j] + row[j] * f
        for j in range(state):
            values[pl.ds((chunks + h) * ROWS + j, 8, stride=ROWS), :] = -back[j]
        for j in range(state, ROWS):
            values[pl.ds(h * ROWS + j, 8, stride=ROWS), :] = jnp.zeros((8, LANE), F32)
            values[pl.ds((chunks + h) * ROWS + j, 8, stride=ROWS), :] = jnp.zeros((8, LANE), F32)
    for n in range(pairs // SUB):
        spread(heads, 0, n)
        spread(tails, chunks, n)
    summed = both(left[...], hot[...], ((1,), (1,)))

    after = jnp.minimum(flat + 1, devices - 1)
    following = row_to_column(other[after // n_clus * half + after % n_clus // 2, state : state + 1, :], state)
    at = slice(width - LANE, width)
    ending = iota((ROWS, LANE), 1) == LANE - 1
    closed = ending & (flat == devices - 1)
    ahead = jnp.where(ending, errors[:, at] + following, errors[:, at])
    last[...] = jnp.where(closed | (iota((ROWS, LANE), 0) >= state), 0.0, ahead)
    energy = last[...] * last[...]
    for start in range(0, width - LANE, LANE):
        block = errors[:, start : start + LANE]
        energy = energy + jnp.where(iota((ROWS, LANE), 0) < state, block * block, 0.0)
    product = total(squares) + total(energy)
    inertial[...] = partial[...]
    back = transition[0, :, at] * last[0:1, :]
    for j in range(1, state):
        back = back + transition[j, :, at] * last[j : j + 1, :]
    inertial[0:state, at] = partial[0:state, at] - back

    sub = iota((ROWS, share), 0)
    damped = jnp.zeros((ROWS, share), F32)
    for k in range(parts):
        one = summed[k * 2 * ROWS : k * 2 * ROWS + ROWS] + summed[k * 2 * ROWS + ROWS : (k + 1) * 2 * ROWS]
        for m in range(per_part):
            piece = k * per_part + m
            c, t = piece // n_time, piece % n_time
            r, l = t * share // LANE, t * share % LANE
            here = jnp.where(clus_at == c, lam[r : r + 1, l : l + share], 0.0)
            states = jnp.where(sub < state, got[t * half + c // 2], 0.0)
            extra = here * states
            damped = damped + extra * states
            send[source(piece)] = one[:, m * share : (m + 1) * share] + extra
    product = product + total(damped)
    notes = note(last[:, LANE - 1 : LANE], product, state, share)
    for d in range(devices):
        send[d, state : state + 1, :] = notes[:, :share]


def image_of(n_time, n_clus, axes, got, inertial, slot, image, state):
    width = image.shape[1]
    per = LANE // got.shape[2]
    flat = lax.axis_index(axes[0]) * n_clus + lax.axis_index(axes[1])
    tiles = []
    for r in range(width // LANE):
        pieces = []
        for t in range(r * per, (r + 1) * per):
            one = got[t * n_clus]
            for c in range(1, n_clus):
                one = one + got[t * n_clus + c]
            pieces.append(one)
        tiles.append(join(pieces))
    prior = row_to_column(got[jnp.maximum(flat - 1, 0), state : state + 1, :], state)
    prior = jnp.where(flat == 0, 0.0, prior)
    for start in range(0, width, LANE):
        at = slice(start, start + LANE)
        out = reorder(tiles, slot[0:1, at]) + inertial[:, at]
        if start == 0:
            out = jnp.where(iota((ROWS, LANE), 1) == 0, out + prior, out)
        image[:, at] = out
    return jnp.sum(got[:, state : state + 1, :], axis=0)[:, state : state + 1]


def step_kernel(n_time, n_clus, axes, got, right, inertial, precond, slot, origin, sums,
                send, scaled, residual, image, scalars):
    state, width = right.shape
    product = image_of(n_time, n_clus, axes, got, inertial, slot, image, state)
    alpha = sums[0:1, state : state + 1] / product
    residual[...] = right[...] - alpha * image[0:state, :]
    dot = apply_precond(precond, residual, scaled)
    send_states(scaled, dot, origin, send, state)
    scalars[...] = jnp.broadcast_to(alpha, scalars.shape)


def end_kernel(n_time, n_clus, axes, got, residual, inertial, slot, first, scaled, along, sums, sums_next, scalars,
               solution_field, residual_out, image):
    state, width = residual.shape
    product = image_of(n_time, n_clus, axes, got, inertial, slot, image, state)
    alpha = scalars[0:1, 0:1]
    rz, rz_next = sums[0:1, state : state + 1], sums_next[0:1, state : state + 1]
    ratio = rz_next / rz
    step = rz_next / (product - ratio * rz_next / alpha)
    direction = scaled[0:state, :] + ratio * first[0:state, :]
    solution_field[...] = alpha * first[0:state, :] + step * direction
    residual_out[...] = residual[...] - step * (image[0:state, :] + ratio * along[0:state, :])


def on_device(
    right_side,
    transition,
    precond,
    slot_of,
    cluster_id,
    damping,
    pair_first,
    pair_second,
    pair_blocks,
):
    axes = ("tm", "clus")
    state, width = right_side.shape
    n_time = lax.axis_size("tm")
    n_clus = lax.axis_size("clus")
    devices = n_time * n_clus
    share = width // n_time
    pairs = pair_first.shape[1]
    positions = n_clus * width
    slot = slot_of.reshape(1, width)
    blocks = pair_blocks.reshape(state * state, pairs // LANE, LANE)
    params = pltpu.CompilerParams(vmem_limit_bytes=VMEM_LIMIT)

    def like(*shape):
        return jax.ShapeDtypeStruct(shape, F32)

    message = like(devices, ROWS, share)
    outgoing = like(n_time, n_clus // 2, ROWS, share)
    row = like(1, share)
    tile = like(ROWS, width)
    hot = pltpu.VMEM((SUB, width), BF16)
    left = pltpu.VMEM((ROWS * width // SUB, width), BF16)

    def exchange(sent):
        return lax.all_to_all(sent.reshape(devices, ROWS, share), axes, split_axis=0, concat_axis=0, tiled=True)

    def held(*arrays):
        return tuple(pltpu.with_memory_space_constraint(array, pltpu.HBM) for array in arrays)

    in_hbm = pl.BlockSpec(memory_space=pltpu.HBM)
    in_vmem = pl.BlockSpec(memory_space=pltpu.VMEM)
    dense = (pairs // LANE, LANE)
    small = (pair_first, pair_second, pair_first.reshape(dense), pair_second.reshape(dense),
             cluster_id.reshape(width // LANE, LANE), damping)
    same = [[t * n_clus + c for t in range(n_time) for c in range(q, n_clus, 2)] for q in range(2)]
    field = pltpu.VMEM((n_clus // 2, width // LANE, ROWS, LANE), F32)

    def collect(sent):
        sent = sent.reshape(devices // 2, ROWS, share)
        got = lax.all_to_all(sent, axes, split_axis=0, concat_axis=0, tiled=True, axis_index_groups=same)
        return got, lax.ppermute(got, "clus", [(c, c ^ 1) for c in range(n_clus)])

    def grouped(sent, scaled, carried, tables):
        got, other = collect(sent)
        heads, tails, heads_tile, tails_tile, hot_of, lam = carried
        shapes = (like(2 * state, *dense), tile, tile)
        operands = (got, heads_tile, tails_tile, scaled, transition)
        scratch = [field]
        if not tables:
            shapes += (like(*blocks.shape),)
            operands += held(blocks)
            scratch += [pltpu.SemaphoreType.DMA((1,))]
        pulled, errors, partial, *fresh = pl.pallas_call(
            functools.partial(half_kernel, axes, not tables),
            out_shape=shapes,
            in_specs=[in_vmem] * (len(operands) - 1) + [in_vmem if tables else in_hbm],
            scratch_shapes=scratch,
            compiler_params=params,
            name="half",
        )(*operands)
        tables = tables or fresh
        return tables, pl.pallas_call(
            functools.partial(group_kernel, n_time, n_clus, axes),
            out_shape=(message, tile, row),
            scratch_shapes=[
                field,
                pltpu.VMEM((2 * pairs // LANE * ROWS, LANE), F32),
                pltpu.VMEM((2 * ROWS * positions // SUB, 2 * pairs), BF16),
                pltpu.VMEM((ROWS, LANE), F32),
            ],
            compiler_params=params,
            name="group",
        )(got, other, pulled, heads, tails, heads_tile, tails_tile, hot_of, lam, *tables, errors, partial, transition)

    sent, first, origin, *carried = pl.pallas_call(
        begin_kernel,
        out_shape=(
            outgoing,
            tile,
            jax.ShapeDtypeStruct((1, width), jnp.int32),
            *(jax.ShapeDtypeStruct(array.shape, array.dtype) for array in small[:4]),
            jax.ShapeDtypeStruct((SUB, 2 * pairs), BF16),
            like(width // LANE, LANE),
        ),
        in_specs=[in_hbm] * (3 + len(small)),
        scratch_shapes=[
            hot,
            left,
            pltpu.VMEM(right_side.shape, F32),
            pltpu.VMEM(precond.shape, F32),
            pltpu.VMEM(slot.shape, jnp.int32),
            pltpu.VMEM((width // LANE, LANE), jnp.int32),
            pltpu.VMEM(damping.shape, F32),
            pltpu.SemaphoreType.DMA((3 + len(small),)),
        ],
        compiler_params=params,
        name="begin",
    )(*held(right_side, precond, slot, *small))
    tables, (back, inertial, sums) = grouped(sent, first, carried, None)
    sent, scaled, residual, along, scalars = pl.pallas_call(
        functools.partial(step_kernel, n_time, n_clus, axes),
        out_shape=(outgoing, tile, like(state, width), tile, like(1, LANE)),
        compiler_params=params,
        name="step",
    )(exchange(back), right_side, inertial, precond, slot, origin, sums)
    _, (back, inertial, sums_next) = grouped(sent, scaled, carried, tables)
    return pl.pallas_call(
        functools.partial(end_kernel, n_time, n_clus, axes),
        out_shape=(like(state, width), like(state, width)),
        scratch_shapes=[pltpu.VMEM((ROWS, width), F32)],
        compiler_params=params,
        name="end",
    )(exchange(back), residual, inertial, slot, first, scaled, along, sums, sums_next, scalars)


def solution(mesh):
    placed = (
        P(None, ("tm", "clus")),
        P(None, None, ("tm", "clus")),
        P(None, None, ("tm", "clus")),
        P(("tm", "clus")),
        P("tm", "clus"),
        P("tm", None),
        P("tm", "clus"),
        P("tm", "clus"),
        P(None, None, "tm", "clus"),
    )
    return jax.shard_map(
        on_device,
        mesh=mesh,
        in_specs=placed,
        out_specs=(P(None, ("tm", "clus")), P(None, ("tm", "clus"))),
        check_vma=False,
    )
```

```python
import functools
import jax
import jax.numpy as jnp
from jax import lax
from jax.experimental import pallas as pl
from jax.experimental.pallas import tpu as pltpu
from jax.sharding import PartitionSpec as P

F32 = jnp.float32
BF16 = jnp.bfloat16
ROWS = 16
SUB = 256
LANE = 128
VMEM_LIMIT = 16 * 1024 * 1024


def iota(shape, axis):
    return lax.broadcasted_iota(jnp.int32, shape, axis)


def halves(value):
    high = value.astype(BF16)
    return high, (value - high.astype(F32)).astype(BF16)


def pick(rows, index):
    numbers = lax.GatherDimensionNumbers(
        offset_dims=(),
        collapsed_slice_dims=(1,),
        start_index_map=(1,),
        operand_batching_dims=(0,),
        start_indices_batching_dims=(0,),
    )
    mode = lax.GatherScatterMode.PROMISE_IN_BOUNDS
    return lax.gather(rows, index[:, :, None], numbers, (1, 1), mode=mode)


def join(pieces):
    return pieces[0] if len(pieces) == 1 else jnp.concatenate(pieces, axis=1)


def spread_rows(numbers):
    return numbers.astype(F32).astype(BF16)


def spread_row(row, count):
    return jnp.broadcast_to(row.astype(F32), (count, row.shape[1])).astype(BF16)


def hot_table(hot, index_ref, width):
    rows = [spread_rows(iota((ROWS, SUB), 0) + r) for r in range(0, SUB, ROWS)]
    for start in range(0, width, SUB):
        at = slice(start, start + SUB)
        low = spread_row(index_ref[0:1, at] & (SUB - 1), ROWS)
        for r, row in enumerate(rows):
            hot[r * ROWS : (r + 1) * ROWS, at] = equal(row, low)


def equal(one, other):
    return jnp.maximum(jnp.asarray(1, BF16) - jnp.abs(one - other), jnp.asarray(0, BF16))


def both(left, right, contract):
    return lax.dot_general(left, right, (contract, ((), ())), preferred_element_type=F32)


def column_to_row(column, state, share):
    spot = iota((ROWS, LANE), 1) % share
    row = iota((ROWS, LANE), 0)
    return jnp.sum(jnp.where((spot == row) & (row < state), column, 0.0), axis=0, keepdims=True)


def row_to_column(row, state):
    width = row.shape[1]
    sub = iota((ROWS, width), 0)
    keep = (sub == iota((ROWS, width), 1)) & (sub < state)
    return jnp.sum(jnp.where(keep, row, 0.0), axis=1, keepdims=True)


def note(column, scalar, state, share):
    spot = iota((1, LANE), 1) % share
    return jnp.where(spot == state, scalar, column_to_row(column, state, share))


def total(value):
    return jnp.sum(jnp.sum(value, axis=0, keepdims=True), axis=1, keepdims=True)


def apply_precond(precond, residual, scaled):
    state, width = residual.shape
    dot = jnp.zeros((state, LANE), F32)
    for start in range(0, width, LANE):
        at = slice(start, start + LANE)
        out = precond[0, :, at] * residual[0:1, at]
        for j in range(1, state):
            out = out + precond[j, :, at] * residual[j : j + 1, at]
        scaled[0:state, at] = out
        scaled[state:ROWS, at] = jnp.zeros((ROWS - state, LANE), F32)
        dot = dot + out * residual[:, at]
    return total(dot)


def reorder(tiles, index):
    low = jnp.broadcast_to(index & (LANE - 1), (ROWS, LANE))
    part = jnp.broadcast_to(index >> 7, (ROWS, LANE))
    out = jnp.zeros((ROWS, LANE), F32)
    for k, one in enumerate(tiles):
        out = jnp.where(part == k, pick(one, low), out)
    return out


def send_states(scaled, dot, origin, send, state):
    width = scaled.shape[1]
    copies, _, share = send.shape[1:]
    notes = note(scaled[:, 0:1], dot, state, share)
    tiles = [scaled[:, start : start + LANE] for start in range(0, width, LANE)]
    sub = iota((ROWS, share), 0)
    for k in range(width // LANE):
        piece = reorder(tiles, origin[0:1, k * LANE : (k + 1) * LANE])
        for m in range(LANE // share):
            one = jnp.where(sub == state, notes[:, :share], piece[:, m * share : (m + 1) * share])
            for copy in range(copies):
                send[k * (LANE // share) + m, copy] = one


def invert(slot, hot, left, origin):
    width = slot.shape[1]
    hot_table(hot, slot, width)
    sub = iota((ROWS, SUB), 0)
    for start in range(0, width, SUB):
        number = iota((ROWS, SUB), 1) + start
        digits = jnp.where(sub == 0, number >> 5, jnp.where(sub == 1, number & 31, 0)).astype(F32).astype(BF16)
        part = spread_row(slot[0:1, start : start + SUB] >> 8, ROWS)
        for k in range(width // SUB):
            left[k * ROWS : (k + 1) * ROWS, start : start + SUB] = equal(part, jnp.asarray(k, BF16)) * digits
    found = both(left[...], hot[...], ((1,), (1,)))
    for k in range(width // SUB):
        row = 32.0 * found[k * ROWS : k * ROWS + 1] + found[k * ROWS + 1 : k * ROWS + 2]
        origin[0:1, k * SUB : (k + 1) * SUB] = row.astype(jnp.int32)


def begin_kernel(right_in, precond_in, slot_in, heads_in, tails_in, heads_tile_in, tails_tile_in, cluster_in, damping_in,
                 send, scaled, origin, heads, tails, heads_tile, tails_tile, hot_pairs, lam,
                 hot, left, right, precond, slot, cluster, damping, sems):
    state = right.shape[0]
    copies = fetch(sems, (precond_in, precond), (heads_in, heads), (tails_in, tails), (slot_in, slot), (right_in, right),
                   (cluster_in, cluster), (damping_in, damping), (heads_tile_in, heads_tile), (tails_tile_in, tails_tile))
    pairs = heads.shape[1]
    copies[3].wait()
    invert(slot, hot, left, origin)
    for copy in copies[1:3] + copies[5:7]:
        copy.wait()
    hot_table(hot_pairs.at[:, 0:pairs], heads, pairs)
    hot_table(hot_pairs.at[:, pairs:], tails, pairs)
    spare = jnp.zeros((1, LANE - damping.shape[1]), F32)
    row = jnp.broadcast_to(jnp.concatenate([damping[...], spare], axis=1), lam.shape)
    lam[...] = pick(row, cluster[...])
    copies[4].wait()
    copies[0].wait()
    dot = apply_precond(precond, right, scaled)
    send_states(scaled, dot, origin, send, state)
    copies[7].wait()
    copies[8].wait()


def fetch(sems, *pairs):
    copies = [pltpu.make_async_copy(source, place, sems.at[i]) for i, (source, place) in enumerate(pairs)]
    for copy in copies:
        copy.start()
    return copies


def back_product(transition, errors, at):
    back = transition[0, :, at] * errors[0:1, at]
    for j in range(1, transition.shape[0]):
        back = back + transition[j, :, at] * errors[j : j + 1, at]
    return back


def pull(ends, h, field, parity, state, found_before):
    index = ends[h : h + 8, :]
    low, part = index & (LANE - 1), index >> 7
    out = list(found_before)
    half, tiles = field.shape[0], field.shape[1]
    for i in range(half):
        for r in range(tiles):
            here = part == (2 * i + parity) * tiles + r
            for c in range(state):
                from_row = jnp.broadcast_to(field[i, r, c : c + 1, :], (8, LANE))
                out[c] = jnp.where(here, pick(from_row, low), out[c])
    return out


def fill(field, got):
    half, tiles = field.shape[0], field.shape[1]
    per = LANE // got.shape[2]
    for i in range(half):
        for r in range(tiles):
            field[i, r] = join([got[(r * per + m) * half + i] for m in range(per)])


def row_sums(tiles):
    row = iota((8, LANE), 0)
    for step in (4, 2, 1):
        tiles = [
            jnp.where(row & step == 0, one + pltpu.roll(one, 8 - step, 0), other + pltpu.roll(other, step, 0))
            for one, other in zip(tiles[:step], tiles[step:])
        ]
    return tiles[0]


def half_kernel(axes, once, got, heads_tile, tails_tile, scaled, transition, *refs):
    state = transition.shape[0]
    width = scaled.shape[1]
    chunks = heads_tile.shape[0]
    if once:
        blocks_in, pulled, errors, inertial, blocks, field, sems = refs
        (copy,) = fetch(sems, (blocks_in, blocks))
    else:
        pulled, errors, inertial, field = refs
    parity = lax.axis_index(axes[1]) % 2

    def work():
        fill(field, got)
        zero = [jnp.zeros((8, LANE), F32)] * state
        for h in range(0, chunks, 8):
            for which, ends in enumerate((heads_tile, tails_tile)):
                for c, value in enumerate(pull(ends, h, field, parity, state, zero)):
                    pulled[which * state + c, h : h + 8, :] = value
        lane = iota((ROWS, width), 1)
        ahead = jnp.where(lane == width - 1, 0.0, pltpu.roll(scaled[...], width - 1, 1))
        empty = jnp.zeros((ROWS - state, LANE), F32)
        for start in range(0, width, LANE):
            at = slice(start, start + LANE)
            low, high = scaled[0:8, at], scaled[8:state, at]
            for first in range(0, ROWS, 8):
                moved = [
                    transition[i, 0:8, at] * low + jnp.concatenate([transition[i, 8:state, at] * high, empty], axis=0)
                    for i in range(first, min(first + 8, state))
                ]
                moved += [jnp.zeros((8, LANE), F32)] * (8 - len(moved))
                errors[first : first + 8, at] = ahead[first : first + 8, at] - row_sums(moved)
        prior = jnp.where(lane == 0, 0.0, pltpu.roll(errors[...], 1, 1))
        inertial[state:ROWS, :] = jnp.zeros((ROWS - state, width), F32)
        for start in range(0, width - LANE, LANE):
            at = slice(start, start + LANE)
            inertial[0:state, at] = prior[0:state, at] - back_product(transition, errors, at)
        inertial[0:state, width - LANE :] = prior[0:state, width - LANE :]

    if once:
        pl.when(parity >= 0)(work)
        copy.wait()
    else:
        work()


def group_kernel(n_time, n_clus, axes, got, other, pulled, heads, tails, heads_tile, tails_tile, hot, lam, blocks,
                 errors, partial, transition, send, inertial, sums, field, values, left, last):
    state = transition.shape[0]
    width = errors.shape[1]
    share = got.shape[2]
    pairs = heads.shape[1]
    parts = n_clus * width // SUB
    per_part = SUB // share
    chunks = pairs // LANE
    half = n_clus // 2
    time_at, clus_at = lax.axis_index(axes[0]), lax.axis_index(axes[1])
    flat = time_at * n_clus + clus_at
    devices = n_time * n_clus

    def source(piece):
        return (piece % n_time) * n_clus + piece // n_time

    sums[...] = jnp.sum(got[:, state : state + 1, :], axis=0) + jnp.sum(other[:, state : state + 1, :], axis=0)
    fill(field, other)
    parity = 1 - clus_at % 2

    def spread(ends, base, n):
        at = slice(base * LANE + n * SUB, base * LANE + (n + 1) * SUB)
        part = spread_row(ends[0:1, n * SUB : (n + 1) * SUB] >> 8, ROWS)
        row = (base + n * (SUB // LANE)) * ROWS
        high, low = halves(join([values[row + m * ROWS : row + (m + 1) * ROWS, :] for m in range(SUB // LANE)]))
        for k in range(parts):
            here = equal(part, jnp.asarray(k, BF16))
            left[k * 2 * ROWS : k * 2 * ROWS + ROWS, at] = here * high
            left[k * 2 * ROWS + ROWS : (k + 1) * 2 * ROWS, at] = here * low

    squares = jnp.zeros((8, LANE), F32)
    for h in range(0, chunks, 8):
        near, far = (
            pull(ends, h, field, parity, state, [pulled[which * state + c, h : h + 8, :] for c in range(state)])
            for which, ends in enumerate((heads_tile, tails_tile))
        )
        back = [None] * state
        for i in range(state):
            row = [blocks[i * state + j, h : h + 8, :] for j in range(state)]
            f = near[i]
            for j in range(state):
                f = f - row[j] * far[j]
            squares = squares + f * f
            values[pl.ds(h * ROWS + i, 8, stride=ROWS), :] = f
            for j in range(state):
                back[j] = row[j] * f if i == 0 else back[j] + row[j] * f
        for j in range(state):
            values[pl.ds((chunks + h) * ROWS + j, 8, stride=ROWS), :] = -back[j]
        for j in range(state, ROWS):
            values[pl.ds(h * ROWS + j, 8, stride=ROWS), :] = jnp.zeros((8, LANE), F32)
            values[pl.ds((chunks + h) * ROWS + j, 8, stride=ROWS), :] = jnp.zeros((8, LANE), F32)
    for n in range(pairs // SUB):
        spread(heads, 0, n)
        spread(tails, chunks, n)
    summed = both(left[...], hot[...], ((1,), (1,)))

    after = jnp.minimum(flat + 1, devices - 1)
    following = row_to_column(other[after // n_clus * half + after % n_clus // 2, state : state + 1, :], state)
    at = slice(width - LANE, width)
    ending = iota((ROWS, LANE), 1) == LANE - 1
    closed = ending & (flat == devices - 1)
    ahead = jnp.where(ending, errors[:, at] + following, errors[:, at])
    last[...] = jnp.where(closed | (iota((ROWS, LANE), 0) >= state), 0.0, ahead)
    energy = last[...] * last[...]
    for start in range(0, width - LANE, LANE):
        block = errors[:, start : start + LANE]
        energy = energy + jnp.where(iota((ROWS, LANE), 0) < state, block * block, 0.0)
    product = total(squares) + total(energy)
    inertial[...] = partial[...]
    back = transition[0, :, at] * last[0:1, :]
    for j in range(1, state):
        back = back + transition[j, :, at] * last[j : j + 1, :]
    inertial[0:state, at] = partial[0:state, at] - back

    sub = iota((ROWS, share), 0)
    damped = jnp.zeros((ROWS, share), F32)
    for k in range(parts):
        one = summed[k * 2 * ROWS : k * 2 * ROWS + ROWS] + summed[k * 2 * ROWS + ROWS : (k + 1) * 2 * ROWS]
        for m in range(per_part):
            piece = k * per_part + m
            c, t = piece // n_time, piece % n_time
            r, l = t * share // LANE, t * share % LANE
            here = jnp.where(clus_at == c, lam[r : r + 1, l : l + share], 0.0)
            states = jnp.where(sub < state, got[t * half + c // 2], 0.0)
            extra = here * states
            damped = damped + extra * states
            send[source(piece)] = one[:, m * share : (m + 1) * share] + extra
    product = product + total(damped)
    notes = note(last[:, LANE - 1 : LANE], product, state, share)
    for d in range(devices):
        send[d, state : state + 1, :] = notes[:, :share]


def image_of(n_time, n_clus, axes, got, inertial, slot, image, state):
    width = image.shape[1]
    per = LANE // got.shape[2]
    flat = lax.axis_index(axes[0]) * n_clus + lax.axis_index(axes[1])
    tiles = []
    for r in range(width // LANE):
        pieces = []
        for t in range(r * per, (r + 1) * per):
            one = got[t * n_clus]
            for c in range(1, n_clus):
                one = one + got[t * n_clus + c]
            pieces.append(one)
        tiles.append(join(pieces))
    prior = row_to_column(got[jnp.maximum(flat - 1, 0), state : state + 1, :], state)
    prior = jnp.where(flat == 0, 0.0, prior)
    for start in range(0, width, LANE):
        at = slice(start, start + LANE)
        out = reorder(tiles, slot[0:1, at]) + inertial[:, at]
        if start == 0:
            out = jnp.where(iota((ROWS, LANE), 1) == 0, out + prior, out)
        image[:, at] = out
    return jnp.sum(got[:, state : state + 1, :], axis=0)[:, state : state + 1]


def step_kernel(n_time, n_clus, axes, got, right, inertial, precond, slot, origin, sums,
                send, scaled, residual, image, scalars):
    state, width = right.shape
    product = image_of(n_time, n_clus, axes, got, inertial, slot, image, state)
    alpha = sums[0:1, state : state + 1] / product
    residual[...] = right[...] - alpha * image[0:state, :]
    dot = apply_precond(precond, residual, scaled)
    send_states(scaled, dot, origin, send, state)
    scalars[...] = jnp.broadcast_to(alpha, scalars.shape)


def end_kernel(n_time, n_clus, axes, got, residual, inertial, slot, first, scaled, along, sums, sums_next, scalars,
               solution_field, residual_out, image):
    state, width = residual.shape
    product = image_of(n_time, n_clus, axes, got, inertial, slot, image, state)
    alpha = scalars[0:1, 0:1]
    rz, rz_next = sums[0:1, state : state + 1], sums_next[0:1, state : state + 1]
    ratio = rz_next / rz
    step = rz_next / (product - ratio * rz_next / alpha)
    direction = scaled[0:state, :] + ratio * first[0:state, :]
    solution_field[...] = alpha * first[0:state, :] + step * direction
    residual_out[...] = residual[...] - step * (image[0:state, :] + ratio * along[0:state, :])


def on_device(
    right_side,
    transition,
    precond,
    slot_of,
    cluster_id,
    damping,
    pair_first,
    pair_second,
    pair_blocks,
):
    axes = ("tm", "clus")
    state, width = right_side.shape
    n_time = lax.axis_size("tm")
    n_clus = lax.axis_size("clus")
    devices = n_time * n_clus
    share = width // n_time
    pairs = pair_first.shape[1]
    positions = n_clus * width
    slot = slot_of.reshape(1, width)
    blocks = pair_blocks.reshape(state * state, pairs // LANE, LANE)
    params = pltpu.CompilerParams(vmem_limit_bytes=VMEM_LIMIT)

    def like(*shape):
        return jax.ShapeDtypeStruct(shape, F32)

    message = like(devices, ROWS, share)
    outgoing = like(n_time, n_clus // 2, ROWS, share)
    row = like(1, share)
    tile = like(ROWS, width)
    hot = pltpu.VMEM((SUB, width), BF16)
    left = pltpu.VMEM((ROWS * width // SUB, width), BF16)

    def exchange(sent):
        return lax.all_to_all(sent.reshape(devices, ROWS, share), axes, split_axis=0, concat_axis=0, tiled=True)

    def held(*arrays):
        return tuple(pltpu.with_memory_space_constraint(array, pltpu.HBM) for array in arrays)

    in_hbm = pl.BlockSpec(memory_space=pltpu.HBM)
    in_vmem = pl.BlockSpec(memory_space=pltpu.VMEM)
    dense = (pairs // LANE, LANE)
    small = (pair_first, pair_second, pair_first.reshape(dense), pair_second.reshape(dense),
             cluster_id.reshape(width // LANE, LANE), damping)
    same = [[t * n_clus + c for t in range(n_time) for c in range(q, n_clus, 2)] for q in range(2)]
    field = pltpu.VMEM((n_clus // 2, width // LANE, ROWS, LANE), F32)

    def collect(sent):
        sent = sent.reshape(devices // 2, ROWS, share)
        got = lax.all_to_all(sent, axes, split_axis=0, concat_axis=0, tiled=True, axis_index_groups=same)
        return got, lax.ppermute(got, "clus", [(c, c ^ 1) for c in range(n_clus)])

    def grouped(sent, scaled, carried, tables):
        got, other = collect(sent)
        heads, tails, heads_tile, tails_tile, hot_of, lam = carried
        shapes = (like(2 * state, *dense), tile, tile)
        operands = (got, heads_tile, tails_tile, scaled, transition)
        scratch = [field]
        if not tables:
            shapes += (like(*blocks.shape),)
            operands += held(blocks)
            scratch += [pltpu.SemaphoreType.DMA((1,))]
        pulled, errors, partial, *fresh = pl.pallas_call(
            functools.partial(half_kernel, axes, not tables),
            out_shape=shapes,
            in_specs=[in_vmem] * (len(operands) - 1) + [in_vmem if tables else in_hbm],
            scratch_shapes=scratch,
            compiler_params=params,
            name="half",
        )(*operands)
        tables = tables or fresh
        return tables, pl.pallas_call(
            functools.partial(group_kernel, n_time, n_clus, axes),
            out_shape=(message, tile, row),
            scratch_shapes=[
                field,
                pltpu.VMEM((2 * pairs // LANE * ROWS, LANE), F32),
                pltpu.VMEM((2 * ROWS * positions // SUB, 2 * pairs), BF16),
                pltpu.VMEM((ROWS, LANE), F32),
            ],
            compiler_params=params,
            name="group",
        )(got, other, pulled, heads, tails, heads_tile, tails_tile, hot_of, lam, *tables, errors, partial, transition)

    sent, first, origin, *carried = pl.pallas_call(
        begin_kernel,
        out_shape=(
            outgoing,
            tile,
            jax.ShapeDtypeStruct((1, width), jnp.int32),
            *(jax.ShapeDtypeStruct(array.shape, array.dtype) for array in small[:4]),
            jax.ShapeDtypeStruct((SUB, 2 * pairs), BF16),
            like(width // LANE, LANE),
        ),
        in_specs=[in_hbm] * (3 + len(small)),
        scratch_shapes=[
            hot,
            left,
            pltpu.VMEM(right_side.shape, F32),
            pltpu.VMEM(precond.shape, F32),
            pltpu.VMEM(slot.shape, jnp.int32),
            pltpu.VMEM((width // LANE, LANE), jnp.int32),
            pltpu.VMEM(damping.shape, F32),
            pltpu.SemaphoreType.DMA((3 + len(small),)),
        ],
        compiler_params=params,
        name="begin",
    )(*held(right_side, precond, slot, *small))
    tables, (back, inertial, sums) = grouped(sent, first, carried, None)
    sent, scaled, residual, along, scalars = pl.pallas_call(
        functools.partial(step_kernel, n_time, n_clus, axes),
        out_shape=(outgoing, tile, like(state, width), tile, like(1, LANE)),
        compiler_params=params,
        name="step",
    )(exchange(back), right_side, inertial, precond, slot, origin, sums)
    _, (back, inertial, sums_next) = grouped(sent, scaled, carried, tables)
    return pl.pallas_call(
        functools.partial(end_kernel, n_time, n_clus, axes),
        out_shape=(like(state, width), like(state, width)),
        scratch_shapes=[pltpu.VMEM((ROWS, width), F32)],
        compiler_params=params,
        name="end",
    )(exchange(back), residual, inertial, slot, first, scaled, along, sums, sums_next, scalars)


def solution(mesh):
    placed = (
        P(None, ("tm", "clus")),
        P(None, None, ("tm", "clus")),
        P(None, None, ("tm", "clus")),
        P(("tm", "clus")),
        P("tm", "clus"),
        P("tm", None),
        P("tm", "clus"),
        P("tm", "clus"),
        P(None, None, "tm", "clus"),
    )
    return jax.shard_map(
        on_device,
        mesh=mesh,
        in_specs=placed,
        out_specs=(P(None, ("tm", "clus")), P(None, ("tm", "clus"))),
        check_vma=False,
    )
```

```python
import functools
import jax
import jax.numpy as jnp
from jax import lax
from jax.experimental import pallas as pl
from jax.experimental.pallas import tpu as pltpu
from jax.sharding import PartitionSpec as P

F32 = jnp.float32
BF16 = jnp.bfloat16
ROWS = 16
SUB = 256
LANE = 128
VMEM_LIMIT = 16 * 1024 * 1024


def iota(shape, axis):
    return lax.broadcasted_iota(jnp.int32, shape, axis)


def halves(value):
    high = value.astype(BF16)
    return high, (value - high.astype(F32)).astype(BF16)


def pick(rows, index):
    numbers = lax.GatherDimensionNumbers(
        offset_dims=(),
        collapsed_slice_dims=(1,),
        start_index_map=(1,),
        operand_batching_dims=(0,),
        start_indices_batching_dims=(0,),
    )
    mode = lax.GatherScatterMode.PROMISE_IN_BOUNDS
    return lax.gather(rows, index[:, :, None], numbers, (1, 1), mode=mode)


def join(pieces):
    return pieces[0] if len(pieces) == 1 else jnp.concatenate(pieces, axis=1)


def spread_rows(numbers):
    return numbers.astype(F32).astype(BF16)


def spread_row(row, count):
    return jnp.broadcast_to(row.astype(F32), (count, row.shape[1])).astype(BF16)


def hot_table(hot, index_ref, width):
    rows = [spread_rows(iota((ROWS, SUB), 0) + r) for r in range(0, SUB, ROWS)]
    for start in range(0, width, SUB):
        at = slice(start, start + SUB)
        low = spread_row(index_ref[0:1, at] & (SUB - 1), ROWS)
        for r, row in enumerate(rows):
            hot[r * ROWS : (r + 1) * ROWS, at] = equal(row, low)


def equal(one, other):
    return jnp.maximum(jnp.asarray(1, BF16) - jnp.abs(one - other), jnp.asarray(0, BF16))


def both(left, right, contract):
    return lax.dot_general(left, right, (contract, ((), ())), preferred_element_type=F32)


def column_to_row(column, state, share):
    spot = iota((ROWS, LANE), 1) % share
    row = iota((ROWS, LANE), 0)
    return jnp.sum(jnp.where((spot == row) & (row < state), column, 0.0), axis=0, keepdims=True)


def row_to_column(row, state):
    width = row.shape[1]
    sub = iota((ROWS, width), 0)
    keep = (sub == iota((ROWS, width), 1)) & (sub < state)
    return jnp.sum(jnp.where(keep, row, 0.0), axis=1, keepdims=True)


def note(column, scalar, state, share):
    spot = iota((1, LANE), 1) % share
    return jnp.where(spot == state, scalar, column_to_row(column, state, share))


def total(value):
    return jnp.sum(jnp.sum(value, axis=0, keepdims=True), axis=1, keepdims=True)


def apply_precond(precond, residual, scaled):
    state, width = residual.shape
    dot = jnp.zeros((state, LANE), F32)
    for start in range(0, width, LANE):
        at = slice(start, start + LANE)
        out = precond[0, :, at] * residual[0:1, at]
        for j in range(1, state):
            out = out + precond[j, :, at] * residual[j : j + 1, at]
        scaled[0:state, at] = out
        scaled[state:ROWS, at] = jnp.zeros((ROWS - state, LANE), F32)
        dot = dot + out * residual[:, at]
    return total(dot)


def reorder(tiles, index):
    low = jnp.broadcast_to(index & (LANE - 1), (ROWS, LANE))
    part = jnp.broadcast_to(index >> 7, (ROWS, LANE))
    out = jnp.zeros((ROWS, LANE), F32)
    for k, one in enumerate(tiles):
        out = jnp.where(part == k, pick(one, low), out)
    return out


def send_states(scaled, dot, origin, send, state):
    width = scaled.shape[1]
    copies, _, share = send.shape[1:]
    notes = note(scaled[:, 0:1], dot, state, share)
    tiles = [scaled[:, start : start + LANE] for start in range(0, width, LANE)]
    sub = iota((ROWS, share), 0)
    for k in range(width // LANE):
        piece = reorder(tiles, origin[0:1, k * LANE : (k + 1) * LANE])
        for m in range(LANE // share):
            one = jnp.where(sub == state, notes[:, :share], piece[:, m * share : (m + 1) * share])
            for copy in range(copies):
                send[k * (LANE // share) + m, copy] = one


def invert(slot, hot, left, origin):
    width = slot.shape[1]
    hot_table(hot, slot, width)
    sub = iota((ROWS, SUB), 0)
    for start in range(0, width, SUB):
        number = iota((ROWS, SUB), 1) + start
        digits = jnp.where(sub == 0, number >> 5, jnp.where(sub == 1, number & 31, 0)).astype(F32).astype(BF16)
        part = spread_row(slot[0:1, start : start + SUB] >> 8, ROWS)
        for k in range(width // SUB):
            left[k * ROWS : (k + 1) * ROWS, start : start + SUB] = equal(part, jnp.asarray(k, BF16)) * digits
    found = both(left[...], hot[...], ((1,), (1,)))
    for k in range(width // SUB):
        row = 32.0 * found[k * ROWS : k * ROWS + 1] + found[k * ROWS + 1 : k * ROWS + 2]
        origin[0:1, k * SUB : (k + 1) * SUB] = row.astype(jnp.int32)


def begin_kernel(right_in, precond_in, slot_in, heads_in, tails_in, heads_tile_in, tails_tile_in, cluster_in, damping_in,
                 send, scaled, origin, heads, tails, heads_tile, tails_tile, lam,
                 hot, left, right, precond, slot, cluster, damping, sems):
    state = right.shape[0]
    copies = fetch(sems, (precond_in, precond), (heads_in, heads), (tails_in, tails), (slot_in, slot), (right_in, right),
                   (cluster_in, cluster), (damping_in, damping), (heads_tile_in, heads_tile), (tails_tile_in, tails_tile))
    copies[3].wait()
    invert(slot, hot, left, origin)
    copies[5].wait()
    copies[6].wait()
    spare = jnp.zeros((1, LANE - damping.shape[1]), F32)
    row = jnp.broadcast_to(jnp.concatenate([damping[...], spare], axis=1), lam.shape)
    lam[...] = pick(row, cluster[...])
    copies[4].wait()
    copies[0].wait()
    dot = apply_precond(precond, right, scaled)
    send_states(scaled, dot, origin, send, state)
    for copy in copies[1:3] + copies[7:]:
        copy.wait()


def fetch(sems, *pairs):
    copies = [pltpu.make_async_copy(source, place, sems.at[i]) for i, (source, place) in enumerate(pairs)]
    for copy in copies:
        copy.start()
    return copies


def back_product(transition, errors, at):
    back = transition[0, :, at] * errors[0:1, at]
    for j in range(1, transition.shape[0]):
        back = back + transition[j, :, at] * errors[j : j + 1, at]
    return back


def pull(ends, h, field, parity, state, found_before):
    index = ends[h : h + 8, :]
    low, part = index & (LANE - 1), index >> 7
    out = list(found_before)
    half, tiles = field.shape[0], field.shape[1]
    for i in range(half):
        for r in range(tiles):
            here = part == (2 * i + parity) * tiles + r
            for c in range(state):
                from_row = jnp.broadcast_to(field[i, r, c : c + 1, :], (8, LANE))
                out[c] = jnp.where(here, pick(from_row, low), out[c])
    return out


def fill(field, got):
    half, tiles = field.shape[0], field.shape[1]
    per = LANE // got.shape[2]
    for i in range(half):
        for r in range(tiles):
            field[i, r] = join([got[(r * per + m) * half + i] for m in range(per)])


def row_sums(tiles):
    row = iota((8, LANE), 0)
    for step in (4, 2, 1):
        tiles = [
            jnp.where(row & step == 0, one + pltpu.roll(one, 8 - step, 0), other + pltpu.roll(other, step, 0))
            for one, other in zip(tiles[:step], tiles[step:])
        ]
    return tiles[0]


def half_kernel(axes, once, got, heads_tile, tails_tile, scaled, transition, *refs):
    state = transition.shape[0]
    width = scaled.shape[1]
    chunks = heads_tile.shape[0]
    if once:
        heads, tails, blocks_in, pulled, errors, inertial, hot, blocks, field, sems = refs
        (copy,) = fetch(sems, (blocks_in, blocks))
    else:
        pulled, errors, inertial, field = refs
    parity = lax.axis_index(axes[1]) % 2

    def work():
        fill(field, got)
        if once:
            pairs = heads.shape[1]
            hot_table(hot.at[:, 0:pairs], heads, pairs)
            hot_table(hot.at[:, pairs:], tails, pairs)
        zero = [jnp.zeros((8, LANE), F32)] * state
        for h in range(0, chunks, 8):
            for which, ends in enumerate((heads_tile, tails_tile)):
                for c, value in enumerate(pull(ends, h, field, parity, state, zero)):
                    pulled[which * state + c, h : h + 8, :] = value
        lane = iota((ROWS, width), 1)
        ahead = jnp.where(lane == width - 1, 0.0, pltpu.roll(scaled[...], width - 1, 1))
        empty = jnp.zeros((ROWS - state, LANE), F32)
        for start in range(0, width, LANE):
            at = slice(start, start + LANE)
            low, high = scaled[0:8, at], scaled[8:state, at]
            for first in range(0, ROWS, 8):
                moved = [
                    transition[i, 0:8, at] * low + jnp.concatenate([transition[i, 8:state, at] * high, empty], axis=0)
                    for i in range(first, min(first + 8, state))
                ]
                moved += [jnp.zeros((8, LANE), F32)] * (8 - len(moved))
                errors[first : first + 8, at] = ahead[first : first + 8, at] - row_sums(moved)
        prior = jnp.where(lane == 0, 0.0, pltpu.roll(errors[...], 1, 1))
        inertial[state:ROWS, :] = jnp.zeros((ROWS - state, width), F32)
        for start in range(0, width - LANE, LANE):
            at = slice(start, start + LANE)
            inertial[0:state, at] = prior[0:state, at] - back_product(transition, errors, at)
        inertial[0:state, width - LANE :] = prior[0:state, width - LANE :]

    if once:
        pl.when(parity >= 0)(work)
        copy.wait()
    else:
        work()


def group_kernel(n_time, n_clus, axes, got, other, pulled, heads, tails, heads_tile, tails_tile, lam, hot, blocks,
                 errors, partial, transition, send, inertial, sums, field, values, left, last):
    state = transition.shape[0]
    width = errors.shape[1]
    share = got.shape[2]
    pairs = heads.shape[1]
    parts = n_clus * width // SUB
    per_part = SUB // share
    chunks = pairs // LANE
    half = n_clus // 2
    time_at, clus_at = lax.axis_index(axes[0]), lax.axis_index(axes[1])
    flat = time_at * n_clus + clus_at
    devices = n_time * n_clus

    def source(piece):
        return (piece % n_time) * n_clus + piece // n_time

    sums[...] = jnp.sum(got[:, state : state + 1, :], axis=0) + jnp.sum(other[:, state : state + 1, :], axis=0)
    fill(field, other)
    parity = 1 - clus_at % 2

    def spread(ends, base, n):
        at = slice(base * LANE + n * SUB, base * LANE + (n + 1) * SUB)
        part = spread_row(ends[0:1, n * SUB : (n + 1) * SUB] >> 8, ROWS)
        row = (base + n * (SUB // LANE)) * ROWS
        high, low = halves(join([values[row + m * ROWS : row + (m + 1) * ROWS, :] for m in range(SUB // LANE)]))
        for k in range(parts):
            here = equal(part, jnp.asarray(k, BF16))
            left[k * 2 * ROWS : k * 2 * ROWS + ROWS, at] = here * high
            left[k * 2 * ROWS + ROWS : (k + 1) * 2 * ROWS, at] = here * low

    squares = jnp.zeros((8, LANE), F32)
    for h in range(0, chunks, 8):
        near, far = (
            pull(ends, h, field, parity, state, [pulled[which * state + c, h : h + 8, :] for c in range(state)])
            for which, ends in enumerate((heads_tile, tails_tile))
        )
        back = [None] * state
        for i in range(state):
            row = [blocks[i * state + j, h : h + 8, :] for j in range(state)]
            f = near[i]
            for j in range(state):
                f = f - row[j] * far[j]
            squares = squares + f * f
            values[pl.ds(h * ROWS + i, 8, stride=ROWS), :] = f
            for j in range(state):
                back[j] = row[j] * f if i == 0 else back[j] + row[j] * f
        for j in range(state):
            values[pl.ds((chunks + h) * ROWS + j, 8, stride=ROWS), :] = -back[j]
        for j in range(state, ROWS):
            values[pl.ds(h * ROWS + j, 8, stride=ROWS), :] = jnp.zeros((8, LANE), F32)
            values[pl.ds((chunks + h) * ROWS + j, 8, stride=ROWS), :] = jnp.zeros((8, LANE), F32)
    for n in range(pairs // SUB):
        spread(heads, 0, n)
        spread(tails, chunks, n)
    summed = both(left[...], hot[...], ((1,), (1,)))

    after = jnp.minimum(flat + 1, devices - 1)
    following = row_to_column(other[after // n_clus * half + after % n_clus // 2, state : state + 1, :], state)
    at = slice(width - LANE, width)
    ending = iota((ROWS, LANE), 1) == LANE - 1
    closed = ending & (flat == devices - 1)
    ahead = jnp.where(ending, errors[:, at] + following, errors[:, at])
    last[...] = jnp.where(closed | (iota((ROWS, LANE), 0) >= state), 0.0, ahead)
    energy = last[...] * last[...]
    for start in range(0, width - LANE, LANE):
        block = errors[:, start : start + LANE]
        energy = energy + jnp.where(iota((ROWS, LANE), 0) < state, block * block, 0.0)
    product = total(squares) + total(energy)
    inertial[...] = partial[...]
    back = transition[0, :, at] * last[0:1, :]
    for j in range(1, state):
        back = back + transition[j, :, at] * last[j : j + 1, :]
    inertial[0:state, at] = partial[0:state, at] - back

    sub = iota((ROWS, share), 0)
    damped = jnp.zeros((ROWS, share), F32)
    for k in range(parts):
        one = summed[k * 2 * ROWS : k * 2 * ROWS + ROWS] + summed[k * 2 * ROWS + ROWS : (k + 1) * 2 * ROWS]
        for m in range(per_part):
            piece = k * per_part + m
            c, t = piece // n_time, piece % n_time
            r, l = t * share // LANE, t * share % LANE
            here = jnp.where(clus_at == c, lam[r : r + 1, l : l + share], 0.0)
            states = jnp.where(sub < state, got[t * half + c // 2], 0.0)
            extra = here * states
            damped = damped + extra * states
            send[source(piece)] = one[:, m * share : (m + 1) * share] + extra
    product = product + total(damped)
    notes = note(last[:, LANE - 1 : LANE], product, state, share)
    for d in range(devices):
        send[d, state : state + 1, :] = notes[:, :share]


def image_of(n_time, n_clus, axes, got, inertial, slot, image, state):
    width = image.shape[1]
    per = LANE // got.shape[2]
    flat = lax.axis_index(axes[0]) * n_clus + lax.axis_index(axes[1])
    tiles = []
    for r in range(width // LANE):
        pieces = []
        for t in range(r * per, (r + 1) * per):
            one = got[t * n_clus]
            for c in range(1, n_clus):
                one = one + got[t * n_clus + c]
            pieces.append(one)
        tiles.append(join(pieces))
    prior = row_to_column(got[jnp.maximum(flat - 1, 0), state : state + 1, :], state)
    prior = jnp.where(flat == 0, 0.0, prior)
    for start in range(0, width, LANE):
        at = slice(start, start + LANE)
        out = reorder(tiles, slot[0:1, at]) + inertial[:, at]
        if start == 0:
            out = jnp.where(iota((ROWS, LANE), 1) == 0, out + prior, out)
        image[:, at] = out
    return jnp.sum(got[:, state : state + 1, :], axis=0)[:, state : state + 1]


def step_kernel(n_time, n_clus, axes, got, right, inertial, precond, slot, origin, sums,
                send, scaled, residual, image, scalars):
    state, width = right.shape
    product = image_of(n_time, n_clus, axes, got, inertial, slot, image, state)
    alpha = sums[0:1, state : state + 1] / product
    residual[...] = right[...] - alpha * image[0:state, :]
    dot = apply_precond(precond, residual, scaled)
    send_states(scaled, dot, origin, send, state)
    scalars[...] = jnp.broadcast_to(alpha, scalars.shape)


def end_kernel(n_time, n_clus, axes, got, residual, inertial, slot, first, scaled, along, sums, sums_next, scalars,
               solution_field, residual_out, image):
    state, width = residual.shape
    product = image_of(n_time, n_clus, axes, got, inertial, slot, image, state)
    alpha = scalars[0:1, 0:1]
    rz, rz_next = sums[0:1, state : state + 1], sums_next[0:1, state : state + 1]
    ratio = rz_next / rz
    step = rz_next / (product - ratio * rz_next / alpha)
    direction = scaled[0:state, :] + ratio * first[0:state, :]
    solution_field[...] = alpha * first[0:state, :] + step * direction
    residual_out[...] = residual[...] - step * (image[0:state, :] + ratio * along[0:state, :])


def on_device(
    right_side,
    transition,
    precond,
    slot_of,
    cluster_id,
    damping,
    pair_first,
    pair_second,
    pair_blocks,
):
    axes = ("tm", "clus")
    state, width = right_side.shape
    n_time = lax.axis_size("tm")
    n_clus = lax.axis_size("clus")
    devices = n_time * n_clus
    share = width // n_time
    pairs = pair_first.shape[1]
    positions = n_clus * width
    slot = slot_of.reshape(1, width)
    blocks = pair_blocks.reshape(state * state, pairs // LANE, LANE)
    params = pltpu.CompilerParams(vmem_limit_bytes=VMEM_LIMIT)

    def like(*shape):
        return jax.ShapeDtypeStruct(shape, F32)

    message = like(devices, ROWS, share)
    outgoing = like(n_time, n_clus // 2, ROWS, share)
    row = like(1, share)
    tile = like(ROWS, width)
    hot = pltpu.VMEM((SUB, width), BF16)
    left = pltpu.VMEM((ROWS * width // SUB, width), BF16)

    def exchange(sent):
        return lax.all_to_all(sent.reshape(devices, ROWS, share), axes, split_axis=0, concat_axis=0, tiled=True)

    def held(*arrays):
        return tuple(pltpu.with_memory_space_constraint(array, pltpu.HBM) for array in arrays)

    in_hbm = pl.BlockSpec(memory_space=pltpu.HBM)
    in_vmem = pl.BlockSpec(memory_space=pltpu.VMEM)
    dense = (pairs // LANE, LANE)
    small = (pair_first, pair_second, pair_first.reshape(dense), pair_second.reshape(dense),
             cluster_id.reshape(width // LANE, LANE), damping)
    same = [[t * n_clus + c for t in range(n_time) for c in range(q, n_clus, 2)] for q in range(2)]
    field = pltpu.VMEM((n_clus // 2, width // LANE, ROWS, LANE), F32)

    def collect(sent):
        sent = sent.reshape(devices // 2, ROWS, share)
        got = lax.all_to_all(sent, axes, split_axis=0, concat_axis=0, tiled=True, axis_index_groups=same)
        return got, lax.ppermute(got, "clus", [(c, c ^ 1) for c in range(n_clus)])

    def grouped(sent, scaled, carried, tables):
        got, other = collect(sent)
        heads, tails, heads_tile, tails_tile, lam = carried
        shapes = (like(2 * state, *dense), tile, tile)
        operands = (got, heads_tile, tails_tile, scaled, transition)
        scratch = [field]
        if not tables:
            shapes += (jax.ShapeDtypeStruct((SUB, 2 * pairs), BF16), like(*blocks.shape))
            operands += (heads, tails, *held(blocks))
            scratch += [pltpu.SemaphoreType.DMA((1,))]
        pulled, errors, partial, *fresh = pl.pallas_call(
            functools.partial(half_kernel, axes, not tables),
            out_shape=shapes,
            in_specs=[in_vmem] * (len(operands) - 1) + [in_vmem if tables else in_hbm],
            scratch_shapes=scratch,
            compiler_params=params,
            name="half",
        )(*operands)
        tables = tables or fresh
        return tables, pl.pallas_call(
            functools.partial(group_kernel, n_time, n_clus, axes),
            out_shape=(message, tile, row),
            scratch_shapes=[
                field,
                pltpu.VMEM((2 * pairs // LANE * ROWS, LANE), F32),
                pltpu.VMEM((2 * ROWS * positions // SUB, 2 * pairs), BF16),
                pltpu.VMEM((ROWS, LANE), F32),
            ],
            compiler_params=params,
            name="group",
        )(got, other, pulled, heads, tails, heads_tile, tails_tile, lam, *tables, errors, partial, transition)

    sent, first, origin, *carried = pl.pallas_call(
        begin_kernel,
        out_shape=(
            outgoing,
            tile,
            jax.ShapeDtypeStruct((1, width), jnp.int32),
            *(jax.ShapeDtypeStruct(array.shape, array.dtype) for array in small[:4]),
            like(width // LANE, LANE),
        ),
        in_specs=[in_hbm] * (3 + len(small)),
        scratch_shapes=[
            hot,
            left,
            pltpu.VMEM(right_side.shape, F32),
            pltpu.VMEM(precond.shape, F32),
            pltpu.VMEM(slot.shape, jnp.int32),
            pltpu.VMEM((width // LANE, LANE), jnp.int32),
            pltpu.VMEM(damping.shape, F32),
            pltpu.SemaphoreType.DMA((3 + len(small),)),
        ],
        compiler_params=params,
        name="begin",
    )(*held(right_side, precond, slot, *small))
    tables, (back, inertial, sums) = grouped(sent, first, carried, None)
    sent, scaled, residual, along, scalars = pl.pallas_call(
        functools.partial(step_kernel, n_time, n_clus, axes),
        out_shape=(outgoing, tile, like(state, width), tile, like(1, LANE)),
        compiler_params=params,
        name="step",
    )(exchange(back), right_side, inertial, precond, slot, origin, sums)
    _, (back, inertial, sums_next) = grouped(sent, scaled, carried, tables)
    return pl.pallas_call(
        functools.partial(end_kernel, n_time, n_clus, axes),
        out_shape=(like(state, width), like(state, width)),
        scratch_shapes=[pltpu.VMEM((ROWS, width), F32)],
        compiler_params=params,
        name="end",
    )(exchange(back), residual, inertial, slot, first, scaled, along, sums, sums_next, scalars)


def solution(mesh):
    placed = (
        P(None, ("tm", "clus")),
        P(None, None, ("tm", "clus")),
        P(None, None, ("tm", "clus")),
        P(("tm", "clus")),
        P("tm", "clus"),
        P("tm", None),
        P("tm", "clus"),
        P("tm", "clus"),
        P(None, None, "tm", "clus"),
    )
    return jax.shard_map(
        on_device,
        mesh=mesh,
        in_specs=placed,
        out_specs=(P(None, ("tm", "clus")), P(None, ("tm", "clus"))),
        check_vma=False,
    )
```

```python
import functools
import jax
import jax.numpy as jnp
from jax import lax
from jax.experimental import pallas as pl
from jax.experimental.pallas import tpu as pltpu
from jax.sharding import PartitionSpec as P

F32 = jnp.float32
BF16 = jnp.bfloat16
ROWS = 16
SUB = 256
LANE = 128
VMEM_LIMIT = 16 * 1024 * 1024


def iota(shape, axis):
    return lax.broadcasted_iota(jnp.int32, shape, axis)


def halves(value):
    high = value.astype(BF16)
    return high, (value - high.astype(F32)).astype(BF16)


def pick(rows, index):
    numbers = lax.GatherDimensionNumbers(
        offset_dims=(),
        collapsed_slice_dims=(1,),
        start_index_map=(1,),
        operand_batching_dims=(0,),
        start_indices_batching_dims=(0,),
    )
    mode = lax.GatherScatterMode.PROMISE_IN_BOUNDS
    return lax.gather(rows, index[:, :, None], numbers, (1, 1), mode=mode)


def join(pieces):
    return pieces[0] if len(pieces) == 1 else jnp.concatenate(pieces, axis=1)


def spread_rows(numbers):
    return numbers.astype(F32).astype(BF16)


def spread_row(row, count):
    return jnp.broadcast_to(row.astype(F32), (count, row.shape[1])).astype(BF16)


def hot_table(hot, index_ref, width):
    rows = [spread_rows(iota((ROWS, SUB), 0) + r) for r in range(0, SUB, ROWS)]
    for start in range(0, width, SUB):
        at = slice(start, start + SUB)
        low = spread_row(index_ref[0:1, at] & (SUB - 1), ROWS)
        for r, row in enumerate(rows):
            hot[r * ROWS : (r + 1) * ROWS, at] = equal(row, low)


def equal(one, other):
    return jnp.maximum(jnp.asarray(1, BF16) - jnp.abs(one - other), jnp.asarray(0, BF16))


def both(left, right, contract):
    return lax.dot_general(left, right, (contract, ((), ())), preferred_element_type=F32)


def column_to_row(column, state, share):
    spot = iota((ROWS, LANE), 1) % share
    row = iota((ROWS, LANE), 0)
    return jnp.sum(jnp.where((spot == row) & (row < state), column, 0.0), axis=0, keepdims=True)


def row_to_column(row, state):
    width = row.shape[1]
    sub = iota((ROWS, width), 0)
    keep = (sub == iota((ROWS, width), 1)) & (sub < state)
    return jnp.sum(jnp.where(keep, row, 0.0), axis=1, keepdims=True)


def note(column, scalar, state, share):
    spot = iota((1, LANE), 1) % share
    return jnp.where(spot == state, scalar, column_to_row(column, state, share))


def total(value):
    return jnp.sum(jnp.sum(value, axis=0, keepdims=True), axis=1, keepdims=True)


def apply_precond(precond, residual, scaled):
    state, width = residual.shape
    dot = jnp.zeros((state, LANE), F32)
    for start in range(0, width, LANE):
        at = slice(start, start + LANE)
        out = precond[0, :, at] * residual[0:1, at]
        for j in range(1, state):
            out = out + precond[j, :, at] * residual[j : j + 1, at]
        scaled[0:state, at] = out
        scaled[state:ROWS, at] = jnp.zeros((ROWS - state, LANE), F32)
        dot = dot + out * residual[:, at]
    return total(dot)


def reorder(tiles, index):
    low = jnp.broadcast_to(index & (LANE - 1), (ROWS, LANE))
    part = jnp.broadcast_to(index >> 7, (ROWS, LANE))
    out = jnp.zeros((ROWS, LANE), F32)
    for k, one in enumerate(tiles):
        out = jnp.where(part == k, pick(one, low), out)
    return out


def send_states(scaled, dot, origin, send, state):
    width = scaled.shape[1]
    copies, _, share = send.shape[1:]
    notes = note(scaled[:, 0:1], dot, state, share)
    tiles = [scaled[:, start : start + LANE] for start in range(0, width, LANE)]
    sub = iota((ROWS, share), 0)
    for k in range(width // LANE):
        piece = reorder(tiles, origin[0:1, k * LANE : (k + 1) * LANE])
        for m in range(LANE // share):
            one = jnp.where(sub == state, notes[:, :share], piece[:, m * share : (m + 1) * share])
            for copy in range(copies):
                send[k * (LANE // share) + m, copy] = one


def invert(slot, hot, left, origin):
    width = slot.shape[1]
    hot_table(hot, slot, width)
    sub = iota((ROWS, SUB), 0)
    for start in range(0, width, SUB):
        number = iota((ROWS, SUB), 1) + start
        digits = jnp.where(sub == 0, number >> 5, jnp.where(sub == 1, number & 31, 0)).astype(F32).astype(BF16)
        part = spread_row(slot[0:1, start : start + SUB] >> 8, ROWS)
        for k in range(width // SUB):
            left[k * ROWS : (k + 1) * ROWS, start : start + SUB] = equal(part, jnp.asarray(k, BF16)) * digits
    found = both(left[...], hot[...], ((1,), (1,)))
    for k in range(width // SUB):
        row = 32.0 * found[k * ROWS : k * ROWS + 1] + found[k * ROWS + 1 : k * ROWS + 2]
        origin[0:1, k * SUB : (k + 1) * SUB] = row.astype(jnp.int32)


def begin_kernel(right_in, precond_in, slot_in, heads_in, tails_in, heads_tile_in, cluster_in, damping_in,
                 send, scaled, origin, heads, tails, heads_tile, lam,
                 hot, left, right, precond, slot, cluster, damping, sems):
    state = right.shape[0]
    copies = fetch(sems, (precond_in, precond), (heads_in, heads), (tails_in, tails), (slot_in, slot), (right_in, right),
                   (cluster_in, cluster), (damping_in, damping), (heads_tile_in, heads_tile))
    copies[3].wait()
    invert(slot, hot, left, origin)
    copies[5].wait()
    copies[6].wait()
    spare = jnp.zeros((1, LANE - damping.shape[1]), F32)
    row = jnp.broadcast_to(jnp.concatenate([damping[...], spare], axis=1), lam.shape)
    lam[...] = pick(row, cluster[...])
    copies[4].wait()
    copies[0].wait()
    dot = apply_precond(precond, right, scaled)
    send_states(scaled, dot, origin, send, state)
    for copy in copies[1:3] + copies[7:]:
        copy.wait()


def fetch(sems, *pairs):
    copies = [pltpu.make_async_copy(source, place, sems.at[i]) for i, (source, place) in enumerate(pairs)]
    for copy in copies:
        copy.start()
    return copies


def back_product(transition, errors, at):
    back = transition[0, :, at] * errors[0:1, at]
    for j in range(1, transition.shape[0]):
        back = back + transition[j, :, at] * errors[j : j + 1, at]
    return back


def pull(ends, h, field, parity, state, found_before):
    index = ends[h : h + 8, :]
    low, part = index & (LANE - 1), index >> 7
    out = list(found_before)
    half, tiles = field.shape[0], field.shape[1]
    for i in range(half):
        for r in range(tiles):
            here = part == (2 * i + parity) * tiles + r
            for c in range(state):
                from_row = jnp.broadcast_to(field[i, r, c : c + 1, :], (8, LANE))
                out[c] = jnp.where(here, pick(from_row, low), out[c])
    return out


def pull_dense(tails, hot, field, stack, parity, before, store):
    half, tiles = field.shape[0], field.shape[1]
    per = SUB // LANE
    parts = tiles // per
    pairs = tails.shape[1]
    for i in range(half):
        for k in range(parts):
            row = (i * parts + k) * 2 * ROWS
            high, low = halves(join([field[i, k * per + m] for m in range(per)]))
            stack[row : row + ROWS, :] = high
            stack[row + ROWS : row + 2 * ROWS, :] = low
    for n in range(pairs // SUB):
        at = slice(n * SUB, (n + 1) * SUB)
        found = both(stack[...], hot[:, pairs + n * SUB : pairs + (n + 1) * SUB], ((1,), (0,)))
        part = tails[0:1, at] >> 8
        out = before(n)
        for i in range(half):
            for k in range(parts):
                row = (i * parts + k) * 2 * ROWS
                one = found[row : row + ROWS] + found[row + ROWS : row + 2 * ROWS]
                out = jnp.where(part == (2 * i + parity) * parts + k, one, out)
        for m in range(per):
            store(n * per + m, out[:, m * LANE : (m + 1) * LANE])


def keep(far):
    def store(n, tile):
        far[n * ROWS : (n + 1) * ROWS, :] = tile

    return store


def fill(field, got):
    half, tiles = field.shape[0], field.shape[1]
    per = LANE // got.shape[2]
    for i in range(half):
        for r in range(tiles):
            field[i, r] = join([got[(r * per + m) * half + i] for m in range(per)])


def row_sums(tiles):
    row = iota((8, LANE), 0)
    for step in (4, 2, 1):
        tiles = [
            jnp.where(row & step == 0, one + pltpu.roll(one, 8 - step, 0), other + pltpu.roll(other, step, 0))
            for one, other in zip(tiles[:step], tiles[step:])
        ]
    return tiles[0]


def half_kernel(axes, once, got, heads_tile, scaled, transition, *refs):
    state = transition.shape[0]
    width = scaled.shape[1]
    chunks = heads_tile.shape[0]
    if once:
        heads, tails, blocks_in, pulled, far, errors, inertial, hot, blocks, field, stack, sems = refs
        (copy,) = fetch(sems, (blocks_in, blocks))
    else:
        tails, hot, pulled, far, errors, inertial, field, stack = refs
    parity = lax.axis_index(axes[1]) % 2

    def work():
        fill(field, got)
        if once:
            pairs = heads.shape[1]
            hot_table(hot.at[:, 0:pairs], heads, pairs)
            hot_table(hot.at[:, pairs:], tails, pairs)
        zero = [jnp.zeros((8, LANE), F32)] * state
        for h in range(0, chunks, 8):
            for c, value in enumerate(pull(heads_tile, h, field, parity, state, zero)):
                pulled[c, h : h + 8, :] = value
        pull_dense(tails, hot, field, stack, parity, lambda n: jnp.zeros((ROWS, SUB), F32), keep(far))
        lane = iota((ROWS, width), 1)
        ahead = jnp.where(lane == width - 1, 0.0, pltpu.roll(scaled[...], width - 1, 1))
        empty = jnp.zeros((ROWS - state, LANE), F32)
        for start in range(0, width, LANE):
            at = slice(start, start + LANE)
            low, high = scaled[0:8, at], scaled[8:state, at]
            for first in range(0, ROWS, 8):
                moved = [
                    transition[i, 0:8, at] * low + jnp.concatenate([transition[i, 8:state, at] * high, empty], axis=0)
                    for i in range(first, min(first + 8, state))
                ]
                moved += [jnp.zeros((8, LANE), F32)] * (8 - len(moved))
                errors[first : first + 8, at] = ahead[first : first + 8, at] - row_sums(moved)
        prior = jnp.where(lane == 0, 0.0, pltpu.roll(errors[...], 1, 1))
        inertial[state:ROWS, :] = jnp.zeros((ROWS - state, width), F32)
        for start in range(0, width - LANE, LANE):
            at = slice(start, start + LANE)
            inertial[0:state, at] = prior[0:state, at] - back_product(transition, errors, at)
        inertial[0:state, width - LANE :] = prior[0:state, width - LANE :]

    if once:
        pl.when(parity >= 0)(work)
        copy.wait()
    else:
        work()


def group_kernel(n_time, n_clus, axes, got, other, pulled, far_half, heads, tails, heads_tile, lam, hot, blocks,
                 errors, partial, transition, send, inertial, sums, field, stack, far_whole, values, left, last):
    state = transition.shape[0]
    width = errors.shape[1]
    share = got.shape[2]
    pairs = heads.shape[1]
    parts = n_clus * width // SUB
    per_part = SUB // share
    chunks = pairs // LANE
    half = n_clus // 2
    time_at, clus_at = lax.axis_index(axes[0]), lax.axis_index(axes[1])
    flat = time_at * n_clus + clus_at
    devices = n_time * n_clus

    def source(piece):
        return (piece % n_time) * n_clus + piece // n_time

    sums[...] = jnp.sum(got[:, state : state + 1, :], axis=0) + jnp.sum(other[:, state : state + 1, :], axis=0)
    fill(field, other)
    parity = 1 - clus_at % 2

    def spread(ends, base, n):
        at = slice(base * LANE + n * SUB, base * LANE + (n + 1) * SUB)
        part = spread_row(ends[0:1, n * SUB : (n + 1) * SUB] >> 8, ROWS)
        row = (base + n * (SUB // LANE)) * ROWS
        high, low = halves(join([values[row + m * ROWS : row + (m + 1) * ROWS, :] for m in range(SUB // LANE)]))
        for k in range(parts):
            here = equal(part, jnp.asarray(k, BF16))
            left[k * 2 * ROWS : k * 2 * ROWS + ROWS, at] = here * high
            left[k * 2 * ROWS + ROWS : (k + 1) * 2 * ROWS, at] = here * low

    def begun(n):
        tiles = range(n * (SUB // LANE), (n + 1) * (SUB // LANE))
        return join([far_half[m * ROWS : (m + 1) * ROWS, :] for m in tiles])

    pull_dense(tails, hot, field, stack, parity, begun, keep(far_whole))

    squares = jnp.zeros((8, LANE), F32)
    for h in range(0, chunks, 8):
        near = pull(heads_tile, h, field, parity, state, [pulled[c, h : h + 8, :] for c in range(state)])
        far = [far_whole[pl.ds(h * ROWS + j, 8, stride=ROWS), :] for j in range(state)]
        back = [None] * state
        for i in range(state):
            row = [blocks[i * state + j, h : h + 8, :] for j in range(state)]
            f = near[i]
            for j in range(state):
                f = f - row[j] * far[j]
            squares = squares + f * f
            values[pl.ds(h * ROWS + i, 8, stride=ROWS), :] = f
            for j in range(state):
                back[j] = row[j] * f if i == 0 else back[j] + row[j] * f
        for j in range(state):
            values[pl.ds((chunks + h) * ROWS + j, 8, stride=ROWS), :] = -back[j]
        for j in range(state, ROWS):
            values[pl.ds(h * ROWS + j, 8, stride=ROWS), :] = jnp.zeros((8, LANE), F32)
            values[pl.ds((chunks + h) * ROWS + j, 8, stride=ROWS), :] = jnp.zeros((8, LANE), F32)
    for n in range(pairs // SUB):
        spread(heads, 0, n)
        spread(tails, chunks, n)
    summed = both(left[...], hot[...], ((1,), (1,)))

    after = jnp.minimum(flat + 1, devices - 1)
    following = row_to_column(other[after // n_clus * half + after % n_clus // 2, state : state + 1, :], state)
    at = slice(width - LANE, width)
    ending = iota((ROWS, LANE), 1) == LANE - 1
    closed = ending & (flat == devices - 1)
    ahead = jnp.where(ending, errors[:, at] + following, errors[:, at])
    last[...] = jnp.where(closed | (iota((ROWS, LANE), 0) >= state), 0.0, ahead)
    energy = last[...] * last[...]
    for start in range(0, width - LANE, LANE):
        block = errors[:, start : start + LANE]
        energy = energy + jnp.where(iota((ROWS, LANE), 0) < state, block * block, 0.0)
    product = total(squares) + total(energy)
    inertial[...] = partial[...]
    back = transition[0, :, at] * last[0:1, :]
    for j in range(1, state):
        back = back + transition[j, :, at] * last[j : j + 1, :]
    inertial[0:state, at] = partial[0:state, at] - back

    sub = iota((ROWS, share), 0)
    damped = jnp.zeros((ROWS, share), F32)
    for k in range(parts):
        one = summed[k * 2 * ROWS : k * 2 * ROWS + ROWS] + summed[k * 2 * ROWS + ROWS : (k + 1) * 2 * ROWS]
        for m in range(per_part):
            piece = k * per_part + m
            c, t = piece // n_time, piece % n_time
            r, l = t * share // LANE, t * share % LANE
            here = jnp.where(clus_at == c, lam[r : r + 1, l : l + share], 0.0)
            states = jnp.where(sub < state, got[t * half + c // 2], 0.0)
            extra = here * states
            damped = damped + extra * states
            send[source(piece)] = one[:, m * share : (m + 1) * share] + extra
    product = product + total(damped)
    notes = note(last[:, LANE - 1 : LANE], product, state, share)
    for d in range(devices):
        send[d, state : state + 1, :] = notes[:, :share]


def image_of(n_time, n_clus, axes, got, inertial, slot, image, state):
    width = image.shape[1]
    per = LANE // got.shape[2]
    flat = lax.axis_index(axes[0]) * n_clus + lax.axis_index(axes[1])
    tiles = []
    for r in range(width // LANE):
        pieces = []
        for t in range(r * per, (r + 1) * per):
            one = got[t * n_clus]
            for c in range(1, n_clus):
                one = one + got[t * n_clus + c]
            pieces.append(one)
        tiles.append(join(pieces))
    prior = row_to_column(got[jnp.maximum(flat - 1, 0), state : state + 1, :], state)
    prior = jnp.where(flat == 0, 0.0, prior)
    for start in range(0, width, LANE):
        at = slice(start, start + LANE)
        out = reorder(tiles, slot[0:1, at]) + inertial[:, at]
        if start == 0:
            out = jnp.where(iota((ROWS, LANE), 1) == 0, out + prior, out)
        image[:, at] = out
    return jnp.sum(got[:, state : state + 1, :], axis=0)[:, state : state + 1]


def step_kernel(n_time, n_clus, axes, got, right, inertial, precond, slot, origin, sums,
                send, scaled, residual, image, scalars):
    state, width = right.shape
    product = image_of(n_time, n_clus, axes, got, inertial, slot, image, state)
    alpha = sums[0:1, state : state + 1] / product
    residual[...] = right[...] - alpha * image[0:state, :]
    dot = apply_precond(precond, residual, scaled)
    send_states(scaled, dot, origin, send, state)
    scalars[...] = jnp.broadcast_to(alpha, scalars.shape)


def end_kernel(n_time, n_clus, axes, got, residual, inertial, slot, first, scaled, along, sums, sums_next, scalars,
               solution_field, residual_out, image):
    state, width = residual.shape
    product = image_of(n_time, n_clus, axes, got, inertial, slot, image, state)
    alpha = scalars[0:1, 0:1]
    rz, rz_next = sums[0:1, state : state + 1], sums_next[0:1, state : state + 1]
    ratio = rz_next / rz
    step = rz_next / (product - ratio * rz_next / alpha)
    direction = scaled[0:state, :] + ratio * first[0:state, :]
    solution_field[...] = alpha * first[0:state, :] + step * direction
    residual_out[...] = residual[...] - step * (image[0:state, :] + ratio * along[0:state, :])


def on_device(
    right_side,
    transition,
    precond,
    slot_of,
    cluster_id,
    damping,
    pair_first,
    pair_second,
    pair_blocks,
):
    axes = ("tm", "clus")
    state, width = right_side.shape
    n_time = lax.axis_size("tm")
    n_clus = lax.axis_size("clus")
    devices = n_time * n_clus
    share = width // n_time
    pairs = pair_first.shape[1]
    positions = n_clus * width
    slot = slot_of.reshape(1, width)
    blocks = pair_blocks.reshape(state * state, pairs // LANE, LANE)
    params = pltpu.CompilerParams(vmem_limit_bytes=VMEM_LIMIT)

    def like(*shape):
        return jax.ShapeDtypeStruct(shape, F32)

    message = like(devices, ROWS, share)
    outgoing = like(n_time, n_clus // 2, ROWS, share)
    row = like(1, share)
    tile = like(ROWS, width)
    hot = pltpu.VMEM((SUB, width), BF16)
    left = pltpu.VMEM((ROWS * width // SUB, width), BF16)

    def exchange(sent):
        return lax.all_to_all(sent.reshape(devices, ROWS, share), axes, split_axis=0, concat_axis=0, tiled=True)

    def held(*arrays):
        return tuple(pltpu.with_memory_space_constraint(array, pltpu.HBM) for array in arrays)

    in_hbm = pl.BlockSpec(memory_space=pltpu.HBM)
    in_vmem = pl.BlockSpec(memory_space=pltpu.VMEM)
    dense = (pairs // LANE, LANE)
    small = (pair_first, pair_second, pair_first.reshape(dense),
             cluster_id.reshape(width // LANE, LANE), damping)
    same = [[t * n_clus + c for t in range(n_time) for c in range(q, n_clus, 2)] for q in range(2)]
    field = pltpu.VMEM((n_clus // 2, width // LANE, ROWS, LANE), F32)

    def collect(sent):
        sent = sent.reshape(devices // 2, ROWS, share)
        got = lax.all_to_all(sent, axes, split_axis=0, concat_axis=0, tiled=True, axis_index_groups=same)
        return got, lax.ppermute(got, "clus", [(c, c ^ 1) for c in range(n_clus)])

    def grouped(sent, scaled, carried, tables):
        got, other = collect(sent)
        heads, tails, heads_tile, lam = carried
        far = (pairs // LANE * ROWS, LANE)
        shapes = (like(state, *dense), like(*far), tile, tile)
        operands = (got, heads_tile, scaled, transition)
        stack = pltpu.VMEM((positions // SUB * ROWS, SUB), BF16)
        scratch = [field, stack]
        if not tables:
            shapes += (jax.ShapeDtypeStruct((SUB, 2 * pairs), BF16), like(*blocks.shape))
            operands += (heads, tails, *held(blocks))
            scratch += [pltpu.SemaphoreType.DMA((1,))]
        else:
            operands += (tails, tables[0])
        pulled, far_half, errors, partial, *fresh = pl.pallas_call(
            functools.partial(half_kernel, axes, not tables),
            out_shape=shapes,
            in_specs=[in_vmem] * (len(operands) - 1) + [in_vmem if tables else in_hbm],
            scratch_shapes=scratch,
            compiler_params=params,
            name="half",
        )(*operands)
        tables = tables or fresh
        return tables, pl.pallas_call(
            functools.partial(group_kernel, n_time, n_clus, axes),
            out_shape=(message, tile, row),
            scratch_shapes=[
                field,
                stack,
                pltpu.VMEM(far, F32),
                pltpu.VMEM((2 * pairs // LANE * ROWS, LANE), F32),
                pltpu.VMEM((2 * ROWS * positions // SUB, 2 * pairs), BF16),
                pltpu.VMEM((ROWS, LANE), F32),
            ],
            compiler_params=params,
            name="group",
        )(got, other, pulled, far_half, heads, tails, heads_tile, lam, *tables, errors, partial, transition)

    sent, first, origin, *carried = pl.pallas_call(
        begin_kernel,
        out_shape=(
            outgoing,
            tile,
            jax.ShapeDtypeStruct((1, width), jnp.int32),
            *(jax.ShapeDtypeStruct(array.shape, array.dtype) for array in small[:3]),
            like(width // LANE, LANE),
        ),
        in_specs=[in_hbm] * (3 + len(small)),
        scratch_shapes=[
            hot,
            left,
            pltpu.VMEM(right_side.shape, F32),
            pltpu.VMEM(precond.shape, F32),
            pltpu.VMEM(slot.shape, jnp.int32),
            pltpu.VMEM((width // LANE, LANE), jnp.int32),
            pltpu.VMEM(damping.shape, F32),
            pltpu.SemaphoreType.DMA((3 + len(small),)),
        ],
        compiler_params=params,
        name="begin",
    )(*held(right_side, precond, slot, *small))
    tables, (back, inertial, sums) = grouped(sent, first, carried, None)
    sent, scaled, residual, along, scalars = pl.pallas_call(
        functools.partial(step_kernel, n_time, n_clus, axes),
        out_shape=(outgoing, tile, like(state, width), tile, like(1, LANE)),
        compiler_params=params,
        name="step",
    )(exchange(back), right_side, inertial, precond, slot, origin, sums)
    _, (back, inertial, sums_next) = grouped(sent, scaled, carried, tables)
    return pl.pallas_call(
        functools.partial(end_kernel, n_time, n_clus, axes),
        out_shape=(like(state, width), like(state, width)),
        scratch_shapes=[pltpu.VMEM((ROWS, width), F32)],
        compiler_params=params,
        name="end",
    )(exchange(back), residual, inertial, slot, first, scaled, along, sums, sums_next, scalars)


def solution(mesh):
    placed = (
        P(None, ("tm", "clus")),
        P(None, None, ("tm", "clus")),
        P(None, None, ("tm", "clus")),
        P(("tm", "clus")),
        P("tm", "clus"),
        P("tm", None),
        P("tm", "clus"),
        P("tm", "clus"),
        P(None, None, "tm", "clus"),
    )
    return jax.shard_map(
        on_device,
        mesh=mesh,
        in_specs=placed,
        out_specs=(P(None, ("tm", "clus")), P(None, ("tm", "clus"))),
        check_vma=False,
    )
```

```python
import functools
import jax
import jax.numpy as jnp
from jax import lax
from jax.experimental import pallas as pl
from jax.experimental.pallas import tpu as pltpu
from jax.sharding import PartitionSpec as P

F32 = jnp.float32
BF16 = jnp.bfloat16
ROWS = 16
SUB = 256
LANE = 128
VMEM_LIMIT = 16 * 1024 * 1024


def iota(shape, axis):
    return lax.broadcasted_iota(jnp.int32, shape, axis)


def halves(value):
    high = value.astype(BF16)
    return high, (value - high.astype(F32)).astype(BF16)


def pick(rows, index):
    numbers = lax.GatherDimensionNumbers(
        offset_dims=(),
        collapsed_slice_dims=(1,),
        start_index_map=(1,),
        operand_batching_dims=(0,),
        start_indices_batching_dims=(0,),
    )
    mode = lax.GatherScatterMode.PROMISE_IN_BOUNDS
    return lax.gather(rows, index[:, :, None], numbers, (1, 1), mode=mode)


def join(pieces):
    return pieces[0] if len(pieces) == 1 else jnp.concatenate(pieces, axis=1)


def spread_rows(numbers):
    return numbers.astype(F32).astype(BF16)


def spread_row(row, count):
    return jnp.broadcast_to(row.astype(F32), (count, row.shape[1])).astype(BF16)


def hot_table(hot, index_ref, width):
    rows = [spread_rows(iota((ROWS, SUB), 0) + r) for r in range(0, SUB, ROWS)]
    for start in range(0, width, SUB):
        at = slice(start, start + SUB)
        low = spread_row(index_ref[0:1, at] & (SUB - 1), ROWS)
        for r, row in enumerate(rows):
            hot[r * ROWS : (r + 1) * ROWS, at] = equal(row, low)


def equal(one, other):
    return jnp.maximum(jnp.asarray(1, BF16) - jnp.abs(one - other), jnp.asarray(0, BF16))


def both(left, right, contract):
    return lax.dot_general(left, right, (contract, ((), ())), preferred_element_type=F32)


def column_to_row(column, state, share):
    spot = iota((ROWS, LANE), 1) % share
    row = iota((ROWS, LANE), 0)
    return jnp.sum(jnp.where((spot == row) & (row < state), column, 0.0), axis=0, keepdims=True)


def row_to_column(row, state):
    width = row.shape[1]
    sub = iota((ROWS, width), 0)
    keep = (sub == iota((ROWS, width), 1)) & (sub < state)
    return jnp.sum(jnp.where(keep, row, 0.0), axis=1, keepdims=True)


def note(column, scalar, state, share):
    spot = iota((1, LANE), 1) % share
    return jnp.where(spot == state, scalar, column_to_row(column, state, share))


def total(value):
    return jnp.sum(jnp.sum(value, axis=0, keepdims=True), axis=1, keepdims=True)


def apply_precond(precond, residual, scaled):
    state, width = residual.shape
    dot = jnp.zeros((state, LANE), F32)
    for start in range(0, width, LANE):
        at = slice(start, start + LANE)
        out = precond[0, :, at] * residual[0:1, at]
        for j in range(1, state):
            out = out + precond[j, :, at] * residual[j : j + 1, at]
        scaled[0:state, at] = out
        scaled[state:ROWS, at] = jnp.zeros((ROWS - state, LANE), F32)
        dot = dot + out * residual[:, at]
    return total(dot)


def reorder(tiles, index):
    low = jnp.broadcast_to(index & (LANE - 1), (ROWS, LANE))
    part = jnp.broadcast_to(index >> 7, (ROWS, LANE))
    out = jnp.zeros((ROWS, LANE), F32)
    for k, one in enumerate(tiles):
        out = jnp.where(part == k, pick(one, low), out)
    return out


def send_states(scaled, dot, origin, send, state):
    width = scaled.shape[1]
    copies, _, share = send.shape[1:]
    notes = note(scaled[:, 0:1], dot, state, share)
    tiles = [scaled[:, start : start + LANE] for start in range(0, width, LANE)]
    sub = iota((ROWS, share), 0)
    for k in range(width // LANE):
        piece = reorder(tiles, origin[0:1, k * LANE : (k + 1) * LANE])
        for m in range(LANE // share):
            one = jnp.where(sub == state, notes[:, :share], piece[:, m * share : (m + 1) * share])
            for copy in range(copies):
                send[k * (LANE // share) + m, copy] = one


def invert(slot, hot, left, origin):
    width = slot.shape[1]
    hot_table(hot, slot, width)
    sub = iota((ROWS, SUB), 0)
    for start in range(0, width, SUB):
        number = iota((ROWS, SUB), 1) + start
        digits = jnp.where(sub == 0, number >> 5, jnp.where(sub == 1, number & 31, 0)).astype(F32).astype(BF16)
        part = spread_row(slot[0:1, start : start + SUB] >> 8, ROWS)
        for k in range(width // SUB):
            left[k * ROWS : (k + 1) * ROWS, start : start + SUB] = equal(part, jnp.asarray(k, BF16)) * digits
    found = both(left[...], hot[...], ((1,), (1,)))
    for k in range(width // SUB):
        row = 32.0 * found[k * ROWS : k * ROWS + 1] + found[k * ROWS + 1 : k * ROWS + 2]
        origin[0:1, k * SUB : (k + 1) * SUB] = row.astype(jnp.int32)


def begin_kernel(right_in, precond_in, slot_in, heads_in, tails_in, heads_tile_in, cluster_in, damping_in,
                 send, scaled, origin, heads, tails, heads_tile, lam,
                 hot, left, right, precond, slot, cluster, damping, sems):
    state = right.shape[0]
    matrix = planes(precond_in, precond, 3)
    copies = fetch(sems, *matrix, (heads_in, heads), (tails_in, tails), (slot_in, slot), (right_in, right),
                   (cluster_in, cluster), (damping_in, damping), (heads_tile_in, heads_tile))
    copies, small = copies[: len(matrix)], copies[len(matrix) :]
    small[2].wait()
    invert(slot, hot, left, origin)
    small[4].wait()
    small[5].wait()
    spare = jnp.zeros((1, LANE - damping.shape[1]), F32)
    row = jnp.broadcast_to(jnp.concatenate([damping[...], spare], axis=1), lam.shape)
    lam[...] = pick(row, cluster[...])
    small[3].wait()
    for copy in copies:
        copy.wait()
    dot = apply_precond(precond, right, scaled)
    send_states(scaled, dot, origin, send, state)
    for copy in small[0:2] + small[6:]:
        copy.wait()


def planes(source, place, count):
    length = source.shape[0]
    step = length // count if length % count == 0 else length
    return [(source.at[first : first + step], place.at[first : first + step]) for first in range(0, length, step)]


def fetch(sems, *pairs):
    copies = [pltpu.make_async_copy(source, place, sems.at[i]) for i, (source, place) in enumerate(pairs)]
    for copy in copies:
        copy.start()
    return copies


def back_product(transition, errors, at):
    back = transition[0, :, at] * errors[0:1, at]
    for j in range(1, transition.shape[0]):
        back = back + transition[j, :, at] * errors[j : j + 1, at]
    return back


def pull(ends, h, field, parity, state, found_before):
    index = ends[h : h + 8, :]
    low, part = index & (LANE - 1), index >> 7
    out = list(found_before)
    half, tiles = field.shape[0], field.shape[1]
    for i in range(half):
        for r in range(tiles):
            here = part == (2 * i + parity) * tiles + r
            for c in range(state):
                from_row = jnp.broadcast_to(field[i, r, c : c + 1, :], (8, LANE))
                out[c] = jnp.where(here, pick(from_row, low), out[c])
    return out


def pull_dense(tails, hot, field, stack, parity, before, store):
    half, tiles = field.shape[0], field.shape[1]
    per = SUB // LANE
    parts = tiles // per
    pairs = tails.shape[1]
    for i in range(half):
        for k in range(parts):
            row = (i * parts + k) * 2 * ROWS
            high, low = halves(join([field[i, k * per + m] for m in range(per)]))
            stack[row : row + ROWS, :] = high
            stack[row + ROWS : row + 2 * ROWS, :] = low
    for n in range(pairs // SUB):
        at = slice(n * SUB, (n + 1) * SUB)
        found = both(stack[...], hot[:, pairs + n * SUB : pairs + (n + 1) * SUB], ((1,), (0,)))
        part = tails[0:1, at] >> 8
        out = before(n)
        for i in range(half):
            for k in range(parts):
                row = (i * parts + k) * 2 * ROWS
                one = found[row : row + ROWS] + found[row + ROWS : row + 2 * ROWS]
                out = jnp.where(part == (2 * i + parity) * parts + k, one, out)
        for m in range(per):
            store(n * per + m, out[:, m * LANE : (m + 1) * LANE])


def keep(far):
    def store(n, tile):
        far[n * ROWS : (n + 1) * ROWS, :] = tile

    return store


def fill(field, got):
    half, tiles = field.shape[0], field.shape[1]
    per = LANE // got.shape[2]
    for i in range(half):
        for r in range(tiles):
            field[i, r] = join([got[(r * per + m) * half + i] for m in range(per)])


def row_sums(tiles):
    row = iota((8, LANE), 0)
    for step in (4, 2, 1):
        tiles = [
            jnp.where(row & step == 0, one + pltpu.roll(one, 8 - step, 0), other + pltpu.roll(other, step, 0))
            for one, other in zip(tiles[:step], tiles[step:])
        ]
    return tiles[0]


def half_kernel(axes, once, got, heads_tile, scaled, transition, *refs):
    state = transition.shape[0]
    width = scaled.shape[1]
    chunks = heads_tile.shape[0]
    if once:
        heads, tails, blocks_in, pulled, far, errors, inertial, hot, blocks, field, stack, sems = refs
        copies = fetch(sems, *planes(blocks_in, blocks, 5))
    else:
        tails, hot, pulled, far, errors, inertial, field, stack = refs
    parity = lax.axis_index(axes[1]) % 2

    def work():
        fill(field, got)
        if once:
            pairs = heads.shape[1]
            hot_table(hot.at[:, 0:pairs], heads, pairs)
            hot_table(hot.at[:, pairs:], tails, pairs)
        zero = [jnp.zeros((8, LANE), F32)] * state
        for h in range(0, chunks, 8):
            for c, value in enumerate(pull(heads_tile, h, field, parity, state, zero)):
                pulled[c, h : h + 8, :] = value
        pull_dense(tails, hot, field, stack, parity, lambda n: jnp.zeros((ROWS, SUB), F32), keep(far))
        lane = iota((ROWS, width), 1)
        ahead = jnp.where(lane == width - 1, 0.0, pltpu.roll(scaled[...], width - 1, 1))
        empty = jnp.zeros((ROWS - state, LANE), F32)
        for start in range(0, width, LANE):
            at = slice(start, start + LANE)
            low, high = scaled[0:8, at], scaled[8:state, at]
            for first in range(0, ROWS, 8):
                moved = [
                    transition[i, 0:8, at] * low + jnp.concatenate([transition[i, 8:state, at] * high, empty], axis=0)
                    for i in range(first, min(first + 8, state))
                ]
                moved += [jnp.zeros((8, LANE), F32)] * (8 - len(moved))
                errors[first : first + 8, at] = ahead[first : first + 8, at] - row_sums(moved)
        prior = jnp.where(lane == 0, 0.0, pltpu.roll(errors[...], 1, 1))
        inertial[state:ROWS, :] = jnp.zeros((ROWS - state, width), F32)
        for start in range(0, width - LANE, LANE):
            at = slice(start, start + LANE)
            inertial[0:state, at] = prior[0:state, at] - back_product(transition, errors, at)
        inertial[0:state, width - LANE :] = prior[0:state, width - LANE :]

    if once:
        pl.when(parity >= 0)(work)
        for copy in copies:
            copy.wait()
    else:
        work()


def group_kernel(n_time, n_clus, axes, got, other, pulled, far_half, heads, tails, heads_tile, lam, hot, blocks,
                 errors, partial, transition, send, inertial, sums, field, stack, far_whole, values, left, last):
    state = transition.shape[0]
    width = errors.shape[1]
    share = got.shape[2]
    pairs = heads.shape[1]
    parts = n_clus * width // SUB
    per_part = SUB // share
    chunks = pairs // LANE
    half = n_clus // 2
    time_at, clus_at = lax.axis_index(axes[0]), lax.axis_index(axes[1])
    flat = time_at * n_clus + clus_at
    devices = n_time * n_clus

    def source(piece):
        return (piece % n_time) * n_clus + piece // n_time

    sums[...] = jnp.sum(got[:, state : state + 1, :], axis=0) + jnp.sum(other[:, state : state + 1, :], axis=0)
    fill(field, other)
    parity = 1 - clus_at % 2

    def spread(ends, base, n):
        at = slice(base * LANE + n * SUB, base * LANE + (n + 1) * SUB)
        part = spread_row(ends[0:1, n * SUB : (n + 1) * SUB] >> 8, ROWS)
        row = (base + n * (SUB // LANE)) * ROWS
        high, low = halves(join([values[row + m * ROWS : row + (m + 1) * ROWS, :] for m in range(SUB // LANE)]))
        for k in range(parts):
            here = equal(part, jnp.asarray(k, BF16))
            left[k * 2 * ROWS : k * 2 * ROWS + ROWS, at] = here * high
            left[k * 2 * ROWS + ROWS : (k + 1) * 2 * ROWS, at] = here * low

    def begun(n):
        tiles = range(n * (SUB // LANE), (n + 1) * (SUB // LANE))
        return join([far_half[m * ROWS : (m + 1) * ROWS, :] for m in tiles])

    pull_dense(tails, hot, field, stack, parity, begun, keep(far_whole))

    squares = jnp.zeros((8, LANE), F32)
    for h in range(0, chunks, 8):
        near = pull(heads_tile, h, field, parity, state, [pulled[c, h : h + 8, :] for c in range(state)])
        far = [far_whole[pl.ds(h * ROWS + j, 8, stride=ROWS), :] for j in range(state)]
        back = [None] * state
        for i in range(state):
            row = [blocks[i * state + j, h : h + 8, :] for j in range(state)]
            f = near[i]
            for j in range(state):
                f = f - row[j] * far[j]
            squares = squares + f * f
            values[pl.ds(h * ROWS + i, 8, stride=ROWS), :] = f
            for j in range(state):
                back[j] = row[j] * f if i == 0 else back[j] + row[j] * f
        for j in range(state):
            values[pl.ds((chunks + h) * ROWS + j, 8, stride=ROWS), :] = -back[j]
        for j in range(state, ROWS):
            values[pl.ds(h * ROWS + j, 8, stride=ROWS), :] = jnp.zeros((8, LANE), F32)
            values[pl.ds((chunks + h) * ROWS + j, 8, stride=ROWS), :] = jnp.zeros((8, LANE), F32)
    for n in range(pairs // SUB):
        spread(heads, 0, n)
        spread(tails, chunks, n)
    summed = both(left[...], hot[...], ((1,), (1,)))

    after = jnp.minimum(flat + 1, devices - 1)
    following = row_to_column(other[after // n_clus * half + after % n_clus // 2, state : state + 1, :], state)
    at = slice(width - LANE, width)
    ending = iota((ROWS, LANE), 1) == LANE - 1
    closed = ending & (flat == devices - 1)
    ahead = jnp.where(ending, errors[:, at] + following, errors[:, at])
    last[...] = jnp.where(closed | (iota((ROWS, LANE), 0) >= state), 0.0, ahead)
    energy = last[...] * last[...]
    for start in range(0, width - LANE, LANE):
        block = errors[:, start : start + LANE]
        energy = energy + jnp.where(iota((ROWS, LANE), 0) < state, block * block, 0.0)
    product = total(squares) + total(energy)
    inertial[...] = partial[...]
    back = transition[0, :, at] * last[0:1, :]
    for j in range(1, state):
        back = back + transition[j, :, at] * last[j : j + 1, :]
    inertial[0:state, at] = partial[0:state, at] - back

    sub = iota((ROWS, share), 0)
    damped = jnp.zeros((ROWS, share), F32)
    for k in range(parts):
        one = summed[k * 2 * ROWS : k * 2 * ROWS + ROWS] + summed[k * 2 * ROWS + ROWS : (k + 1) * 2 * ROWS]
        for m in range(per_part):
            piece = k * per_part + m
            c, t = piece // n_time, piece % n_time
            r, l = t * share // LANE, t * share % LANE
            here = jnp.where(clus_at == c, lam[r : r + 1, l : l + share], 0.0)
            states = jnp.where(sub < state, got[t * half + c // 2], 0.0)
            extra = here * states
            damped = damped + extra * states
            send[source(piece)] = one[:, m * share : (m + 1) * share] + extra
    product = product + total(damped)
    notes = note(last[:, LANE - 1 : LANE], product, state, share)
    for d in range(devices):
        send[d, state : state + 1, :] = notes[:, :share]


def image_of(n_time, n_clus, axes, got, inertial, slot, image, state):
    width = image.shape[1]
    per = LANE // got.shape[2]
    flat = lax.axis_index(axes[0]) * n_clus + lax.axis_index(axes[1])
    tiles = []
    for r in range(width // LANE):
        pieces = []
        for t in range(r * per, (r + 1) * per):
            one = got[t * n_clus]
            for c in range(1, n_clus):
                one = one + got[t * n_clus + c]
            pieces.append(one)
        tiles.append(join(pieces))
    prior = row_to_column(got[jnp.maximum(flat - 1, 0), state : state + 1, :], state)
    prior = jnp.where(flat == 0, 0.0, prior)
    for start in range(0, width, LANE):
        at = slice(start, start + LANE)
        out = reorder(tiles, slot[0:1, at]) + inertial[:, at]
        if start == 0:
            out = jnp.where(iota((ROWS, LANE), 1) == 0, out + prior, out)
        image[:, at] = out
    return jnp.sum(got[:, state : state + 1, :], axis=0)[:, state : state + 1]


def step_kernel(n_time, n_clus, axes, got, right, inertial, precond, slot, origin, sums,
                send, scaled, residual, image, scalars):
    state, width = right.shape
    product = image_of(n_time, n_clus, axes, got, inertial, slot, image, state)
    alpha = sums[0:1, state : state + 1] / product
    residual[...] = right[...] - alpha * image[0:state, :]
    dot = apply_precond(precond, residual, scaled)
    send_states(scaled, dot, origin, send, state)
    scalars[...] = jnp.broadcast_to(alpha, scalars.shape)


def end_kernel(n_time, n_clus, axes, got, residual, inertial, slot, first, scaled, along, sums, sums_next, scalars,
               solution_field, residual_out, image):
    state, width = residual.shape
    product = image_of(n_time, n_clus, axes, got, inertial, slot, image, state)
    alpha = scalars[0:1, 0:1]
    rz, rz_next = sums[0:1, state : state + 1], sums_next[0:1, state : state + 1]
    ratio = rz_next / rz
    step = rz_next / (product - ratio * rz_next / alpha)
    direction = scaled[0:state, :] + ratio * first[0:state, :]
    solution_field[...] = alpha * first[0:state, :] + step * direction
    residual_out[...] = residual[...] - step * (image[0:state, :] + ratio * along[0:state, :])


def on_device(
    right_side,
    transition,
    precond,
    slot_of,
    cluster_id,
    damping,
    pair_first,
    pair_second,
    pair_blocks,
):
    axes = ("tm", "clus")
    state, width = right_side.shape
    n_time = lax.axis_size("tm")
    n_clus = lax.axis_size("clus")
    devices = n_time * n_clus
    share = width // n_time
    pairs = pair_first.shape[1]
    positions = n_clus * width
    slot = slot_of.reshape(1, width)
    blocks = pair_blocks.reshape(state * state, pairs // LANE, LANE)
    params = pltpu.CompilerParams(vmem_limit_bytes=VMEM_LIMIT)

    def like(*shape):
        return jax.ShapeDtypeStruct(shape, F32)

    message = like(devices, ROWS, share)
    outgoing = like(n_time, n_clus // 2, ROWS, share)
    row = like(1, share)
    tile = like(ROWS, width)
    hot = pltpu.VMEM((SUB, width), BF16)
    left = pltpu.VMEM((ROWS * width // SUB, width), BF16)

    def exchange(sent):
        return lax.all_to_all(sent.reshape(devices, ROWS, share), axes, split_axis=0, concat_axis=0, tiled=True)

    def held(*arrays):
        return tuple(pltpu.with_memory_space_constraint(array, pltpu.HBM) for array in arrays)

    in_hbm = pl.BlockSpec(memory_space=pltpu.HBM)
    in_vmem = pl.BlockSpec(memory_space=pltpu.VMEM)
    dense = (pairs // LANE, LANE)
    small = (pair_first, pair_second, pair_first.reshape(dense),
             cluster_id.reshape(width // LANE, LANE), damping)
    same = [[t * n_clus + c for t in range(n_time) for c in range(q, n_clus, 2)] for q in range(2)]
    field = pltpu.VMEM((n_clus // 2, width // LANE, ROWS, LANE), F32)

    def collect(sent):
        sent = sent.reshape(devices // 2, ROWS, share)
        got = lax.all_to_all(sent, axes, split_axis=0, concat_axis=0, tiled=True, axis_index_groups=same)
        return got, lax.ppermute(got, "clus", [(c, c ^ 1) for c in range(n_clus)])

    def grouped(sent, scaled, carried, tables):
        got, other = collect(sent)
        heads, tails, heads_tile, lam = carried
        far = (pairs // LANE * ROWS, LANE)
        shapes = (like(state, *dense), like(*far), tile, tile)
        operands = (got, heads_tile, scaled, transition)
        stack = pltpu.VMEM((positions // SUB * ROWS, SUB), BF16)
        scratch = [field, stack]
        if not tables:
            shapes += (jax.ShapeDtypeStruct((SUB, 2 * pairs), BF16), like(*blocks.shape))
            operands += (heads, tails, *held(blocks))
            scratch += [pltpu.SemaphoreType.DMA((5,))]
        else:
            operands += (tails, tables[0])
        pulled, far_half, errors, partial, *fresh = pl.pallas_call(
            functools.partial(half_kernel, axes, not tables),
            out_shape=shapes,
            in_specs=[in_vmem] * (len(operands) - 1) + [in_vmem if tables else in_hbm],
            scratch_shapes=scratch,
            compiler_params=params,
            name="half",
        )(*operands)
        tables = tables or fresh
        return tables, pl.pallas_call(
            functools.partial(group_kernel, n_time, n_clus, axes),
            out_shape=(message, tile, row),
            scratch_shapes=[
                field,
                stack,
                pltpu.VMEM(far, F32),
                pltpu.VMEM((2 * pairs // LANE * ROWS, LANE), F32),
                pltpu.VMEM((2 * ROWS * positions // SUB, 2 * pairs), BF16),
                pltpu.VMEM((ROWS, LANE), F32),
            ],
            compiler_params=params,
            name="group",
        )(got, other, pulled, far_half, heads, tails, heads_tile, lam, *tables, errors, partial, transition)

    sent, first, origin, *carried = pl.pallas_call(
        begin_kernel,
        out_shape=(
            outgoing,
            tile,
            jax.ShapeDtypeStruct((1, width), jnp.int32),
            *(jax.ShapeDtypeStruct(array.shape, array.dtype) for array in small[:3]),
            like(width // LANE, LANE),
        ),
        in_specs=[in_hbm] * (3 + len(small)),
        scratch_shapes=[
            hot,
            left,
            pltpu.VMEM(right_side.shape, F32),
            pltpu.VMEM(precond.shape, F32),
            pltpu.VMEM(slot.shape, jnp.int32),
            pltpu.VMEM((width // LANE, LANE), jnp.int32),
            pltpu.VMEM(damping.shape, F32),
            pltpu.SemaphoreType.DMA((5 + len(small),)),
        ],
        compiler_params=params,
        name="begin",
    )(*held(right_side, precond, slot, *small))
    tables, (back, inertial, sums) = grouped(sent, first, carried, None)
    sent, scaled, residual, along, scalars = pl.pallas_call(
        functools.partial(step_kernel, n_time, n_clus, axes),
        out_shape=(outgoing, tile, like(state, width), tile, like(1, LANE)),
        compiler_params=params,
        name="step",
    )(exchange(back), right_side, inertial, precond, slot, origin, sums)
    _, (back, inertial, sums_next) = grouped(sent, scaled, carried, tables)
    return pl.pallas_call(
        functools.partial(end_kernel, n_time, n_clus, axes),
        out_shape=(like(state, width), like(state, width)),
        scratch_shapes=[pltpu.VMEM((ROWS, width), F32)],
        compiler_params=params,
        name="end",
    )(exchange(back), residual, inertial, slot, first, scaled, along, sums, sums_next, scalars)


def solution(mesh):
    placed = (
        P(None, ("tm", "clus")),
        P(None, None, ("tm", "clus")),
        P(None, None, ("tm", "clus")),
        P(("tm", "clus")),
        P("tm", "clus"),
        P("tm", None),
        P("tm", "clus"),
        P("tm", "clus"),
        P(None, None, "tm", "clus"),
    )
    return jax.shard_map(
        on_device,
        mesh=mesh,
        in_specs=placed,
        out_specs=(P(None, ("tm", "clus")), P(None, ("tm", "clus"))),
        check_vma=False,
    )
```

```python
import functools
import jax
import jax.numpy as jnp
from jax import lax
from jax.experimental import pallas as pl
from jax.experimental.pallas import tpu as pltpu
from jax.sharding import PartitionSpec as P

F32 = jnp.float32
BF16 = jnp.bfloat16
ROWS = 16
SUB = 256
LANE = 128
VMEM_LIMIT = 16 * 1024 * 1024


def iota(shape, axis):
    return lax.broadcasted_iota(jnp.int32, shape, axis)


def halves(value):
    high = value.astype(BF16)
    return high, (value - high.astype(F32)).astype(BF16)


def pick(rows, index):
    numbers = lax.GatherDimensionNumbers(
        offset_dims=(),
        collapsed_slice_dims=(1,),
        start_index_map=(1,),
        operand_batching_dims=(0,),
        start_indices_batching_dims=(0,),
    )
    mode = lax.GatherScatterMode.PROMISE_IN_BOUNDS
    return lax.gather(rows, index[:, :, None], numbers, (1, 1), mode=mode)


def join(pieces):
    return pieces[0] if len(pieces) == 1 else jnp.concatenate(pieces, axis=1)


def spread_rows(numbers):
    return numbers.astype(F32).astype(BF16)


def spread_row(row, count):
    return jnp.broadcast_to(row.astype(F32), (count, row.shape[1])).astype(BF16)


def hot_table(hot, index_ref, width):
    rows = [spread_rows(iota((ROWS, SUB), 0) + r) for r in range(0, SUB, ROWS)]
    for start in range(0, width, SUB):
        at = slice(start, start + SUB)
        low = spread_row(index_ref[0:1, at] & (SUB - 1), ROWS)
        for r, row in enumerate(rows):
            hot[r * ROWS : (r + 1) * ROWS, at] = equal(row, low)


def equal(one, other):
    return jnp.maximum(jnp.asarray(1, BF16) - jnp.abs(one - other), jnp.asarray(0, BF16))


def both(left, right, contract):
    return lax.dot_general(left, right, (contract, ((), ())), preferred_element_type=F32)


def column_to_row(column, state, share):
    spot = iota((ROWS, LANE), 1) % share
    row = iota((ROWS, LANE), 0)
    return jnp.sum(jnp.where((spot == row) & (row < state), column, 0.0), axis=0, keepdims=True)


def row_to_column(row, state):
    width = row.shape[1]
    sub = iota((ROWS, width), 0)
    keep = (sub == iota((ROWS, width), 1)) & (sub < state)
    return jnp.sum(jnp.where(keep, row, 0.0), axis=1, keepdims=True)


def note(column, scalar, state, share):
    spot = iota((1, LANE), 1) % share
    return jnp.where(spot == state, scalar, column_to_row(column, state, share))


def total(value):
    return jnp.sum(jnp.sum(value, axis=0, keepdims=True), axis=1, keepdims=True)


def apply_precond(precond, residual, scaled):
    state, width = residual.shape
    dot = jnp.zeros((state, LANE), F32)
    for start in range(0, width, LANE):
        at = slice(start, start + LANE)
        out = precond[0, :, at] * residual[0:1, at]
        for j in range(1, state):
            out = out + precond[j, :, at] * residual[j : j + 1, at]
        scaled[0:state, at] = out
        scaled[state:ROWS, at] = jnp.zeros((ROWS - state, LANE), F32)
        dot = dot + out * residual[:, at]
    return total(dot)


def reorder(tiles, index):
    low = jnp.broadcast_to(index & (LANE - 1), (ROWS, LANE))
    part = jnp.broadcast_to(index >> 7, (ROWS, LANE))
    out = jnp.zeros((ROWS, LANE), F32)
    for k, one in enumerate(tiles):
        out = jnp.where(part == k, pick(one, low), out)
    return out


def send_states(scaled, dot, origin, send, state):
    width = scaled.shape[1]
    copies, _, share = send.shape[1:]
    notes = note(scaled[:, 0:1], dot, state, share)
    tiles = [scaled[:, start : start + LANE] for start in range(0, width, LANE)]
    sub = iota((ROWS, share), 0)
    for k in range(width // LANE):
        piece = reorder(tiles, origin[0:1, k * LANE : (k + 1) * LANE])
        for m in range(LANE // share):
            one = jnp.where(sub == state, notes[:, :share], piece[:, m * share : (m + 1) * share])
            for copy in range(copies):
                send[k * (LANE // share) + m, copy] = one


def invert(slot, hot, left, origin):
    width = slot.shape[1]
    hot_table(hot, slot, width)
    sub = iota((ROWS, SUB), 0)
    for start in range(0, width, SUB):
        number = iota((ROWS, SUB), 1) + start
        digits = jnp.where(sub == 0, number >> 5, jnp.where(sub == 1, number & 31, 0)).astype(F32).astype(BF16)
        part = spread_row(slot[0:1, start : start + SUB] >> 8, ROWS)
        for k in range(width // SUB):
            left[k * ROWS : (k + 1) * ROWS, start : start + SUB] = equal(part, jnp.asarray(k, BF16)) * digits
    found = both(left[...], hot[...], ((1,), (1,)))
    for k in range(width // SUB):
        row = 32.0 * found[k * ROWS : k * ROWS + 1] + found[k * ROWS + 1 : k * ROWS + 2]
        origin[0:1, k * SUB : (k + 1) * SUB] = row.astype(jnp.int32)


def begin_kernel(right_in, precond_in, slot_in, heads_in, tails_in, heads_tile_in, cluster_in, damping_in,
                 send, scaled, origin, heads, tails, heads_tile, lam,
                 hot, left, right, precond, slot, cluster, damping, sems):
    state = right.shape[0]
    copies = fetch(sems, (precond_in, precond), (heads_in, heads), (tails_in, tails), (slot_in, slot), (right_in, right),
                   (cluster_in, cluster), (damping_in, damping), (heads_tile_in, heads_tile))
    copies[3].wait()
    invert(slot, hot, left, origin)
    copies[5].wait()
    copies[6].wait()
    spare = jnp.zeros((1, LANE - damping.shape[1]), F32)
    row = jnp.broadcast_to(jnp.concatenate([damping[...], spare], axis=1), lam.shape)
    lam[...] = pick(row, cluster[...])
    copies[4].wait()
    copies[0].wait()
    dot = apply_precond(precond, right, scaled)
    send_states(scaled, dot, origin, send, state)
    for copy in copies[1:3] + copies[7:]:
        copy.wait()


def fetch(sems, *pairs):
    copies = [pltpu.make_async_copy(source, place, sems.at[i]) for i, (source, place) in enumerate(pairs)]
    for copy in copies:
        copy.start()
    return copies


def back_product(transition, errors, at):
    back = transition[0, :, at] * errors[0:1, at]
    for j in range(1, transition.shape[0]):
        back = back + transition[j, :, at] * errors[j : j + 1, at]
    return back


def pull(ends, h, field, parity, state, found_before):
    index = ends[h : h + 8, :]
    low, part = index & (LANE - 1), index >> 7
    out = list(found_before)
    half, tiles = field.shape[0], field.shape[1]
    for i in range(half):
        for r in range(tiles):
            here = part == (2 * i + parity) * tiles + r
            for c in range(state):
                from_row = jnp.broadcast_to(field[i, r, c : c + 1, :], (8, LANE))
                out[c] = jnp.where(here, pick(from_row, low), out[c])
    return out


def pull_dense(tails, hot, field, stack, parity, before, store):
    half, tiles = field.shape[0], field.shape[1]
    per = SUB // LANE
    parts = tiles // per
    pairs = tails.shape[1]
    for i in range(half):
        for k in range(parts):
            row = (i * parts + k) * 2 * ROWS
            high, low = halves(join([field[i, k * per + m] for m in range(per)]))
            stack[row : row + ROWS, :] = high
            stack[row + ROWS : row + 2 * ROWS, :] = low
    for n in range(pairs // SUB):
        at = slice(n * SUB, (n + 1) * SUB)
        found = both(stack[...], hot[:, pairs + n * SUB : pairs + (n + 1) * SUB], ((1,), (0,)))
        part = tails[0:1, at] >> 8
        out = before(n)
        for i in range(half):
            for k in range(parts):
                row = (i * parts + k) * 2 * ROWS
                one = found[row : row + ROWS] + found[row + ROWS : row + 2 * ROWS]
                out = jnp.where(part == (2 * i + parity) * parts + k, one, out)
        for m in range(per):
            store(n * per + m, out[:, m * LANE : (m + 1) * LANE])


def keep(far):
    def store(n, tile):
        far[n * ROWS : (n + 1) * ROWS, :] = tile

    return store


def fill(field, got):
    half, tiles = field.shape[0], field.shape[1]
    per = LANE // got.shape[2]
    for i in range(half):
        for r in range(tiles):
            field[i, r] = join([got[(r * per + m) * half + i] for m in range(per)])


def row_sums(tiles):
    row = iota((8, LANE), 0)
    for step in (4, 2, 1):
        tiles = [
            jnp.where(row & step == 0, one + pltpu.roll(one, 8 - step, 0), other + pltpu.roll(other, step, 0))
            for one, other in zip(tiles[:step], tiles[step:])
        ]
    return tiles[0]


def half_kernel(axes, once, got, heads_tile, scaled, transition, *refs):
    state = transition.shape[0]
    width = scaled.shape[1]
    chunks = heads_tile.shape[0]
    if once:
        heads, tails, blocks_in, pulled, far, errors, inertial, energy, hot, blocks, field, stack, sems = refs
        (copy,) = fetch(sems, (blocks_in, blocks))
    else:
        tails, hot, pulled, far, errors, inertial, energy, field, stack = refs
    parity = lax.axis_index(axes[1]) % 2

    def work():
        fill(field, got)
        if once:
            pairs = heads.shape[1]
            hot_table(hot.at[:, 0:pairs], heads, pairs)
            hot_table(hot.at[:, pairs:], tails, pairs)
        zero = [jnp.zeros((8, LANE), F32)] * state
        for h in range(0, chunks, 8):
            for c, value in enumerate(pull(heads_tile, h, field, parity, state, zero)):
                pulled[c, h : h + 8, :] = value
        pull_dense(tails, hot, field, stack, parity, lambda n: jnp.zeros((ROWS, SUB), F32), keep(far))
        lane = iota((ROWS, width), 1)
        ahead = jnp.where(lane == width - 1, 0.0, pltpu.roll(scaled[...], width - 1, 1))
        empty = jnp.zeros((ROWS - state, LANE), F32)
        for start in range(0, width, LANE):
            at = slice(start, start + LANE)
            low, high = scaled[0:8, at], scaled[8:state, at]
            for first in range(0, ROWS, 8):
                moved = [
                    transition[i, 0:8, at] * low + jnp.concatenate([transition[i, 8:state, at] * high, empty], axis=0)
                    for i in range(first, min(first + 8, state))
                ]
                moved += [jnp.zeros((8, LANE), F32)] * (8 - len(moved))
                errors[first : first + 8, at] = ahead[first : first + 8, at] - row_sums(moved)
        prior = jnp.where(lane == 0, 0.0, pltpu.roll(errors[...], 1, 1))
        inertial[state:ROWS, :] = jnp.zeros((ROWS - state, width), F32)
        for start in range(0, width - LANE, LANE):
            at = slice(start, start + LANE)
            inertial[0:state, at] = prior[0:state, at] - back_product(transition, errors, at)
        inertial[0:state, width - LANE :] = prior[0:state, width - LANE :]
        squares = jnp.zeros((ROWS, LANE), F32)
        for start in range(0, width - LANE, LANE):
            squares = squares + errors[:, start : start + LANE] * errors[:, start : start + LANE]
        energy[...] = squares

    if once:
        pl.when(parity >= 0)(work)
        copy.wait()
    else:
        work()


def group_kernel(n_time, n_clus, axes, got, other, pulled, far_half, heads, tails, heads_tile, lam, hot, blocks,
                 errors, partial, begun_energy, transition, send, inertial, sums, field, stack, far_whole, values, left, last):
    state = transition.shape[0]
    width = errors.shape[1]
    share = got.shape[2]
    pairs = heads.shape[1]
    parts = n_clus * width // SUB
    per_part = SUB // share
    chunks = pairs // LANE
    half = n_clus // 2
    time_at, clus_at = lax.axis_index(axes[0]), lax.axis_index(axes[1])
    flat = time_at * n_clus + clus_at
    devices = n_time * n_clus

    def source(piece):
        return (piece % n_time) * n_clus + piece // n_time

    sums[...] = jnp.sum(got[:, state : state + 1, :], axis=0) + jnp.sum(other[:, state : state + 1, :], axis=0)
    fill(field, other)
    parity = 1 - clus_at % 2

    def spread(ends, base, n):
        at = slice(base * LANE + n * SUB, base * LANE + (n + 1) * SUB)
        part = spread_row(ends[0:1, n * SUB : (n + 1) * SUB] >> 8, ROWS)
        row = (base + n * (SUB // LANE)) * ROWS
        high, low = halves(join([values[row + m * ROWS : row + (m + 1) * ROWS, :] for m in range(SUB // LANE)]))
        for k in range(parts):
            here = equal(part, jnp.asarray(k, BF16))
            left[k * 2 * ROWS : k * 2 * ROWS + ROWS, at] = here * high
            left[k * 2 * ROWS + ROWS : (k + 1) * 2 * ROWS, at] = here * low

    def begun(n):
        tiles = range(n * (SUB // LANE), (n + 1) * (SUB // LANE))
        return join([far_half[m * ROWS : (m + 1) * ROWS, :] for m in tiles])

    pull_dense(tails, hot, field, stack, parity, begun, keep(far_whole))

    squares = jnp.zeros((8, LANE), F32)
    for h in range(0, chunks, 8):
        near = pull(heads_tile, h, field, parity, state, [pulled[c, h : h + 8, :] for c in range(state)])
        far = [far_whole[pl.ds(h * ROWS + j, 8, stride=ROWS), :] for j in range(state)]
        back = [None] * state
        for i in range(state):
            row = [blocks[i * state + j, h : h + 8, :] for j in range(state)]
            f = near[i]
            for j in range(state):
                f = f - row[j] * far[j]
            squares = squares + f * f
            values[pl.ds(h * ROWS + i, 8, stride=ROWS), :] = f
            for j in range(state):
                back[j] = row[j] * f if i == 0 else back[j] + row[j] * f
        for j in range(state):
            values[pl.ds((chunks + h) * ROWS + j, 8, stride=ROWS), :] = -back[j]
        for j in range(state, ROWS):
            values[pl.ds(h * ROWS + j, 8, stride=ROWS), :] = jnp.zeros((8, LANE), F32)
            values[pl.ds((chunks + h) * ROWS + j, 8, stride=ROWS), :] = jnp.zeros((8, LANE), F32)
    for n in range(pairs // SUB):
        spread(heads, 0, n)
        spread(tails, chunks, n)
    summed = both(left[...], hot[...], ((1,), (1,)))

    after = jnp.minimum(flat + 1, devices - 1)
    following = row_to_column(other[after // n_clus * half + after % n_clus // 2, state : state + 1, :], state)
    at = slice(width - LANE, width)
    ending = iota((ROWS, LANE), 1) == LANE - 1
    closed = ending & (flat == devices - 1)
    ahead = jnp.where(ending, errors[:, at] + following, errors[:, at])
    last[...] = jnp.where(closed | (iota((ROWS, LANE), 0) >= state), 0.0, ahead)
    energy = last[...] * last[...] + begun_energy[...]
    product = total(squares) + total(energy)
    inertial[...] = partial[...]
    back = transition[0, :, at] * last[0:1, :]
    for j in range(1, state):
        back = back + transition[j, :, at] * last[j : j + 1, :]
    inertial[0:state, at] = partial[0:state, at] - back

    sub = iota((ROWS, share), 0)
    damped = jnp.zeros((ROWS, share), F32)
    for k in range(parts):
        one = summed[k * 2 * ROWS : k * 2 * ROWS + ROWS] + summed[k * 2 * ROWS + ROWS : (k + 1) * 2 * ROWS]
        for m in range(per_part):
            piece = k * per_part + m
            c, t = piece // n_time, piece % n_time
            r, l = t * share // LANE, t * share % LANE
            here = jnp.where(clus_at == c, lam[r : r + 1, l : l + share], 0.0)
            states = jnp.where(sub < state, got[t * half + c // 2], 0.0)
            extra = here * states
            damped = damped + extra * states
            send[source(piece)] = one[:, m * share : (m + 1) * share] + extra
    product = product + total(damped)
    notes = note(last[:, LANE - 1 : LANE], product, state, share)
    for d in range(devices):
        send[d, state : state + 1, :] = notes[:, :share]


def image_of(n_time, n_clus, axes, got, inertial, slot, image, state):
    width = image.shape[1]
    per = LANE // got.shape[2]
    flat = lax.axis_index(axes[0]) * n_clus + lax.axis_index(axes[1])
    tiles = []
    for r in range(width // LANE):
        pieces = []
        for t in range(r * per, (r + 1) * per):
            one = got[t * n_clus]
            for c in range(1, n_clus):
                one = one + got[t * n_clus + c]
            pieces.append(one)
        tiles.append(join(pieces))
    prior = row_to_column(got[jnp.maximum(flat - 1, 0), state : state + 1, :], state)
    prior = jnp.where(flat == 0, 0.0, prior)
    for start in range(0, width, LANE):
        at = slice(start, start + LANE)
        out = reorder(tiles, slot[0:1, at]) + inertial[:, at]
        if start == 0:
            out = jnp.where(iota((ROWS, LANE), 1) == 0, out + prior, out)
        image[:, at] = out
    return jnp.sum(got[:, state : state + 1, :], axis=0)[:, state : state + 1]


def step_kernel(n_time, n_clus, axes, got, right, inertial, precond, slot, origin, sums,
                send, scaled, residual, image, scalars):
    state, width = right.shape
    product = image_of(n_time, n_clus, axes, got, inertial, slot, image, state)
    alpha = sums[0:1, state : state + 1] / product
    residual[...] = right[...] - alpha * image[0:state, :]
    dot = apply_precond(precond, residual, scaled)
    send_states(scaled, dot, origin, send, state)
    scalars[...] = jnp.broadcast_to(alpha, scalars.shape)


def end_kernel(n_time, n_clus, axes, got, residual, inertial, slot, first, scaled, along, sums, sums_next, scalars,
               solution_field, residual_out, image):
    state, width = residual.shape
    product = image_of(n_time, n_clus, axes, got, inertial, slot, image, state)
    alpha = scalars[0:1, 0:1]
    rz, rz_next = sums[0:1, state : state + 1], sums_next[0:1, state : state + 1]
    ratio = rz_next / rz
    step = rz_next / (product - ratio * rz_next / alpha)
    direction = scaled[0:state, :] + ratio * first[0:state, :]
    solution_field[...] = alpha * first[0:state, :] + step * direction
    residual_out[...] = residual[...] - step * (image[0:state, :] + ratio * along[0:state, :])


def on_device(
    right_side,
    transition,
    precond,
    slot_of,
    cluster_id,
    damping,
    pair_first,
    pair_second,
    pair_blocks,
):
    axes = ("tm", "clus")
    state, width = right_side.shape
    n_time = lax.axis_size("tm")
    n_clus = lax.axis_size("clus")
    devices = n_time * n_clus
    share = width // n_time
    pairs = pair_first.shape[1]
    positions = n_clus * width
    slot = slot_of.reshape(1, width)
    blocks = pair_blocks.reshape(state * state, pairs // LANE, LANE)
    params = pltpu.CompilerParams(vmem_limit_bytes=VMEM_LIMIT)

    def like(*shape):
        return jax.ShapeDtypeStruct(shape, F32)

    message = like(devices, ROWS, share)
    outgoing = like(n_time, n_clus // 2, ROWS, share)
    row = like(1, share)
    tile = like(ROWS, width)
    hot = pltpu.VMEM((SUB, width), BF16)
    left = pltpu.VMEM((ROWS * width // SUB, width), BF16)

    def exchange(sent):
        return lax.all_to_all(sent.reshape(devices, ROWS, share), axes, split_axis=0, concat_axis=0, tiled=True)

    def held(*arrays):
        return tuple(pltpu.with_memory_space_constraint(array, pltpu.HBM) for array in arrays)

    in_hbm = pl.BlockSpec(memory_space=pltpu.HBM)
    in_vmem = pl.BlockSpec(memory_space=pltpu.VMEM)
    dense = (pairs // LANE, LANE)
    small = (pair_first, pair_second, pair_first.reshape(dense),
             cluster_id.reshape(width // LANE, LANE), damping)
    same = [[t * n_clus + c for t in range(n_time) for c in range(q, n_clus, 2)] for q in range(2)]
    field = pltpu.VMEM((n_clus // 2, width // LANE, ROWS, LANE), F32)

    def collect(sent):
        sent = sent.reshape(devices // 2, ROWS, share)
        got = lax.all_to_all(sent, axes, split_axis=0, concat_axis=0, tiled=True, axis_index_groups=same)
        return got, lax.ppermute(got, "clus", [(c, c ^ 1) for c in range(n_clus)])

    def grouped(sent, scaled, carried, tables):
        got, other = collect(sent)
        heads, tails, heads_tile, lam = carried
        far = (pairs // LANE * ROWS, LANE)
        shapes = (like(state, *dense), like(*far), tile, tile, like(ROWS, LANE))
        operands = (got, heads_tile, scaled, transition)
        stack = pltpu.VMEM((positions // SUB * ROWS, SUB), BF16)
        scratch = [field, stack]
        if not tables:
            shapes += (jax.ShapeDtypeStruct((SUB, 2 * pairs), BF16), like(*blocks.shape))
            operands += (heads, tails, *held(blocks))
            scratch += [pltpu.SemaphoreType.DMA((1,))]
        else:
            operands += (tails, tables[0])
        pulled, far_half, errors, partial, energy, *fresh = pl.pallas_call(
            functools.partial(half_kernel, axes, not tables),
            out_shape=shapes,
            in_specs=[in_vmem] * (len(operands) - 1) + [in_vmem if tables else in_hbm],
            scratch_shapes=scratch,
            compiler_params=params,
            name="half",
        )(*operands)
        tables = tables or fresh
        return tables, pl.pallas_call(
            functools.partial(group_kernel, n_time, n_clus, axes),
            out_shape=(message, tile, row),
            scratch_shapes=[
                field,
                stack,
                pltpu.VMEM(far, F32),
                pltpu.VMEM((2 * pairs // LANE * ROWS, LANE), F32),
                pltpu.VMEM((2 * ROWS * positions // SUB, 2 * pairs), BF16),
                pltpu.VMEM((ROWS, LANE), F32),
            ],
            compiler_params=params,
            name="group",
        )(got, other, pulled, far_half, heads, tails, heads_tile, lam, *tables, errors, partial, energy, transition)

    sent, first, origin, *carried = pl.pallas_call(
        begin_kernel,
        out_shape=(
            outgoing,
            tile,
            jax.ShapeDtypeStruct((1, width), jnp.int32),
            *(jax.ShapeDtypeStruct(array.shape, array.dtype) for array in small[:3]),
            like(width // LANE, LANE),
        ),
        in_specs=[in_hbm] * (3 + len(small)),
        scratch_shapes=[
            hot,
            left,
            pltpu.VMEM(right_side.shape, F32),
            pltpu.VMEM(precond.shape, F32),
            pltpu.VMEM(slot.shape, jnp.int32),
            pltpu.VMEM((width // LANE, LANE), jnp.int32),
            pltpu.VMEM(damping.shape, F32),
            pltpu.SemaphoreType.DMA((3 + len(small),)),
        ],
        compiler_params=params,
        name="begin",
    )(*held(right_side, precond, slot, *small))
    tables, (back, inertial, sums) = grouped(sent, first, carried, None)
    sent, scaled, residual, along, scalars = pl.pallas_call(
        functools.partial(step_kernel, n_time, n_clus, axes),
        out_shape=(outgoing, tile, like(state, width), tile, like(1, LANE)),
        compiler_params=params,
        name="step",
    )(exchange(back), right_side, inertial, precond, slot, origin, sums)
    _, (back, inertial, sums_next) = grouped(sent, scaled, carried, tables)
    return pl.pallas_call(
        functools.partial(end_kernel, n_time, n_clus, axes),
        out_shape=(like(state, width), like(state, width)),
        scratch_shapes=[pltpu.VMEM((ROWS, width), F32)],
        compiler_params=params,
        name="end",
    )(exchange(back), residual, inertial, slot, first, scaled, along, sums, sums_next, scalars)


def solution(mesh):
    placed = (
        P(None, ("tm", "clus")),
        P(None, None, ("tm", "clus")),
        P(None, None, ("tm", "clus")),
        P(("tm", "clus")),
        P("tm", "clus"),
        P("tm", None),
        P("tm", "clus"),
        P("tm", "clus"),
        P(None, None, "tm", "clus"),
    )
    return jax.shard_map(
        on_device,
        mesh=mesh,
        in_specs=placed,
        out_specs=(P(None, ("tm", "clus")), P(None, ("tm", "clus"))),
        check_vma=False,
    )
```
